512 devices in a mesh: wide: 128 (over y, z, core), head: 4 (over x).
Axes of the slice: x: 4, y: 4, z: 16, core: 2. Of those that a mesh axis runs over, the one named last changes fastest.
Arguments:
- hidden_in: bfloat16 [16384, 4096], P('wide', 'head'), may hold values from -6 to 6
- enc_query: bfloat16 [16384, 2048], P('wide', 'head'), may hold values from -160 to 160
- enc_key: bfloat16 [16384, 2048], P('wide', 'head'), may hold values from -6 to 6
- enc_value: bfloat16 [16384, 2048], P('wide', 'head'), may hold values from -6 to 6
- dec_query: bfloat16 [8192, 2048], P('wide', 'head'), may hold values from -6 to 6
- out_proj: bfloat16 [2048, 4096], P('head', 'wide'), may hold values from -0.125 to 0.125
- key_proj: bfloat16 [4096, 2048], P('wide', 'head'), may hold values from -0.09375 to 0.09375
- value_proj: bfloat16 [4096, 2048], P('wide', 'head'), may hold values from -0.09375 to 0.09375
- norm_gain: float32 [4096], replicated, may hold values from 0.25 to 1.75
- enc_len: int32 [256], replicated, may hold values from 33 to 128, as said below
- dec_len: int32 [256], replicated, may hold values from 17 to 64, as said below
- example_order: int32 [256], replicated, may hold values from 0 to 255, as said below
- enc_bounds: int32 [129], replicated, may hold values from 0 to 256, as said below
- dec_bounds: int32 [129], replicated, may hold values from 0 to 256, as said below
Outputs:
- encoder_hidden: bfloat16 [16384, 4096], P('wide', 'head')
- cross_context: bfloat16 [8192, 2048], P('wide', 'head')
The draws below stay inside these ranges and needn't reach their ends.
Inputs may be any that keep to these rules, and one draw needn't show every extreme that they name: `enc_len`: the examples of one wide device in the encoder layout fill at most 128 rows; the last device holds one example of exactly 128 rows. `dec_len`: the examples of one wide device in the decoder layout fill at most 64 rows; the first device holds one example of exactly 64 rows. `example_order`: A permutation of the examples. `enc_bounds`: nondecreasing from 0 to 256; every device gets one to three examples. `dec_bounds`: nondecreasing from 0 to 256; every device gets one to three examples; one less than enc_bounds at every inner index.
All inputs are finite; a program needn't handle non-finite values.
Results may differ from the reference program's by a relative error of at most 0.0073.
Values may be sent and summed in bfloat16 or wider, within the bound.
A program may use at most 64 MiB of HBM per device.

```python
import math
import jax
import jax.numpy as jnp
from jax import lax

D = 4096
HEAD_DIM = 256
HEAD_DEV = 2
ENC_CAP = 128
HEADS = 8
DEC_CAP = 64
EXAMPLES = 256
ENC_TOKENS = 16384
DEC_TOKENS = 8192
N_WIDE = 128
N_HEAD = 4


def spread_lengths(key, bounds, capacity, example_order, full_place):
    places = jnp.arange(EXAMPLES, dtype=jnp.int32)
    owner = jnp.sum((bounds[None, 1:] <= places[:, None]).astype(jnp.int32), axis=1)
    counts = bounds[1:] - bounds[:-1]
    held = jnp.sum(jnp.where(owner[:, None] == jnp.arange(N_WIDE, dtype=jnp.int32)[None, :], counts[None, :], 0), axis=1)
    lowest = capacity // (held + 1) + 1
    highest = capacity // held
    drawn = jax.random.randint(key, (EXAMPLES,), lowest, highest + 1).astype(jnp.int32)
    drawn = jnp.where(places == full_place, capacity, drawn)
    return jnp.zeros((EXAMPLES,), jnp.int32).at[example_order].set(drawn)


def edge_shifts(key):
    edge_index = jnp.arange(N_WIDE + 1, dtype=jnp.int32)
    shifts = jax.random.randint(key, (N_WIDE + 1,), 0, 2).astype(jnp.int32)
    shifts = jnp.where((edge_index == 0) | (edge_index == N_WIDE) | (edge_index == 1), 0, shifts)
    shifts = jnp.where(edge_index == N_WIDE - 1, 1, shifts)
    return 2 * edge_index + shifts


def layout(key):
    enc_bounds = edge_shifts(jax.random.fold_in(key, 11))
    edge_index = jnp.arange(N_WIDE + 1, dtype=jnp.int32)
    inner = ((edge_index > 0) & (edge_index < N_WIDE)).astype(jnp.int32)
    dec_bounds = (enc_bounds - inner).astype(jnp.int32)
    example_order = jax.random.permutation(jax.random.fold_in(key, 13), EXAMPLES).astype(jnp.int32)
    enc_len = spread_lengths(jax.random.fold_in(key, 14), enc_bounds, ENC_CAP, example_order, EXAMPLES - 1)
    dec_len = spread_lengths(jax.random.fold_in(key, 15), dec_bounds, DEC_CAP, example_order, 0)
    return (example_order, enc_bounds, dec_bounds, enc_len, dec_len)


def key_field(key):
    shape = (ENC_CAP * N_WIDE, HEAD_DEV * N_HEAD * HEAD_DIM)
    return jnp.clip(jax.random.normal(jax.random.fold_in(key, 21), shape, jnp.float32), -6.0, 6.0)


def draw_example_order(key, part):
    return layout(key)[0]


def draw_enc_bounds(key, part):
    return layout(key)[1]


def draw_dec_bounds(key, part):
    return layout(key)[2]


def draw_enc_len(key, part):
    return layout(key)[3]


def draw_dec_len(key, part):
    return layout(key)[4]


def draw_enc_key(key, part):
    return key_field(key).astype(jnp.bfloat16)


def draw_enc_query(key, part):
    base_keys = key_field(key)
    key = jax.random.fold_in(key, 3)
    shape = base_keys.shape
    entries = jnp.clip(jax.random.normal(jax.random.fold_in(key, 1), shape, jnp.float32), -6.0, 6.0)
    return entries.astype(jnp.bfloat16)


def steps_of(rng, shape, cuts, smallest, top_value):
    level = 1.0
    for dim, shards_of in cuts:
        draws = jax.random.uniform(jax.random.fold_in(jax.random.fold_in(rng, 6), dim), (shards_of,), jnp.float32, smallest / len(cuts), top_value / len(cuts))
        level = level * jnp.repeat(jnp.exp(draws), shape[dim] // shards_of).reshape((-1,) + (1,) * (len(shape) - 1 - dim))
    return level


def gaussian(stream_key, dims, width, most, split=(), kind=jnp.bfloat16):
    values = width * jax.random.normal(stream_key, dims, jnp.float32)
    if split:
        values = values * steps_of(stream_key, dims, split, -0.22, 0.18)
    return jnp.clip(values, -most, most).astype(kind)


def setup_inputs(seed: int = 0) -> dict:
    seeds = jax.random.split(jax.random.key(seed), 15)
    return {
        "hidden_in": gaussian(seeds[0], (ENC_TOKENS, D), 1.0, 6.0, ((0, 128), (1, 4))),
        "enc_query": draw_enc_query(jax.random.fold_in(seeds[14], 71), 0),
        "enc_key": draw_enc_key(jax.random.fold_in(seeds[14], 71), 0),
        "enc_value": gaussian(seeds[3], (ENC_TOKENS, HEADS * HEAD_DIM), 1.0, 6.0, ((0, 128), (1, 4))),
        "dec_query": gaussian(seeds[4], (DEC_TOKENS, HEADS * HEAD_DIM), 1.0, 6.0, ((0, 128), (1, 4))),
        "out_proj": gaussian(seeds[5], (HEADS * HEAD_DIM, D), (HEADS * HEAD_DIM) ** -0.5, 0.125, ((0, 4), (1, 128))),
        "key_proj": gaussian(seeds[6], (D, HEADS * HEAD_DIM), D ** -0.5, 0.09375, ((0, 128), (1, 4))),
        "value_proj": gaussian(seeds[7], (D, HEADS * HEAD_DIM), D ** -0.5, 0.09375, ((0, 128), (1, 4))),
        "norm_gain": jnp.clip(1.0 + 0.15 * jax.random.normal(seeds[8], (D,), jnp.float32), 0.25, 1.75),
        "enc_len": draw_enc_len(jax.random.fold_in(seeds[14], 71), 0),
        "dec_len": draw_dec_len(jax.random.fold_in(seeds[14], 71), 0),
        "example_order": draw_example_order(jax.random.fold_in(seeds[14], 71), 0),
        "enc_bounds": draw_enc_bounds(jax.random.fold_in(seeds[14], 71), 0),
        "dec_bounds": draw_dec_bounds(jax.random.fold_in(seeds[14], 71), 0),
    }


epsilon = 1e-06

def row_tags(lengths, example_order, bounds, device, row_count):
    example_count = example_order.shape[0]
    places = jnp.arange(example_count, dtype=jnp.int32)
    picked = (example_order[:, None] == places[None, :]).astype(jnp.int32)
    sorted_len = lax.optimization_barrier(jnp.sum(picked * lengths[None, :], axis=1)).astype(jnp.int32)
    end_rows = jnp.cumsum(sorted_len).astype(jnp.int32)
    start_rows = (end_rows - sorted_len).astype(jnp.int32)
    edge_index = jnp.arange(bounds.shape[0], dtype=jnp.int32)
    first_pos = jnp.sum(jnp.where(edge_index == device, bounds, 0)).astype(jnp.int32)
    last_pos = jnp.sum(jnp.where(edge_index == device + 1, bounds, 0)).astype(jnp.int32)
    row_base = jnp.sum(jnp.where(places == first_pos, start_rows, 0)).astype(jnp.int32)
    offsets = row_base + jnp.arange(row_count, dtype=jnp.int32)
    position = lax.optimization_barrier(jnp.sum((end_rows[None, :] <= offsets[:, None]).astype(jnp.int32), axis=1)).astype(jnp.int32)
    inside = (position < last_pos) & (device >= 0) & (device < bounds.shape[0] - 1)
    return jnp.where(inside, position, -1).astype(jnp.int32)

def attend(queries, key_rows, value_rows, query_tags, key_tags):
    query_count = queries.shape[0]
    heads_here = queries.shape[1] // HEAD_DIM
    query_heads = queries.astype(jnp.float32).reshape(query_count, heads_here, HEAD_DIM)
    key_heads = key_rows.astype(jnp.float32).reshape(key_rows.shape[0], heads_here, HEAD_DIM)
    value_heads = value_rows.astype(jnp.float32).reshape(value_rows.shape[0], heads_here, HEAD_DIM)
    scores = jnp.einsum('qhd,khd->hqk', query_heads, key_heads) * (1.0 / math.sqrt(HEAD_DIM))
    matched = (query_tags[:, None] == key_tags[None, :]) & (key_tags[None, :] >= 0)
    scores = jnp.where(matched[None], scores, -1e+30)
    row_max = lax.optimization_barrier(jnp.max(scores, axis=2, keepdims=True))
    weights = jnp.exp(scores - row_max) * matched[None].astype(jnp.float32)
    denominator = jnp.maximum(lax.optimization_barrier(jnp.sum(weights, axis=2, keepdims=True)), 1.0)
    shares = (weights / denominator).astype(jnp.bfloat16)
    context = jnp.einsum('hqk,khd->qhd', shares.astype(jnp.float32), value_heads)
    return context.reshape(query_count, -1).astype(jnp.bfloat16)

def reference(hidden_in, enc_query, enc_key, enc_value, dec_query, out_proj, key_proj, value_proj, norm_gain, enc_len, dec_len, example_order, enc_bounds, dec_bounds):
    devices = jnp.arange(N_WIDE, dtype=jnp.int32)
    enc_tags = jax.vmap(lambda device: row_tags(enc_len, example_order, enc_bounds, device, ENC_CAP))(devices)
    dec_tags = jax.vmap(lambda device: row_tags(dec_len, example_order, dec_bounds, device, DEC_CAP))(devices)
    head_cols = enc_query.shape[1]
    blocks = (enc_query.reshape(N_WIDE, ENC_CAP, head_cols), enc_key.reshape(N_WIDE, ENC_CAP, head_cols), enc_value.reshape(N_WIDE, ENC_CAP, head_cols), enc_tags)
    context = lax.map(lambda block: attend(block[0], block[1], block[2], block[3], block[3]), blocks)
    context = context.reshape(N_WIDE * ENC_CAP, head_cols)
    projected = jnp.dot(context, out_proj, preferred_element_type=jnp.float32)
    residual = hidden_in.astype(jnp.float32) + projected
    mean_square = lax.optimization_barrier(jnp.mean(residual * residual, axis=1, keepdims=True))
    normed = (residual * lax.rsqrt(mean_square + epsilon) * norm_gain[None, :]).astype(jnp.bfloat16)
    cross_keys = jnp.dot(normed, key_proj, preferred_element_type=jnp.float32).astype(jnp.bfloat16)
    cross_values = jnp.dot(normed, value_proj, preferred_element_type=jnp.float32).astype(jnp.bfloat16)
    key_blocks = jnp.pad(cross_keys.reshape(N_WIDE, ENC_CAP, head_cols), ((1, 0), (0, 0), (0, 0)))
    value_blocks = jnp.pad(cross_values.reshape(N_WIDE, ENC_CAP, head_cols), ((1, 0), (0, 0), (0, 0)))
    tag_blocks = jnp.pad(enc_tags, ((1, 0), (0, 0)), constant_values=-1)
    near_keys = jnp.concatenate([key_blocks[:-1], key_blocks[1:]], axis=1)
    near_values = jnp.concatenate([value_blocks[:-1], value_blocks[1:]], axis=1)
    near_tags = jnp.concatenate([tag_blocks[:-1], tag_blocks[1:]], axis=1)
    cross_blocks = (dec_query.reshape(N_WIDE, DEC_CAP, head_cols), near_keys, near_values, dec_tags, near_tags)
    cross_context = lax.map(lambda block: attend(block[0], block[1], block[2], block[3], block[4]), cross_blocks)
    return (residual.astype(jnp.bfloat16), cross_context.reshape(N_WIDE * DEC_CAP, head_cols))
```

```python
import jax
import jax.numpy as jnp
from jax import lax
from jax.experimental import pallas as pl
from jax.experimental.pallas import tpu as pltpu
from jax.sharding import PartitionSpec as P

MESH = pl.DeviceIdType.MESH
F32 = jnp.float32
BF16 = jnp.bfloat16

HEAD_DIM = 256
NZ = 16
NY = 4
NX = 4
NW = NY * NZ * 2
ROWS = 128
DROWS = 64
WID = 512
PIECE = 32
BLK = 2 * PIECE
FEAT = NZ * BLK
STEPS = NZ // 2
GROUP = NY * ROWS
EPSILON = 1e-06
SCALE = 1.0 / 16.0
VMEM_LIMIT = 60 * 1024 * 1024


def nt(a, b):
    return lax.dot_general(a, b, (((1,), (1,)), ((), ())), preferred_element_type=F32)


def nn(a, b):
    return lax.dot_general(a, b, (((1,), (0,)), ((), ())), preferred_element_type=F32)


def iota(shape, dim):
    return lax.broadcasted_iota(jnp.int32, shape, dim)


def attend(q, k, v, allowed):
    scores = jnp.where(allowed, nt(q, k) * SCALE, -1e30)
    weights = jnp.where(allowed, jnp.exp(scores - jnp.max(scores, axis=1, keepdims=True)), 0.0)
    total = jnp.maximum(jnp.sum(weights, axis=1, keepdims=True), 1.0)
    return nn((weights / total).astype(BF16), v).astype(BF16)


def kernel(
    hidden, q_hbm, k_hbm, v_hbm, dq_hbm, wo_hbm, wk_hbm, wv_hbm, gain_hbm,
    elen_hbm, dlen_hbm, order_hbm, ebound_hbm, dbound_hbm,
    enc_out, cross_out,
    q_ref, k_ref, v_ref, gain_ref, gain_col, lens_ref, ebound, dbound,
    wo, kvw, ctx, hid, hid_t, hid_c, hid_in, part, x1s, x1r, x2s, x2r, res_t, acc, sums, out_t, out_c, out_in,
    ys, yr, ss_s, ss_r, dq2, dres, drecv,
    in_sem, sib_s, sib_r, wo_s, wo_r, wof_s, wof_r, key_s, key_r, keyf_s, keyf_r,
    val_s, val_r, valf_s, valf_r, misc_s, misc_r, hid_s, hid_r, out_s, out_r, ctx_s, ctx_r, xs1, xr1, xs2, xr2, y_s, y_r, st_s, st_r,
):
    w = lax.axis_index("wide")
    x = lax.axis_index("head")
    c = w % 2
    z = (w // 2) % NZ
    y = w // (2 * NZ)
    step_dir = 1 - 2 * c

    def wide(yy, zz, cc):
        return (yy * NZ + zz) * 2 + cc

    sib = (w + step_dir, x)
    z_next = (wide(y, (z + step_dir + NZ) % NZ, c), x)
    z_prev = (wide(y, (z - step_dir + NZ) % NZ, c), x)
    ya, yb, y2 = y + 1 - 2 * (y % 2), NY - 1 - y, (y + 2) % NY
    y_a, y_b, y_2 = (wide(ya, z, c), x), (wide(yb, z, c), x), (wide(y2, z, c), x)
    x_a, x_b = (w, x + 1 - 2 * (x % 2)), (w, NX - 1 - x)
    upper, lower = ((w + 1) % NW, x), ((w + NW - 1) % NW, x)
    adder = (wide(x, z, c), x)
    off_diagonal = x != y
    greet = (sib, z_next, z_prev, y_a, y_b, y_2, x_a, x_b, upper, lower)

    def remote(src, dst, ss, rs, dev):
        return pltpu.make_async_remote_copy(
            src_ref=src, dst_ref=dst, send_sem=ss, recv_sem=rs, device_id=dev, device_id_type=MESH
        )

    barrier = pltpu.get_barrier_semaphore()
    for dev in greet:
        pl.semaphore_signal(barrier, inc=1, device_id=dev, device_id_type=MESH)

    mine = pl.ds(pl.multiple_of(z * BLK + c * PIECE, PIECE), PIECE)
    pairs = (
        (wo_hbm, wo.at[mine]), (elen_hbm, lens_ref.at[0]), (dlen_hbm, lens_ref.at[1]),
        (order_hbm, lens_ref.at[2]), (ebound_hbm, ebound), (dbound_hbm, dbound),
        (q_hbm, q_ref), (k_hbm, k_ref), (v_hbm, v_ref),
        (wk_hbm, kvw.at[0, mine]), (wv_hbm, kvw.at[1, mine]), (hidden, hid),
        (gain_hbm, gain_ref), (dq_hbm, dq2.at[pl.ds(0, DROWS)]),
    )
    loads = [pltpu.make_async_copy(a, b, in_sem.at[i]) for i, (a, b) in enumerate(pairs)]
    for load in loads:
        load.start()
    for load in loads[:6]:
        load.wait()

    n = 256
    onehot = jnp.where(lens_ref[2] == iota((n, n), 0), 1.0, 0.0).astype(BF16)
    lens = jnp.concatenate([lens_ref[0], lens_ref[1], jnp.zeros((6, n), jnp.int32)], axis=0)
    ordered = nn(lens.astype(F32).astype(BF16), onehot)
    upto = jnp.where(iota((n, n), 0) <= iota((n, n), 1), 1.0, 0.0).astype(BF16)
    ends = nn(ordered.astype(BF16), upto)
    place = iota((1, n), 1)

    def start(row, first):
        return jnp.sum(jnp.where(place < first, row, 0.0), axis=1, keepdims=True)

    def tags(ends_row, offsets, last):
        pos = jnp.sum(jnp.where(ends_row <= offsets, 1.0, 0.0), axis=1, keepdims=True)
        return jnp.where(pos < last, pos, -1.0)

    rows_i = iota((ROWS, 1), 0)
    enc_base = start(ordered[0:1], ebound[w])
    enc_col = tags(ends[0:1], enc_base + rows_i.astype(F32), ebound[w + 1].astype(F32))
    diag = iota((ROWS, ROWS), 0) == iota((ROWS, ROWS), 1)
    enc_row = jnp.sum(jnp.where(diag, enc_col, 0.0), axis=0, keepdims=True)
    enc_allowed = (enc_col == enc_row) & (enc_row >= 0.0)

    pl.semaphore_wait(barrier, len(greet))

    sib_wo = remote(wo.at[mine], wo.at[mine], sib_s.at[0], sib_r.at[0], sib)
    sib_wo.start()
    for load in loads[6:]:
        load.wait()
    sib_kv = remote(kvw.at[:, mine], kvw.at[:, mine], sib_s.at[1], sib_r.at[1], sib)
    sib_kv.start()
    dq_copy = remote(dq_hbm, dq2.at[pl.ds(DROWS, DROWS)], misc_s.at[1], misc_r.at[1], lower)
    dq_copy.start()

    def block(i):
        return pl.ds(pl.multiple_of(((i + NZ) % NZ) * BLK, BLK), BLK)

    def hop(i, buffer, ss, rs):
        at = buffer(z - step_dir * (i - 1))
        return remote(at, at, ss.at[i - 1], rs.at[i - 1], z_next)

    def got(i, buffer, ss, rs):
        at = buffer(z - step_dir * i)
        return remote(at, at, ss.at[i - 1], rs.at[i - 1], z_next)

    def fan(i, buffer, ss, rs):
        at = buffer(z - step_dir * i)
        return remote(at, at, ss.at[i - 1], rs.at[i - 1], sib)

    def fan_got(i, buffer, ss, rs):
        at = buffer(z + step_dir * i)
        return remote(at, at, ss.at[i - 1], rs.at[i - 1], sib)

    ring_wo = (lambda i: wo.at[block(i)], wo_s, wo_r)
    ring_key = (lambda i: kvw.at[0, block(i)], key_s, key_r)
    ring_val = (lambda i: kvw.at[1, block(i)], val_s, val_r)
    fan_wo = (ring_wo[0], wof_s, wof_r)
    fan_key = (ring_key[0], keyf_s, keyf_r)
    fan_val = (ring_val[0], valf_s, valf_r)

    def pass_on(i, ring, side):
        got(i, *ring).wait_recv()

        @pl.when(i < STEPS)
        def _():
            hop(i + 1, *ring).start()
            fan(i, *side).start()

    def pair(h):
        low = jnp.where(h == STEPS, z, z - h)
        return low, z + h

    def round_one(h):
        return [
            remote(
                x1s.at[h - 1, pl.ds(half * BLK, BLK)], x1r.at[h - 1, pl.ds(half * BLK, BLK)],
                xs1.at[h - 1, half], xr1.at[h - 1, half], (x_a, x_b)[half],
            )
            for half in range(2)
        ]

    def round_two(h):
        return [
            remote(
                x2s.at[h - 1, pl.ds(half * BLK, BLK)], x2r.at[h - 1, pl.ds(half * BLK, BLK)],
                xs2.at[h - 1, half], xr2.at[h - 1, half], (x_b, x_a)[half],
            )
            for half in range(2)
        ]

    away = (y - x + NY) % NY

    def hid_copy(h):
        at = jnp.maximum(away, 1) - 1
        return remote(hid_c.at[h - 1], hid_in.at[h - 1, y], hid_s.at[h - 1], hid_r.at[h - 1, at], adder)

    def hid_got(h, d):
        at = hid_in.at[h - 1, (y + d) % NY]
        return remote(at, at, hid_s.at[h - 1], hid_r.at[h - 1, d - 1], adder)

    def out_copy(h, d):
        g = (y + d) % NY
        return remote(
            out_c.at[h - 1, g], out_in.at[h - 1], out_s.at[h - 1, d - 1], out_r.at[h - 1],
            (wide(g, z, c), x),
        )

    sib_wo.wait_recv()
    hop(1, *ring_wo).start()

    def ctx_copy(head, slot, index, dev):
        at = ctx.at[head, slot]
        return remote(at, at, ctx_s.at[index], ctx_r.at[index], dev)

    ctx_sent = []
    for head in range(2):
        cols = slice(head * HEAD_DIM, (head + 1) * HEAD_DIM)
        ctx[head, y] = attend(q_ref[:, cols], k_ref[:, cols], v_ref[:, cols], enc_allowed)
        for side, dev in enumerate((y_a, y_b)):
            copy = ctx_copy(head, y, head * 2 + side, dev)
            copy.start()
            ctx_sent.append(copy)
        if head == 0:
            sib_kv.wait_recv()
            hop(1, *ring_key).start()
            hop(1, *ring_val).start()

    pass_on(1, ring_wo, fan_wo)
    ctx_copy(0, ya, 0, y_a).wait_recv()
    ctx_sent.append(ctx_copy(0, ya, 4, y_b))
    ctx_sent[-1].start()
    ctx_copy(1, yb, 3, y_b).wait_recv()
    ctx_sent.append(ctx_copy(1, yb, 5, y_a))
    ctx_sent[-1].start()

    for i in range(FEAT // 128):
        cols = slice(i * 128, (i + 1) * 128)
        hid_t[cols, :] = jnp.transpose(hid[:, cols].astype(F32))
    for h in range(1, STEPS + 1):
        p0, p1 = pair(h)
        hid_c[h - 1] = jnp.concatenate([hid_t[block(p0), :], hid_t[block(p1), :]], axis=0).astype(BF16)

    @pl.when(jnp.logical_not(off_diagonal))
    def _():
        for h in range(1, STEPS + 1):
            hid_in[h - 1, y] = hid_c[h - 1]

    @pl.when(off_diagonal)
    def _():
        hid_copy(1).start()
        hid_copy(2).start()

    pass_on(2, ring_wo, fan_wo)
    pass_on(1, ring_key, fan_key)
    pass_on(1, ring_val, fan_val)
    for i in range(FEAT // 128):
        cols = slice(i * 128, (i + 1) * 128)
        row = gain_ref[pl.ds(y * (FEAT // 128) + i, 1), :]
        column = jnp.sum(jnp.where(diag, row, 0.0), axis=1, keepdims=True)
        gain_col[cols, :] = jnp.broadcast_to(column, (128, 128))
    acc[...] = jnp.zeros_like(acc)
    sums[...] = jnp.zeros_like(sums)
    ctx_copy(0, yb, 1, y_b).wait_recv()
    ctx_copy(1, ya, 2, y_a).wait_recv()
    ctx_copy(0, y2, 4, y_b).wait_recv()
    ctx_copy(1, y2, 5, y_a).wait_recv()

    def kv_weights(i, s):
        blocks = pair(2 * s + 1) + pair(2 * s + 2)
        return jnp.concatenate([kvw[i, block(p), :] for p in blocks], axis=0)

    @pl.loop(1, STEPS + 5)
    def _(h):
        @pl.when(h <= STEPS - 2)
        def _():
            pass_on(h + 2, ring_wo, fan_wo)

            @pl.when(off_diagonal)
            def _():
                hid_copy(h + 2).start()

        @pl.when((h >= 3) & (h <= STEPS + 2))
        def _():
            t = h - 2
            for copy in round_one(t):
                copy.wait_recv()
            total = part[t - 1] + x1r[t - 1].astype(F32)
            part[t - 1] = total
            x2s[t - 1] = total.astype(BF16)
            for copy in round_two(t):
                copy.start()

        @pl.when(h < STEPS)
        def _():
            pass_on(h + 1, ring_key, fan_key)

        @pl.when(h <= STEPS)
        def _():
            @pl.when(h < STEPS)
            def _():
                fan_got(h, *fan_wo).wait_recv()

            p0, p1 = pair(h)
            weights = jnp.concatenate([wo[block(p0), :], wo[block(p1), :]], axis=0)
            part[h - 1] = nt(weights[:, 0:HEAD_DIM], ctx[0].reshape(GROUP, HEAD_DIM)) + nt(
                weights[:, HEAD_DIM:WID], ctx[1].reshape(GROUP, HEAD_DIM)
            )

            @pl.when(jnp.logical_not(off_diagonal))
            def _():
                for d in range(1, NY):
                    hid_got(h, d).wait_recv()
                for g in range(NY):
                    rows = slice(g * ROWS, (g + 1) * ROWS)
                    part[h - 1, :, rows] = part[h - 1, :, rows] + hid_in[h - 1, g].astype(F32)

            x1s[h - 1] = part[h - 1].astype(BF16)
            for copy in round_one(h):
                copy.start()

            @pl.when(h < STEPS)
            def _():
                pass_on(h + 1, ring_val, fan_val)

        @pl.when(h >= 5)
        def _():
            t = h - 4
            for copy in round_two(t):
                copy.wait_recv()
            p0, p1 = pair(t)
            total = part[t - 1] + x2r[t - 1].astype(F32)
            part[t - 1] = total
            sums[...] += jnp.sum(total * total, axis=0, keepdims=True)
            gain = jnp.concatenate([gain_col[block(p0), :], gain_col[block(p1), :]], axis=0)
            total = total * jnp.concatenate([gain] * NY, axis=1)
            at = pl.ds(pl.multiple_of(((t - 1) % 2) * 128, 128), 128)
            res_t[(t - 1) // 2, :, at] = jnp.transpose(total).astype(BF16)

            @pl.when(jnp.logical_not(off_diagonal))
            def _():
                for g in range(NY):
                    out_c[t - 1, g] = part[t - 1, :, g * ROWS : (g + 1) * ROWS].astype(BF16)
                for d in range(1, NY):
                    out_copy(t, d).start()
                out_in[t - 1] = out_c[t - 1, y]

            @pl.when(t < STEPS)
            def _():
                fan_got(t, *fan_key).wait_recv()
                fan_got(t, *fan_val).wait_recv()

            @pl.when((t % 2 == 0) & (t < STEPS))
            def _():
                s = t // 2 - 1
                for i in range(2):
                    acc[i] += nn(res_t[s], kv_weights(i, s)).reshape(NY, ROWS, WID)

    def lanes(g):
        return pl.ds(pl.multiple_of(g * ROWS, ROWS), ROWS)

    def finished(i, g):
        s = STEPS // 2 - 1
        return acc[i, g] + nn(res_t[s, lanes(g), :], kv_weights(i, s))

    y_copies = [remote(ys.at[i], yr.at[i], y_s.at[i], y_r.at[i], (y_a, y_b)[i % 2]) for i in range(6)]
    ys[0] = finished(0, y2).astype(BF16)
    y_copies[0].start()
    ys[1] = finished(1, y2).astype(BF16)
    y_copies[1].start()
    ys[2] = finished(0, ya).astype(BF16)
    y_copies[2].start()
    ys[3] = finished(1, yb).astype(BF16)
    y_copies[3].start()
    stat_copies = []
    for i, (g, dev) in enumerate(((ya, y_a), (yb, y_b), (y2, y_2))):
        ss_s[i] = sums[:, lanes(g)]
        copy = remote(ss_s.at[i], ss_r.at[i], st_s.at[i], st_r.at[i], dev)
        copy.start()
        stat_copies.append(copy)
    to_a = finished(1, ya)
    y_copies[1].wait_recv()
    ys[4] = (to_a + yr[1].astype(F32)).astype(BF16)
    y_copies[4].start()
    to_b = finished(0, yb)
    y_copies[0].wait_recv()
    ys[5] = (to_b + yr[0].astype(F32)).astype(BF16)
    y_copies[5].start()
    acc[0, y] = finished(0, y)
    acc[1, y] = finished(1, y)

    for h in range(1, STEPS + 1):
        @pl.when(off_diagonal)
        def _():
            out_copy(h, 1).wait_recv()

        p0, p1 = pair(h)
        out_t[block(p0), :] = out_in[h - 1, 0:BLK, :].astype(F32)
        out_t[block(p1), :] = out_in[h - 1, BLK : 2 * BLK, :].astype(F32)
    for i in range(FEAT // 128):
        cols = slice(i * 128, (i + 1) * 128)
        enc_out[:, cols] = jnp.transpose(out_t[cols, :]).astype(BF16)

    lower_half = rows_i < DROWS
    above_end = jnp.minimum(w + 2, NW)
    base = jnp.where(lower_half, start(ordered[1:2], dbound[w]), start(ordered[1:2], dbound[w + 1]))
    last = jnp.where(lower_half, dbound[w + 1].astype(F32), dbound[above_end].astype(F32))
    offset = (rows_i % DROWS).astype(F32)
    dec_col = tags(ends[1:2], base + offset, last)
    dec_allowed = (dec_col == enc_row) & (enc_row >= 0.0)

    for copy in stat_copies:
        copy.wait_recv()
    square = sums[:, lanes(y)] + ss_r[0] + ss_r[1] + ss_r[2]
    square_col = jnp.sum(jnp.where(diag, square[0:1], 0.0), axis=1, keepdims=True)
    norm = lax.rsqrt(square_col * (1.0 / (NY * FEAT)) + EPSILON)
    dq_copy.wait_recv()

    y_copies[2].wait_recv()
    y_copies[3].wait_recv()
    y_copies[4].wait_recv()
    near_values = acc[1, y] + yr[3].astype(F32) + yr[4].astype(F32)
    near_values = (near_values * norm).astype(BF16)
    y_copies[5].wait_recv()
    near_keys = acc[0, y] + yr[2].astype(F32) + yr[5].astype(F32)
    near_keys = (near_keys * norm).astype(BF16)

    def near(rows, head):
        cols = slice(head * HEAD_DIM, (head + 1) * HEAD_DIM)
        return attend(dq2[rows, cols], near_keys[:, cols], near_values[:, cols], dec_allowed[rows])

    for head in range(2):
        dres[:, head * HEAD_DIM : (head + 1) * HEAD_DIM] = near(slice(DROWS, ROWS), head)
    up = remote(dres, drecv, misc_s.at[3], misc_r.at[3], upper)
    up.start()
    found = [near(slice(0, DROWS), head) for head in range(2)]

    for copy in [sib_wo, sib_kv, dq_copy] + ctx_sent + stat_copies + y_copies:
        copy.wait_send()

    @pl.loop(1, STEPS + 1)
    def _(h):
        hop(h, *ring_wo).wait_send()
        hop(h, *ring_key).wait_send()
        hop(h, *ring_val).wait_send()
        for copy in round_one(h) + round_two(h):
            copy.wait_send()

        @pl.when(h < STEPS)
        def _():
            fan(h, *fan_wo).wait_send()
            fan(h, *fan_key).wait_send()
            fan(h, *fan_val).wait_send()

        @pl.when(off_diagonal)
        def _():
            hid_copy(h).wait_send()

        @pl.when(jnp.logical_not(off_diagonal))
        def _():
            for d in range(1, NY):
                out_copy(h, d).wait_send()

    up.wait()
    cross_out[...] = jnp.concatenate(found, axis=1) + drecv[...]


def body(
    hidden_in, enc_query, enc_key, enc_value, dec_query, out_proj, key_proj, value_proj,
    norm_gain, enc_len, dec_len, example_order, enc_bounds, dec_bounds,
):
    vmem = pl.BlockSpec(memory_space=pltpu.VMEM)
    anywhere = pl.BlockSpec(memory_space=pl.ANY)
    dma = pltpu.SemaphoreType.DMA
    gain = norm_gain.reshape(32, 128)
    return pl.pallas_call(
        kernel,
        out_shape=(
            jax.ShapeDtypeStruct((ROWS, FEAT), BF16),
            jax.ShapeDtypeStruct((DROWS, WID), BF16),
        ),
        in_specs=[anywhere] * 14,
        out_specs=(vmem, vmem),
        scratch_shapes=[
            pltpu.VMEM((ROWS, WID), BF16),
            pltpu.VMEM((ROWS, WID), BF16),
            pltpu.VMEM((ROWS, WID), BF16),
            pltpu.VMEM(gain.shape, F32),
            pltpu.VMEM((FEAT, 128), F32),
            pltpu.VMEM((3, 1, 256), jnp.int32),
            pltpu.SMEM(enc_bounds.shape, jnp.int32),
            pltpu.SMEM(dec_bounds.shape, jnp.int32),
            pltpu.VMEM((FEAT, WID), BF16),
            pltpu.VMEM((2, FEAT, WID), BF16),
            pltpu.VMEM((2, NY, ROWS, HEAD_DIM), BF16),
            pltpu.VMEM((ROWS, FEAT), BF16),
            pltpu.VMEM((FEAT, ROWS), F32),
            pltpu.VMEM((STEPS, 2 * BLK, ROWS), BF16),
            pltpu.VMEM((STEPS, NY, 2 * BLK, ROWS), BF16),
            pltpu.VMEM((STEPS, 2 * BLK, GROUP), F32),
            pltpu.VMEM((STEPS, 2 * BLK, GROUP), BF16),
            pltpu.VMEM((STEPS, 2 * BLK, GROUP), BF16),
            pltpu.VMEM((STEPS, 2 * BLK, GROUP), BF16),
            pltpu.VMEM((STEPS, 2 * BLK, GROUP), BF16),
            pltpu.VMEM((STEPS // 2, GROUP, 4 * BLK), BF16),
            pltpu.VMEM((2, NY, ROWS, WID), F32),
            pltpu.VMEM((8, GROUP), F32),
            pltpu.VMEM((FEAT, ROWS), F32),
            pltpu.VMEM((STEPS, NY, 2 * BLK, ROWS), BF16),
            pltpu.VMEM((STEPS, 2 * BLK, ROWS), BF16),
            pltpu.VMEM((6, ROWS, WID), BF16),
            pltpu.VMEM((6, ROWS, WID), BF16),
            pltpu.VMEM((3, 8, ROWS), F32),
            pltpu.VMEM((3, 8, ROWS), F32),
            pltpu.VMEM((2 * DROWS, WID), BF16),
            pltpu.VMEM((DROWS, WID), BF16),
            pltpu.VMEM((DROWS, WID), BF16),
            dma((14,)),
            dma((2,)), dma((2,)),
            dma((STEPS,)), dma((STEPS,)),
            dma((STEPS,)), dma((STEPS,)),
            dma((STEPS,)), dma((STEPS,)),
            dma((STEPS,)), dma((STEPS,)),
            dma((STEPS,)), dma((STEPS,)),
            dma((STEPS,)), dma((STEPS,)),
            dma((4,)), dma((4,)),
            dma((STEPS,)), dma((STEPS, NY - 1)),
            dma((STEPS, NY - 1)), dma((STEPS,)),
            dma((6,)), dma((6,)),
            dma((STEPS, 2)), dma((STEPS, 2)),
            dma((STEPS, 2)), dma((STEPS, 2)),
            dma((6,)), dma((6,)),
            dma((3,)), dma((3,)),
        ],
        compiler_params=pltpu.CompilerParams(
            collective_id=0, has_side_effects=True, vmem_limit_bytes=VMEM_LIMIT
        ),
        name="encoder_to_cross",
    )(
        hidden_in, enc_query, enc_key, enc_value, dec_query, out_proj.T, key_proj, value_proj,
        gain, enc_len.reshape(1, 256), dec_len.reshape(1, 256),
        example_order.reshape(1, 256), enc_bounds, dec_bounds,
    )


def solution(mesh):
    return jax.shard_map(
        body,
        mesh=mesh,
        in_specs=(
            P("wide", "head"), P("wide", "head"), P("wide", "head"), P("wide", "head"),
            P("wide", "head"), P("head", "wide"), P("wide", "head"), P("wide", "head"),
            P(), P(), P(), P(), P(), P(),
        ),
        out_specs=(P("wide", "head"), P("wide", "head")),
        check_vma=False,
    )
```

```python
import jax
import jax.numpy as jnp
from jax import lax
from jax.experimental import pallas as pl
from jax.experimental.pallas import tpu as pltpu
from jax.sharding import PartitionSpec as P

MESH = pl.DeviceIdType.MESH
F32 = jnp.float32
BF16 = jnp.bfloat16

HEAD_DIM = 256
NZ = 16
NY = 4
NX = 4
NW = NY * NZ * 2
ROWS = 128
DROWS = 64
WID = 512
PIECE = 32
BLK = 2 * PIECE
FEAT = NZ * BLK
STEPS = NZ // 2
GROUP = NY * ROWS
EPSILON = 1e-06
SCALE = 1.0 / 16.0
VMEM_LIMIT = 60 * 1024 * 1024


def nt(a, b):
    return lax.dot_general(a, b, (((1,), (1,)), ((), ())), preferred_element_type=F32)


def nn(a, b):
    return lax.dot_general(a, b, (((1,), (0,)), ((), ())), preferred_element_type=F32)


def iota(shape, dim):
    return lax.broadcasted_iota(jnp.int32, shape, dim)


def attend(q, k, v, allowed):
    scores = jnp.where(allowed, nt(q, k) * SCALE, -1e30)
    weights = jnp.where(allowed, jnp.exp(scores - jnp.max(scores, axis=1, keepdims=True)), 0.0)
    total = jnp.maximum(jnp.sum(weights, axis=1, keepdims=True), 1.0)
    return nn((weights / total).astype(BF16), v).astype(BF16)


def kernel(
    hidden, q_hbm, k_hbm, v_hbm, dq_hbm, wo_hbm, wk_hbm, wv_hbm, gain_hbm,
    elen_hbm, dlen_hbm, order_hbm, ebound_hbm, dbound_hbm,
    enc_out, cross_out,
    q_ref, k_ref, v_ref, gain_ref, gain_col, lens_ref, ebound, dbound,
    wo, kvw, ctx, hid, hid_t, hid_c, hid_in, part, x1s, x1r, x2s, x2r, res_t, acc, sums, out_t, out_c, out_in,
    ys, yr, ss_r, dq2, dres, drecv,
    in_sem, sib_s, sib_r, wo_s, wo_r, wof_s, wof_r, key_s, key_r, keyf_s, keyf_r,
    val_s, val_r, valf_s, valf_r, misc_s, misc_r, hid_s, hid_r, out_s, out_r, ctx_s, ctx_r, xs1, xr1, xs2, xr2, gs, gr, y_s, y_r, st_s, st_r,
):
    w = lax.axis_index("wide")
    x = lax.axis_index("head")
    c = w % 2
    z = (w // 2) % NZ
    y = w // (2 * NZ)
    step_dir = 1 - 2 * c

    def wide(yy, zz, cc):
        return (yy * NZ + zz) * 2 + cc

    sib = (w + step_dir, x)
    z_next = (wide(y, (z + step_dir + NZ) % NZ, c), x)
    z_prev = (wide(y, (z - step_dir + NZ) % NZ, c), x)
    ya, yb, y2 = y + 1 - 2 * (y % 2), NY - 1 - y, (y + 2) % NY
    y_a, y_b, y_2 = (wide(ya, z, c), x), (wide(yb, z, c), x), (wide(y2, z, c), x)
    x_a, x_b = (w, x + 1 - 2 * (x % 2)), (w, NX - 1 - x)
    upper, lower = ((w + 1) % NW, x), ((w + NW - 1) % NW, x)
    adder = (wide(x, z, c), x)
    off_diagonal = x != y
    greet = (sib, z_next, z_prev, y_a, y_b, y_2, x_a, x_b, upper, lower)

    def remote(src, dst, ss, rs, dev):
        return pltpu.make_async_remote_copy(
            src_ref=src, dst_ref=dst, send_sem=ss, recv_sem=rs, device_id=dev, device_id_type=MESH
        )

    barrier = pltpu.get_barrier_semaphore()
    for dev in greet:
        pl.semaphore_signal(barrier, inc=1, device_id=dev, device_id_type=MESH)

    mine = pl.ds(pl.multiple_of(z * BLK + c * PIECE, PIECE), PIECE)
    pairs = (
        (wo_hbm, wo.at[mine]), (elen_hbm, lens_ref.at[0]), (dlen_hbm, lens_ref.at[1]),
        (order_hbm, lens_ref.at[2]), (ebound_hbm, ebound), (dbound_hbm, dbound),
        (q_hbm, q_ref), (k_hbm, k_ref), (v_hbm, v_ref),
        (wk_hbm, kvw.at[0, mine]), (wv_hbm, kvw.at[1, mine]), (hidden, hid),
        (gain_hbm, gain_ref), (dq_hbm, dq2.at[pl.ds(0, DROWS)]),
    )
    loads = [pltpu.make_async_copy(a, b, in_sem.at[i]) for i, (a, b) in enumerate(pairs)]
    for load in loads:
        load.start()
    for load in loads[:6]:
        load.wait()

    n = 256
    onehot = jnp.where(lens_ref[2] == iota((n, n), 0), 1.0, 0.0).astype(BF16)
    lens = jnp.concatenate([lens_ref[0], lens_ref[1], jnp.zeros((6, n), jnp.int32)], axis=0)
    ordered = nn(lens.astype(F32).astype(BF16), onehot)
    upto = jnp.where(iota((n, n), 0) <= iota((n, n), 1), 1.0, 0.0).astype(BF16)
    ends = nn(ordered.astype(BF16), upto)
    place = iota((1, n), 1)

    def start(row, first):
        return jnp.sum(jnp.where(place < first, row, 0.0), axis=1, keepdims=True)

    def tags(ends_row, offsets, last):
        pos = jnp.sum(jnp.where(ends_row <= offsets, 1.0, 0.0), axis=1, keepdims=True)
        return jnp.where(pos < last, pos, -1.0)

    rows_i = iota((ROWS, 1), 0)
    enc_base = start(ordered[0:1], ebound[w])
    enc_col = tags(ends[0:1], enc_base + rows_i.astype(F32), ebound[w + 1].astype(F32))
    diag = iota((ROWS, ROWS), 0) == iota((ROWS, ROWS), 1)
    enc_row = jnp.sum(jnp.where(diag, enc_col, 0.0), axis=0, keepdims=True)
    enc_allowed = (enc_col == enc_row) & (enc_row >= 0.0)

    pl.semaphore_wait(barrier, len(greet))

    sib_wo = remote(wo.at[mine], wo.at[mine], sib_s.at[0], sib_r.at[0], sib)
    sib_wo.start()
    for load in loads[6:]:
        load.wait()
    sib_kv = remote(kvw.at[:, mine], kvw.at[:, mine], sib_s.at[1], sib_r.at[1], sib)
    sib_kv.start()
    dq_copy = remote(dq_hbm, dq2.at[pl.ds(DROWS, DROWS)], misc_s.at[1], misc_r.at[1], lower)
    dq_copy.start()

    def block(i):
        return pl.ds(pl.multiple_of(((i + NZ) % NZ) * BLK, BLK), BLK)

    def hop(i, buffer, ss, rs):
        at = buffer(z - step_dir * (i - 1))
        return remote(at, at, ss.at[i - 1], rs.at[i - 1], z_next)

    def got(i, buffer, ss, rs):
        at = buffer(z - step_dir * i)
        return remote(at, at, ss.at[i - 1], rs.at[i - 1], z_next)

    def fan(i, buffer, ss, rs):
        at = buffer(z - step_dir * i)
        return remote(at, at, ss.at[i - 1], rs.at[i - 1], sib)

    def fan_got(i, buffer, ss, rs):
        at = buffer(z + step_dir * i)
        return remote(at, at, ss.at[i - 1], rs.at[i - 1], sib)

    ring_wo = (lambda i: wo.at[block(i)], wo_s, wo_r)
    ring_key = (lambda i: kvw.at[0, block(i)], key_s, key_r)
    ring_val = (lambda i: kvw.at[1, block(i)], val_s, val_r)
    fan_wo = (ring_wo[0], wof_s, wof_r)
    fan_key = (ring_key[0], keyf_s, keyf_r)
    fan_val = (ring_val[0], valf_s, valf_r)

    def pass_on(i, ring, side):
        got(i, *ring).wait_recv()

        @pl.when(i < STEPS)
        def _():
            hop(i + 1, *ring).start()
            fan(i, *side).start()

    def pair(h):
        low = jnp.where(h == STEPS, z, z - h)
        return low, z + h

    halves = (pl.ds(0, BLK), pl.ds(BLK, BLK))

    def round_one(h):
        return [
            remote(
                x1s.at[h - 1, :, rows], x1r.at[h - 1, :, rows],
                xs1.at[h - 1, i], xr1.at[h - 1, i], (x_a, x_b)[i],
            )
            for i, rows in enumerate(halves)
        ]

    def round_two(h):
        return [
            remote(
                x2s.at[h - 1, :, rows], x2r.at[h - 1, :, rows],
                xs2.at[h - 1, i], xr2.at[h - 1, i], (x_b, x_a)[i],
            )
            for i, rows in enumerate(halves)
        ]

    def group_one(h, g):
        at = 0 if h == 1 else 1
        return [
            remote(
                x1s.at[h - 1, g, rows], x1r.at[h - 1, g, rows],
                gs.at[at, g, i], gr.at[at, g, i], (x_a, x_b)[i],
            )
            for i, rows in enumerate(halves)
        ]

    def group_two(h, g):
        return [
            remote(
                x2s.at[h - 1, g, rows], x2r.at[h - 1, g, rows],
                gs.at[2, g, i], gr.at[2, g, i], (x_b, x_a)[i],
            )
            for i, rows in enumerate(halves)
        ]

    away = (y - x + NY) % NY

    def hid_copy(h):
        at = jnp.maximum(away, 1) - 1
        return remote(hid_c.at[h - 1], hid_in.at[h - 1, y], hid_s.at[h - 1], hid_r.at[h - 1, at], adder)

    def hid_got(h, d):
        at = hid_in.at[h - 1, (y + d) % NY]
        return remote(at, at, hid_s.at[h - 1], hid_r.at[h - 1, d - 1], adder)

    def out_copy(h, d):
        g = (y + d) % NY
        return remote(
            out_c.at[h - 1, g], out_in.at[h - 1], out_s.at[h - 1, d - 1], out_r.at[h - 1],
            (wide(g, z, c), x),
        )

    sib_wo.wait_recv()
    hop(1, *ring_wo).start()

    def ctx_copy(head, slot, index, dev):
        at = ctx.at[head, slot]
        return remote(at, at, ctx_s.at[index], ctx_r.at[index], dev)

    ctx_sent = []
    for head in range(2):
        cols = slice(head * HEAD_DIM, (head + 1) * HEAD_DIM)
        ctx[head, y] = attend(q_ref[:, cols], k_ref[:, cols], v_ref[:, cols], enc_allowed)
        for side, dev in enumerate((y_a, y_b)):
            copy = ctx_copy(head, y, head * 2 + side, dev)
            copy.start()
            ctx_sent.append(copy)
        if head == 0:
            sib_kv.wait_recv()
            hop(1, *ring_key).start()
            hop(1, *ring_val).start()

    for i in range(FEAT // 128):
        cols = slice(i * 128, (i + 1) * 128)
        hid_t[cols, :] = jnp.transpose(hid[:, cols].astype(F32))

    def of_pair(ref, h):
        p0, p1 = pair(h)
        return jnp.concatenate([ref[block(p0), :], ref[block(p1), :]], axis=0)

    @pl.loop(1, STEPS + 1)
    def _(h):
        hid_c[h - 1] = of_pair(hid_t, h).astype(BF16)

    @pl.when(off_diagonal)
    def _():
        hid_copy(1).start()
        hid_copy(2).start()

    @pl.when(jnp.logical_not(off_diagonal))
    def _():
        for h in range(1, STEPS + 1):
            hid_in[h - 1, y] = hid_c[h - 1]

    pass_on(1, ring_wo, fan_wo)

    def project_group(h, g, d):
        weights = of_pair(wo, h)
        part[h - 1, g] = nt(weights[:, 0:HEAD_DIM], ctx[0, g]) + nt(weights[:, HEAD_DIM:WID], ctx[1, g])

        @pl.when(jnp.logical_not(off_diagonal))
        def _():
            if d:
                hid_got(h, d).wait_recv()
            part[h - 1, g] = part[h - 1, g] + hid_in[h - 1, g].astype(F32)

        x1s[h - 1, g] = part[h - 1, g].astype(BF16)
        for copy in group_one(h, g):
            copy.start()

    d_a, d_b = (ya - y + NY) % NY, (yb - y + NY) % NY

    def project_other(h, which):
        if which == 2:
            project_group(h, y2, 2)
            return
        g, d = ((ya, d_a), (yb, d_b))[which]
        weights = of_pair(wo, h)
        part[h - 1, g] = nt(weights[:, 0:HEAD_DIM], ctx[0, g]) + nt(weights[:, HEAD_DIM:WID], ctx[1, g])

        @pl.when(jnp.logical_not(off_diagonal))
        def _():
            hid_got(h, d).wait_recv()
            part[h - 1, g] = part[h - 1, g] + hid_in[h - 1, g].astype(F32)

        x1s[h - 1, g] = part[h - 1, g].astype(BF16)
        for copy in group_one(h, g):
            copy.start()

    fan_got(1, *fan_wo).wait_recv()
    project_group(1, y, 0)
    ctx_copy(0, ya, 0, y_a).wait_recv()
    ctx_sent.append(ctx_copy(0, ya, 4, y_b))
    ctx_sent[-1].start()
    ctx_copy(1, yb, 3, y_b).wait_recv()
    ctx_sent.append(ctx_copy(1, yb, 5, y_a))
    ctx_sent[-1].start()
    pass_on(2, ring_wo, fan_wo)
    ctx_copy(1, ya, 2, y_a).wait_recv()
    project_other(1, 0)
    ctx_copy(0, yb, 1, y_b).wait_recv()
    project_other(1, 1)
    pass_on(1, ring_key, fan_key)
    pass_on(1, ring_val, fan_val)
    for i in range(FEAT // 128):
        cols = slice(i * 128, (i + 1) * 128)
        row = gain_ref[pl.ds(y * (FEAT // 128) + i, 1), :]
        column = jnp.sum(jnp.where(diag, row, 0.0), axis=1, keepdims=True)
        gain_col[cols, :] = jnp.broadcast_to(column, (128, 128))
    acc[...] = jnp.zeros_like(acc)
    sums[...] = jnp.zeros_like(sums)
    ctx_copy(0, y2, 4, y_b).wait_recv()
    ctx_copy(1, y2, 5, y_a).wait_recv()
    project_other(1, 2)

    def kv_weights(i, s):
        blocks = pair(2 * s + 1) + pair(2 * s + 2)
        return jnp.concatenate([kvw[i, block(p), :] for p in blocks], axis=0)

    def project(h):
        fan_got(h, *fan_wo).wait_recv()
        weights = of_pair(wo, h)
        term = nt(weights[:, 0:HEAD_DIM], ctx[0].reshape(GROUP, HEAD_DIM)) + nt(
            weights[:, HEAD_DIM:WID], ctx[1].reshape(GROUP, HEAD_DIM)
        )
        for g in range(NY):
            part[h - 1, g] = term[:, g * ROWS : (g + 1) * ROWS]

        @pl.when(jnp.logical_not(off_diagonal))
        def _():
            for d in range(1, NY):
                hid_got(h, d).wait_recv()
            part[h - 1] = part[h - 1] + hid_in[h - 1].astype(F32)

        x1s[h - 1] = part[h - 1].astype(BF16)
        for copy in round_one(h):
            copy.start()

    def exchange(h):
        @pl.when(h == 1)
        def _():
            for g in range(NY):
                for copy in group_one(1, g):
                    copy.wait_recv()

        @pl.when(h > 1)
        def _():
            for copy in round_one(h):
                copy.wait_recv()

        total = part[h - 1] + x1r[h - 1].astype(F32)
        part[h - 1] = total
        x2s[h - 1] = total.astype(BF16)
        for copy in round_two(h):
            copy.start()

    def finish_group(h, g):
        total = part[h - 1, g] + x2r[h - 1, g].astype(F32)
        sums[g] += jnp.sum(total * total, axis=0, keepdims=True)
        at = pl.ds(pl.multiple_of(((h - 1) % 2) * 128, 128), 128)
        res_t[(h - 1) // 2, g, :, at] = jnp.transpose(total * of_pair(gain_col, h)).astype(BF16)
        out_c[h - 1, g] = total.astype(BF16)

    def send_home(h):
        @pl.when(jnp.logical_not(off_diagonal))
        def _():
            for d in range(1, NY):
                out_copy(h, d).start()
            out_in[h - 1] = out_c[h - 1, y]

    def accumulate(s):
        for i in range(2):
            acc[i] += nn(res_t[s].reshape(GROUP, 4 * BLK), kv_weights(i, s)).reshape(NY, ROWS, WID)

    @pl.loop(1, STEPS + 4)
    def _(h):
        @pl.when(h <= STEPS - 2)
        def _():
            pass_on(h + 2, ring_wo, fan_wo)

            @pl.when(off_diagonal)
            def _():
                hid_copy(h + 2).start()

        @pl.when((h >= 3) & (h <= STEPS + 1))
        def _():
            exchange(h - 2)

        @pl.when(h < STEPS)
        def _():
            pass_on(h + 1, ring_key, fan_key)

            @pl.when(h > 1)
            def _():
                project(h)

            pass_on(h + 1, ring_val, fan_val)

        @pl.when(h == STEPS)
        def _():
            for which in (2, 0, 1):
                project_other(STEPS, which)
            project_group(STEPS, y, 0)

        @pl.when(h == STEPS + 2)
        def _():
            for g in (y2, ya, yb, y):
                for copy in group_one(STEPS, g):
                    copy.wait_recv()
                total = part[STEPS - 1, g] + x1r[STEPS - 1, g].astype(F32)
                part[STEPS - 1, g] = total
                x2s[STEPS - 1, g] = total.astype(BF16)
                for copy in group_two(STEPS, g):
                    copy.start()

        @pl.when(h >= 5)
        def _():
            t = h - 4
            for copy in round_two(t):
                copy.wait_recv()

            @pl.loop(0, NY)
            def _(g):
                finish_group(t, g)

            send_home(t)
            fan_got(t, *fan_key).wait_recv()
            fan_got(t, *fan_val).wait_recv()

            @pl.when(t % 2 == 0)
            def _():
                accumulate(t // 2 - 1)

    def head_cols(head):
        return slice(head * HEAD_DIM, (head + 1) * HEAD_DIM)

    def finished(i, g, head):
        s = STEPS // 2 - 1
        return acc[i, g, :, head_cols(head)] + nn(res_t[s, g], kv_weights(i, s)[:, head_cols(head)])

    def last_group(g):
        for copy in group_two(STEPS, g):
            copy.wait_recv()
        finish_group(STEPS, g)

    def y_copy(i, head):
        return remote(
            ys.at[i, head], yr.at[i, head], y_s.at[i, head], y_r.at[i, head], (y_a, y_b)[i % 2]
        )

    def y_send(i, head, value):
        ys[i, head] = value.astype(BF16)
        y_copy(i, head).start()

    def y_read(i, head):
        return yr[i, head].astype(F32)

    def relay(head):
        to_a = finished(1, ya, head)
        y_copy(1, head).wait_recv()
        y_send(4, head, to_a + y_read(1, head))
        to_b = finished(0, yb, head)
        y_copy(0, head).wait_recv()
        y_send(5, head, to_b + y_read(0, head))

    last_group(y2)
    for head in range(2):
        y_send(0, head, finished(0, y2, head))
        y_send(1, head, finished(1, y2, head))
    last_group(ya)
    y_send(2, 0, finished(0, ya, 0))
    last_group(yb)
    y_send(3, 0, finished(1, yb, 0))
    relay(0)
    y_send(2, 1, finished(0, ya, 1))
    y_send(3, 1, finished(1, yb, 1))
    stat_copies = []
    for i, (g, dev) in enumerate(((ya, y_a), (yb, y_b), (y2, y_2))):
        copy = remote(sums.at[g], ss_r.at[i], st_s.at[i], st_r.at[i], dev)
        copy.start()
        stat_copies.append(copy)
    relay(1)
    last_group(y)
    send_home(STEPS)
    for head in range(2):
        for i in range(2):
            acc[i, y, :, head_cols(head)] = finished(i, y, head)

    for h in range(1, STEPS + 1):
        @pl.when(off_diagonal)
        def _():
            out_copy(h, 1).wait_recv()

        p0, p1 = pair(h)
        out_t[block(p0), :] = out_in[h - 1, 0:BLK, :].astype(F32)
        out_t[block(p1), :] = out_in[h - 1, BLK : 2 * BLK, :].astype(F32)
    for i in range(FEAT // 128):
        cols = slice(i * 128, (i + 1) * 128)
        enc_out[:, cols] = jnp.transpose(out_t[cols, :]).astype(BF16)

    lower_half = rows_i < DROWS
    above_end = jnp.minimum(w + 2, NW)
    base = jnp.where(lower_half, start(ordered[1:2], dbound[w]), start(ordered[1:2], dbound[w + 1]))
    last = jnp.where(lower_half, dbound[w + 1].astype(F32), dbound[above_end].astype(F32))
    offset = (rows_i % DROWS).astype(F32)
    dec_col = tags(ends[1:2], base + offset, last)
    dec_allowed = (dec_col == enc_row) & (enc_row >= 0.0)

    for copy in stat_copies:
        copy.wait_recv()
    square = sums[y] + ss_r[0] + ss_r[1] + ss_r[2]
    square_col = jnp.sum(jnp.where(diag, square[0:1], 0.0), axis=1, keepdims=True)
    norm = lax.rsqrt(square_col * (1.0 / (NY * FEAT)) + EPSILON)
    dq_copy.wait_recv()

    def up_copy(head):
        return remote(
            dres.at[head], drecv.at[head], misc_s.at[2 + head], misc_r.at[2 + head], upper
        )

    found = []
    for head in range(2):
        cols = head_cols(head)
        for i in (2, 3, 4, 5):
            y_copy(i, head).wait_recv()
        near_keys = acc[0, y, :, cols] + y_read(2, head) + y_read(5, head)
        near_values = acc[1, y, :, cols] + y_read(3, head) + y_read(4, head)
        both = attend(
            dq2[:, cols], (near_keys * norm).astype(BF16), (near_values * norm).astype(BF16), dec_allowed
        )
        dres[head] = both[DROWS:ROWS]
        up_copy(head).start()
        found.append(both[0:DROWS])

    for copy in [sib_wo, sib_kv, dq_copy] + ctx_sent + stat_copies:
        copy.wait_send()
    for head in range(2):
        for i in range(6):
            y_copy(i, head).wait_send()

    @pl.loop(0, NY)
    def _(g):
        for copy in group_one(1, g) + group_one(STEPS, g) + group_two(STEPS, g):
            copy.wait_send()

    @pl.loop(1, STEPS + 1)
    def _(h):
        hop(h, *ring_wo).wait_send()
        hop(h, *ring_key).wait_send()
        hop(h, *ring_val).wait_send()

        @pl.when((h > 1) & (h < STEPS))
        def _():
            for copy in round_one(h):
                copy.wait_send()

        @pl.when(h < STEPS)
        def _():
            for copy in round_two(h):
                copy.wait_send()
            fan(h, *fan_wo).wait_send()
            fan(h, *fan_key).wait_send()
            fan(h, *fan_val).wait_send()

        @pl.when(off_diagonal)
        def _():
            hid_copy(h).wait_send()

        @pl.when(jnp.logical_not(off_diagonal))
        def _():
            for d in range(1, NY):
                out_copy(h, d).wait_send()

    for head in range(2):
        up_copy(head).wait()
        cross_out[:, head_cols(head)] = found[head] + drecv[head]


def body(
    hidden_in, enc_query, enc_key, enc_value, dec_query, out_proj, key_proj, value_proj,
    norm_gain, enc_len, dec_len, example_order, enc_bounds, dec_bounds,
):
    vmem = pl.BlockSpec(memory_space=pltpu.VMEM)
    anywhere = pl.BlockSpec(memory_space=pl.ANY)
    dma = pltpu.SemaphoreType.DMA
    gain = norm_gain.reshape(32, 128)
    return pl.pallas_call(
        kernel,
        out_shape=(
            jax.ShapeDtypeStruct((ROWS, FEAT), BF16),
            jax.ShapeDtypeStruct((DROWS, WID), BF16),
        ),
        in_specs=[anywhere] * 14,
        out_specs=(vmem, vmem),
        scratch_shapes=[
            pltpu.VMEM((ROWS, WID), BF16),
            pltpu.VMEM((ROWS, WID), BF16),
            pltpu.VMEM((ROWS, WID), BF16),
            pltpu.VMEM(gain.shape, F32),
            pltpu.VMEM((FEAT, 128), F32),
            pltpu.VMEM((3, 1, 256), jnp.int32),
            pltpu.SMEM(enc_bounds.shape, jnp.int32),
            pltpu.SMEM(dec_bounds.shape, jnp.int32),
            pltpu.VMEM((FEAT, WID), BF16),
            pltpu.VMEM((2, FEAT, WID), BF16),
            pltpu.VMEM((2, NY, ROWS, HEAD_DIM), BF16),
            pltpu.VMEM((ROWS, FEAT), BF16),
            pltpu.VMEM((FEAT, ROWS), F32),
            pltpu.VMEM((STEPS, 2 * BLK, ROWS), BF16),
            pltpu.VMEM((STEPS, NY, 2 * BLK, ROWS), BF16),
            pltpu.VMEM((STEPS, NY, 2 * BLK, ROWS), F32),
            pltpu.VMEM((STEPS, NY, 2 * BLK, ROWS), BF16),
            pltpu.VMEM((STEPS, NY, 2 * BLK, ROWS), BF16),
            pltpu.VMEM((STEPS, NY, 2 * BLK, ROWS), BF16),
            pltpu.VMEM((STEPS, NY, 2 * BLK, ROWS), BF16),
            pltpu.VMEM((STEPS // 2, NY, ROWS, 4 * BLK), BF16),
            pltpu.VMEM((2, NY, ROWS, WID), F32),
            pltpu.VMEM((NY, 8, ROWS), F32),
            pltpu.VMEM((FEAT, ROWS), F32),
            pltpu.VMEM((STEPS, NY, 2 * BLK, ROWS), BF16),
            pltpu.VMEM((STEPS, 2 * BLK, ROWS), BF16),
            pltpu.VMEM((6, 2, ROWS, HEAD_DIM), BF16),
            pltpu.VMEM((6, 2, ROWS, HEAD_DIM), BF16),
            pltpu.VMEM((3, 8, ROWS), F32),
            pltpu.VMEM((2 * DROWS, WID), BF16),
            pltpu.VMEM((2, DROWS, HEAD_DIM), BF16),
            pltpu.VMEM((2, DROWS, HEAD_DIM), BF16),
            dma((14,)),
            dma((2,)), dma((2,)),
            dma((STEPS,)), dma((STEPS,)),
            dma((STEPS,)), dma((STEPS,)),
            dma((STEPS,)), dma((STEPS,)),
            dma((STEPS,)), dma((STEPS,)),
            dma((STEPS,)), dma((STEPS,)),
            dma((STEPS,)), dma((STEPS,)),
            dma((4,)), dma((4,)),
            dma((STEPS,)), dma((STEPS, NY - 1)),
            dma((STEPS, NY - 1)), dma((STEPS,)),
            dma((6,)), dma((6,)),
            dma((STEPS, 2)), dma((STEPS, 2)),
            dma((STEPS, 2)), dma((STEPS, 2)),
            dma((3, NY, 2)), dma((3, NY, 2)),
            dma((6, 2)), dma((6, 2)),
            dma((3,)), dma((3,)),
        ],
        compiler_params=pltpu.CompilerParams(
            collective_id=0, has_side_effects=True, vmem_limit_bytes=VMEM_LIMIT
        ),
        name="encoder_to_cross",
    )(
        hidden_in, enc_query, enc_key, enc_value, dec_query, out_proj.T, key_proj, value_proj,
        gain, enc_len.reshape(1, 256), dec_len.reshape(1, 256),
        example_order.reshape(1, 256), enc_bounds, dec_bounds,
    )


def solution(mesh):
    return jax.shard_map(
        body,
        mesh=mesh,
        in_specs=(
            P("wide", "head"), P("wide", "head"), P("wide", "head"), P("wide", "head"),
            P("wide", "head"), P("head", "wide"), P("wide", "head"), P("wide", "head"),
            P(), P(), P(), P(), P(), P(),
        ),
        out_specs=(P("wide", "head"), P("wide", "head")),
        check_vma=False,
    )
```

```python
import jax
import jax.numpy as jnp
from jax import lax
from jax.experimental import pallas as pl
from jax.experimental.pallas import tpu as pltpu
from jax.sharding import PartitionSpec as P

MESH = pl.DeviceIdType.MESH
F32 = jnp.float32
BF16 = jnp.bfloat16

HEAD_DIM = 256
NZ = 16
NY = 4
NX = 4
NW = NY * NZ * 2
ROWS = 128
DROWS = 64
WID = 512
PIECE = 32
BLK = 2 * PIECE
FEAT = NZ * BLK
LANES = FEAT // 128
HOPS = NZ // 2
STEPS = NZ // 4
UNITS = STEPS * NY
GROUP = NY * ROWS
EPSILON = 1e-06
SCALE = 1.0 / 16.0
VMEM_LIMIT = 60 * 1024 * 1024


def nt(a, b):
    return lax.dot_general(a, b, (((1,), (1,)), ((), ())), preferred_element_type=F32)


def nn(a, b):
    return lax.dot_general(a, b, (((1,), (0,)), ((), ())), preferred_element_type=F32)


def iota(shape, dim):
    return lax.broadcasted_iota(jnp.int32, shape, dim)


def attend(q, k, v, allowed):
    scores = jnp.where(allowed, nt(q, k) * SCALE, -1e30)
    weights = jnp.where(allowed, jnp.exp(scores - jnp.max(scores, axis=1, keepdims=True)), 0.0)
    total = jnp.maximum(jnp.sum(weights, axis=1, keepdims=True), 1.0)
    return nn((weights / total).astype(BF16), v).astype(BF16)


def kernel(
    hidden, q_hbm, k_hbm, v_hbm, dq_hbm, wo_hbm, wk_hbm, wv_hbm, gain_hbm,
    elen_hbm, dlen_hbm, order_hbm, ebound_hbm, dbound_hbm,
    enc_out, cross_out,
    q_ref, k_ref, v_ref, gain_ref, gain_c, lens_ref, ebound, dbound,
    wo, kvw, ctx, hid, hid_c, hid_in, part, x1s, x1r, x2s, x2r, res, acc, sums, out_c, out_in, out_w,
    ys, yr, st, str_, dq2, dres, drecv,
    in_sem, first_s, first_r, wo_s, wo_r, wof_s, wof_r, kv_s, kv_r, kvf_s, kvf_r,
    dq_s, dq_r, up_s, up_r, hid_s, hid_r, out_s, out_r, ctx_s, ctx_r, xs1, xr1, xs2, xr2,
    y_s, y_r, st_s, st_r,
):
    w = lax.axis_index("wide")
    x = lax.axis_index("head")
    c = w % 2
    z = (w // 2) % NZ
    y = w // (2 * NZ)
    step_dir = 1 - 2 * c

    def wide(yy, zz, cc):
        return (yy * NZ + zz) * 2 + cc

    sib = (w + step_dir, x)
    z_next = (wide(y, (z + step_dir + NZ) % NZ, c), x)
    z_prev = (wide(y, (z - step_dir + NZ) % NZ, c), x)
    ya, yb, y2 = y + 1 - 2 * (y % 2), NY - 1 - y, (y + 2) % NY
    y_a, y_b, y_2 = (wide(ya, z, c), x), (wide(yb, z, c), x), (wide(y2, z, c), x)
    x_a, x_b = (w, x + 1 - 2 * (x % 2)), (w, NX - 1 - x)
    upper, lower = ((w + 1) % NW, x), ((w + NW - 1) % NW, x)
    adder = (wide(x, z, c), x)
    off_diagonal = x != y
    near = (y_2, y_a, y_b)
    relation = jnp.where(ya == x, 1, jnp.where(yb == x, 2, 0))
    own = NY - 1
    cross = (wide(y, (z - step_dir + NZ) % NZ, 1 - c), x)
    greet = (sib, z_next, z_prev, cross, y_a, y_b, y_2, x_a, x_b, upper, lower)

    def remote(src, dst, ss, rs, dev):
        return pltpu.make_async_remote_copy(
            src_ref=src, dst_ref=dst, send_sem=ss, recv_sem=rs, device_id=dev, device_id_type=MESH
        )

    def cols_of(i, width):
        return pl.ds(pl.multiple_of(i * width, width), width)

    barrier = pltpu.get_barrier_semaphore()
    for dev in greet:
        pl.semaphore_signal(barrier, inc=1, device_id=dev, device_id_type=MESH)

    piece = cols_of(c, PIECE)
    mine = pl.ds(pl.multiple_of(z * BLK + c * PIECE, PIECE), PIECE)
    pairs = (
        (wk_hbm, kvw.at[z, 0, piece]), (wv_hbm, kvw.at[z, 1, piece]),
        (hidden, hid.at[:, pl.ds(0, FEAT)]), (hidden, hid.at[:, pl.ds(FEAT, FEAT)]), (wo_hbm, wo.at[mine]),
        (elen_hbm, lens_ref.at[0]), (dlen_hbm, lens_ref.at[1]), (order_hbm, lens_ref.at[2]),
        (ebound_hbm, ebound), (dbound_hbm, dbound),
        (q_hbm, q_ref), (k_hbm, k_ref), (v_hbm, v_ref),
        (gain_hbm, gain_ref), (dq_hbm, dq2.at[pl.ds(0, DROWS)]),
    )
    loads = [pltpu.make_async_copy(a, b, in_sem.at[i]) for i, (a, b) in enumerate(pairs)]
    for load in loads:
        load.start()

    pl.semaphore_wait(barrier, len(greet))

    around = (z_next, cross, sib)
    wo_first = [
        remote(wo_hbm, wo.at[mine], first_s.at[i], first_r.at[i], dev) for i, dev in enumerate(around)
    ]
    kv_first = [
        remote(kvw.at[z, :, piece], kvw.at[z, :, piece], first_s.at[3 + i], first_r.at[3 + i], dev)
        for i, dev in enumerate(around)
    ]
    for copy in wo_first:
        copy.start()
    for load in loads[:2]:
        load.wait()
    for copy in kv_first:
        copy.start()
    dq_copy = remote(dq_hbm, dq2.at[pl.ds(DROWS, DROWS)], dq_s, dq_r, lower)
    dq_copy.start()

    def turned(ref, by):
        wider = ref[:, pl.ds(pl.multiple_of((by // 2) * 128, 128), FEAT + 128)].astype(F32)
        return jnp.where(by % 2 == 1, wider[:, BLK : BLK + FEAT], wider[:, 0:FEAT])

    def sides(s):
        return slice(s * 128, (s + 1) * 128), slice((LANES - 1 - s) * 128, (LANES - s) * 128)

    def hid_copy(s):
        return remote(hid_c.at[s], hid_in.at[s, relation], hid_s.at[s], hid_r.at[s, relation], adder)

    def hid_got(s, r):
        return remote(hid_in.at[s, r], hid_in.at[s, r], hid_s.at[s], hid_r.at[s, r], adder)

    def out_copy(s, r):
        return remote(out_c.at[s, r], out_in.at[s], out_s.at[s, r], out_r.at[s], near[r])

    for load in loads[2:4]:
        load.wait()
    hid_turned = turned(hid, z)
    for s in range(STEPS):
        for half, cols in enumerate(sides(s)):
            hid_c[s, half] = hid_turned[:, cols].astype(BF16)

    @pl.when(off_diagonal)
    def _():
        hid_copy(0).start()
        hid_in[:, own] = jnp.zeros_like(hid_c)

    @pl.when(jnp.logical_not(off_diagonal))
    def _():
        hid_in[:, own] = hid_c[...]

    for load in loads[4:10]:
        load.wait()

    n = 256
    onehot = jnp.where(lens_ref[2] == iota((n, n), 0), 1.0, 0.0).astype(BF16)
    lens = jnp.concatenate([lens_ref[0], lens_ref[1], jnp.zeros((6, n), jnp.int32)], axis=0)
    ordered = nn(lens.astype(F32).astype(BF16), onehot)
    upto = jnp.where(iota((n, n), 0) <= iota((n, n), 1), 1.0, 0.0).astype(BF16)
    ends = nn(ordered.astype(BF16), upto)
    place = iota((1, n), 1)

    def start(row, first):
        return jnp.sum(jnp.where(place < first, row, 0.0), axis=1, keepdims=True)

    def tags(ends_row, offsets, last):
        pos = jnp.sum(jnp.where(ends_row <= offsets, 1.0, 0.0), axis=1, keepdims=True)
        return jnp.where(pos < last, pos, -1.0)

    rows_i = iota((ROWS, 1), 0)
    enc_base = start(ordered[0:1], ebound[w])
    enc_col = tags(ends[0:1], enc_base + rows_i.astype(F32), ebound[w + 1].astype(F32))
    diag = iota((ROWS, ROWS), 0) == iota((ROWS, ROWS), 1)
    enc_row = jnp.sum(jnp.where(diag, enc_col, 0.0), axis=0, keepdims=True)
    enc_allowed = (enc_col == enc_row) & (enc_row >= 0.0)

    def number(i):
        return (i + 2 * NZ) % NZ

    def wo_block(i):
        return wo.at[cols_of(number(i), BLK)]

    def kv_block(i):
        return kvw.at[number(i)]

    def hop(i, buffer, ss, rs):
        at = buffer(z - step_dir * (i - 1))
        return remote(at, at, ss.at[i - 1], rs.at[i - 1], z_next)

    def got(i, buffer, ss, rs):
        at = buffer(z - step_dir * i)
        return remote(at, at, ss.at[i - 1], rs.at[i - 1], z_next)

    def fan(i, buffer, ss, rs):
        at = buffer(z - step_dir * i)
        return remote(at, at, ss.at[i - 1], rs.at[i - 1], sib)

    def fan_got(i, buffer, ss, rs):
        at = buffer(z + step_dir * i)
        return remote(at, at, ss.at[i - 1], rs.at[i - 1], sib)

    ring_wo, fan_wo = (wo_block, wo_s, wo_r), (wo_block, wof_s, wof_r)
    ring_kv, fan_kv = (kv_block, kv_s, kv_r), (kv_block, kvf_s, kvf_r)

    def forward(i, ring, side):
        hop(i + 1, *ring).start()
        fan(i, *side).start()

    def pass_on(i, ring, side):
        got(i, *ring).wait_recv()

        @pl.when(i < HOPS)
        def _():
            forward(i, ring, side)

    def quad(s):
        return z + 2 * s, z + 2 * s + 1, z - 2 * s - 2, z - 2 * s - 1

    def ctx_copy(head, src, dst, index, dev):
        return remote(ctx.at[head, src], ctx.at[head, dst], ctx_s.at[index], ctx_r.at[index], dev)

    for copy in wo_first[:2]:
        copy.wait_recv()
    forward(1, ring_wo, fan_wo)
    for load in loads[10:]:
        load.wait()
    for head in range(2):
        cols = slice(head * HEAD_DIM, (head + 1) * HEAD_DIM)
        ctx[head, own] = attend(q_ref[:, cols], k_ref[:, cols], v_ref[:, cols], enc_allowed)
    ctx_sent = [
        ctx_copy(0, own, 1, 0, y_a), ctx_copy(1, own, 2, 3, y_b),
        ctx_copy(1, own, 1, 2, y_a), ctx_copy(0, own, 2, 1, y_b),
    ]
    for copy in ctx_sent:
        copy.start()
    for copy in kv_first[:2]:
        copy.wait_recv()
    forward(1, ring_kv, fan_kv)
    pass_on(2, ring_wo, fan_wo)

    ctx_copy(0, 1, 1, 0, y_a).wait_recv()
    ctx_sent.append(ctx_copy(0, 1, 0, 4, y_b))
    ctx_sent[-1].start()
    ctx_copy(1, 2, 2, 3, y_b).wait_recv()
    ctx_sent.append(ctx_copy(1, 2, 0, 5, y_a))
    ctx_sent[-1].start()

    @pl.when(off_diagonal)
    def _():
        hid_copy(1).start()
        hid_in[:, 0:own] = jnp.zeros((STEPS, own, 2, ROWS, 128), BF16)

    for i in range(2 * LANES):
        row = gain_ref[pl.ds(y * LANES + i % LANES, 1), :]
        out_w[0:8, i * 128 : (i + 1) * 128] = jnp.broadcast_to(row, (8, 128))
    gain_turned = turned(out_w.at[pl.ds(0, 8)], z)
    for s in range(STEPS):
        for half, cols in enumerate(sides(s)):
            gain_c[s, half] = gain_turned[:, cols]
    sums[...] = jnp.zeros_like(sums)

    def round_one(s, first, count, index):
        return [
            remote(
                x1s.at[s, i, pl.ds(first, count)], x1r.at[s, i, pl.ds(first, count)],
                xs1.at[index, i], xr1.at[index, i], (x_a, x_b)[i],
            )
            for i in range(2)
        ]

    def round_two(s, first, count, index):
        return [
            remote(
                x2s.at[s, i, pl.ds(first, count)], x2r.at[s, i, pl.ds(first, count)],
                xs2.at[index, i], xr2.at[index, i], (x_b, x_a)[i],
            )
            for i in range(2)
        ]

    x_sent = []

    def project(s, first, count, index):
        @pl.when(jnp.logical_not(off_diagonal))
        def _():
            for r in range(first, min(first + count, own)):
                hid_got(s, r).wait_recv()

        groups = slice(first, first + count)
        weights = jnp.concatenate([wo_block(i)[...] for i in quad(s)], axis=0)
        rows = [ctx[head, groups].reshape(count * ROWS, HEAD_DIM) for head in range(2)]
        term = nt(rows[0], weights[:, 0:HEAD_DIM]) + nt(rows[1], weights[:, HEAD_DIM:WID])
        for half in range(2):
            value = term[:, half * 128 : (half + 1) * 128].reshape(count, ROWS, 128)
            value = value + hid_in[s, groups, half].astype(F32)
            part[s, half, groups] = value
            x1s[s, half, groups] = value.astype(BF16)
        for copy in round_one(s, first, count, index):
            copy.start()
            x_sent.append(copy)

    def exchange(s, first, count, index):
        groups = slice(first, first + count)
        for half, copy in enumerate(round_one(s, first, count, index)):
            copy.wait_recv()
            total = part[s, half, groups] + x1r[s, half, groups].astype(F32)
            part[s, half, groups] = total
            x2s[s, half, groups] = total.astype(BF16)
            copy = round_two(s, first, count, index)[half]
            copy.start()
            x_sent.append(copy)

    def finish(s, first, count, index):
        groups = slice(first, first + count)
        for half, copy in enumerate(round_two(s, first, count, index)):
            copy.wait_recv()
            total = part[s, half, groups] + x2r[s, half, groups].astype(F32)
            sums[groups] += total * total
            res[s, groups, :, half * 128 : (half + 1) * 128] = (total * gain_c[s, half, 0:1, :]).astype(BF16)
            out_c[s, groups, half] = total.astype(BF16)

        @pl.when(jnp.logical_not(off_diagonal))
        def _():
            for r in range(first, min(first + count, own)):
                out_copy(s, r).start()
            if first + count > own:
                out_in[s] = out_c[s, own]

    def kv_weights(s, kind):
        return jnp.concatenate([kvw[number(i), kind] for i in quad(s)], axis=0)

    def accumulate(s, first, count):
        groups = slice(first, first + count)
        rows = res[s, groups].reshape(count * ROWS, 4 * BLK)
        for kind in range(2):
            term = nn(rows, kv_weights(s, kind)).reshape(count, ROWS, WID)
            acc[kind, groups] = term if s == 0 else acc[kind, groups] + term

    def fans(s, side):
        for i in (2 * s + 1, 2 * s + 2):
            if i < HOPS:
                fan_got(i, *side).wait_recv()

    def send_hidden(s):
        @pl.when(off_diagonal)
        def _():
            hid_copy(s).start()

    all_rows, early, late, end = (0, NY), (0, 2), (2, 2), STEPS - 1
    for copy in wo_first[2:]:
        copy.wait_recv()
    pass_on(3, ring_wo, fan_wo)
    fans(0, fan_wo)
    ctx_copy(0, 2, 2, 1, y_b).wait_recv()
    project(0, *late, 0)
    pass_on(2, ring_kv, fan_kv)
    pass_on(4, ring_wo, fan_wo)
    ctx_copy(1, 1, 1, 2, y_a).wait_recv()
    ctx_copy(0, 0, 0, 4, y_b).wait_recv()
    ctx_copy(1, 0, 0, 5, y_a).wait_recv()
    project(0, *early, 1)
    send_hidden(2)
    fans(1, fan_wo)
    project(1, *all_rows, 2)
    pass_on(5, ring_wo, fan_wo)
    pass_on(3, ring_kv, fan_kv)
    exchange(0, *late, 0)
    exchange(0, *early, 1)
    send_hidden(3)
    pass_on(6, ring_wo, fan_wo)
    pass_on(4, ring_kv, fan_kv)
    fans(2, fan_wo)
    project(2, *all_rows, 3)
    pass_on(7, ring_wo, fan_wo)
    exchange(1, *all_rows, 2)
    pass_on(5, ring_kv, fan_kv)
    finish(0, *late, 0)
    finish(0, *early, 1)
    pass_on(8, ring_wo, fan_wo)
    fans(3, fan_wo)
    project(3, *early, 4)
    project(3, *late, 5)
    pass_on(6, ring_kv, fan_kv)
    for copy in kv_first[2:]:
        copy.wait_recv()
    fans(0, fan_kv)
    accumulate(0, *all_rows)
    exchange(2, *all_rows, 3)
    pass_on(7, ring_kv, fan_kv)
    finish(1, *all_rows, 2)
    fans(1, fan_kv)
    accumulate(1, *all_rows)
    exchange(3, *early, 4)
    exchange(3, *late, 5)
    pass_on(8, ring_kv, fan_kv)
    finish(2, *all_rows, 3)
    fans(2, fan_kv)
    accumulate(2, *all_rows)
    fans(3, fan_kv)

    y_copies = [remote(ys.at[i], yr.at[i], y_s.at[i], y_r.at[i], (y_a, y_b)[i % 2]) for i in range(6)]

    def y_send(i, value):
        ys[i] = value.astype(BF16)
        y_copies[i].start()

    def y_read(i):
        return yr[i].astype(F32)

    finish(end, *early, 4)
    accumulate(end, *early)
    y_send(0, acc[0, 0])
    y_send(1, acc[1, 0])
    y_send(2, acc[0, 1])
    finish(end, *late, 5)
    accumulate(end, *late)
    y_send(3, acc[1, 2])
    y_copies[1].wait_recv()
    y_send(4, acc[1, 1] + y_read(1))
    y_copies[0].wait_recv()
    y_send(5, acc[0, 2] + y_read(0))

    columns = jnp.sum(sums[...], axis=2, keepdims=True)
    squares = jnp.sum(jnp.where(diag[None], columns, 0.0), axis=1, keepdims=True)
    st[...] = jnp.broadcast_to(squares, (NY, 8, ROWS))
    stat_copies = [remote(st.at[r], str_.at[r], st_s.at[r], st_r.at[r], near[r]) for r in range(own)]
    for copy in stat_copies:
        copy.start()

    @pl.when(off_diagonal)
    def _():
        for s in range(STEPS):
            out_copy(s, 0).wait_recv()

    for s in range(STEPS):
        for half, cols in enumerate(sides(s)):
            for copy in range(2):
                at = slice(cols.start + copy * FEAT, cols.stop + copy * FEAT)
                out_w[:, at] = out_in[s, half].astype(F32)
    enc_out[...] = turned(out_w, (NZ - z) % NZ).astype(BF16)

    lower_half = rows_i < DROWS
    above_end = jnp.minimum(w + 2, NW)
    base = jnp.where(lower_half, start(ordered[1:2], dbound[w]), start(ordered[1:2], dbound[w + 1]))
    last = jnp.where(lower_half, dbound[w + 1].astype(F32), dbound[above_end].astype(F32))
    offset = (rows_i % DROWS).astype(F32)
    dec_col = tags(ends[1:2], base + offset, last)
    dec_allowed = (dec_col == enc_row) & (enc_row >= 0.0)

    for copy in stat_copies:
        copy.wait_recv()
    square = st[own] + str_[0] + str_[1] + str_[2]
    square_col = jnp.sum(jnp.where(diag, square[0:1], 0.0), axis=1, keepdims=True)
    norm = lax.rsqrt(square_col * (1.0 / (NY * FEAT)) + EPSILON)
    dq_copy.wait_recv()

    for i in (2, 3, 4, 5):
        y_copies[i].wait_recv()
    near_keys = ((acc[0, own] + y_read(2) + y_read(5)) * norm).astype(BF16)
    near_values = ((acc[1, own] + y_read(3) + y_read(4)) * norm).astype(BF16)

    def cross(rows, head):
        cols = slice(head * HEAD_DIM, (head + 1) * HEAD_DIM)
        return attend(dq2[rows, cols], near_keys[:, cols], near_values[:, cols], dec_allowed[rows])

    dres[...] = jnp.concatenate([cross(slice(DROWS, ROWS), head) for head in range(2)], axis=1)
    up = remote(dres, drecv, up_s, up_r, upper)
    up.start()
    cross_out[...] = jnp.concatenate([cross(slice(0, DROWS), head) for head in range(2)], axis=1)

    for copy in wo_first + kv_first + [dq_copy] + ctx_sent + x_sent + y_copies + stat_copies:
        copy.wait_send()

    @pl.loop(1, HOPS)
    def _(i):
        hop(i + 1, *ring_wo).wait_send()
        hop(i + 1, *ring_kv).wait_send()
        fan(i, *fan_wo).wait_send()
        fan(i, *fan_kv).wait_send()

    @pl.when(off_diagonal)
    def _():
        for s in range(STEPS):
            hid_copy(s).wait_send()

    @pl.when(jnp.logical_not(off_diagonal))
    def _():
        for s in range(STEPS):
            for r in range(own):
                out_copy(s, r).wait_send()

    up.wait()
    cross_out[...] = cross_out[...] + drecv[...]


def body(
    hidden_in, enc_query, enc_key, enc_value, dec_query, out_proj, key_proj, value_proj,
    norm_gain, enc_len, dec_len, example_order, enc_bounds, dec_bounds,
):
    vmem = pl.BlockSpec(memory_space=pltpu.VMEM)
    anywhere = pl.BlockSpec(memory_space=pl.ANY)
    dma = pltpu.SemaphoreType.DMA
    gain = norm_gain.reshape(32, 128)
    square = (ROWS, 128)
    return pl.pallas_call(
        kernel,
        out_shape=(
            jax.ShapeDtypeStruct((ROWS, FEAT), BF16),
            jax.ShapeDtypeStruct((DROWS, WID), BF16),
        ),
        in_specs=[anywhere] * 14,
        out_specs=(vmem, vmem),
        scratch_shapes=[
            pltpu.VMEM((ROWS, WID), BF16),
            pltpu.VMEM((ROWS, WID), BF16),
            pltpu.VMEM((ROWS, WID), BF16),
            pltpu.VMEM(gain.shape, F32),
            pltpu.VMEM((STEPS, 2, 8, 128), F32),
            pltpu.VMEM((3, 1, 256), jnp.int32),
            pltpu.SMEM(enc_bounds.shape, jnp.int32),
            pltpu.SMEM(dec_bounds.shape, jnp.int32),
            pltpu.VMEM((FEAT, WID), BF16),
            pltpu.VMEM((NZ, 2, BLK, WID), BF16),
            pltpu.VMEM((2, NY, ROWS, HEAD_DIM), BF16),
            pltpu.VMEM((ROWS, 2 * FEAT), BF16),
            pltpu.VMEM((STEPS, 2) + square, BF16),
            pltpu.VMEM((STEPS, NY, 2) + square, BF16),
            pltpu.VMEM((STEPS, 2, NY) + square, F32),
            pltpu.VMEM((STEPS, 2, NY) + square, BF16),
            pltpu.VMEM((STEPS, 2, NY) + square, BF16),
            pltpu.VMEM((STEPS, 2, NY) + square, BF16),
            pltpu.VMEM((STEPS, 2, NY) + square, BF16),
            pltpu.VMEM((STEPS, NY, ROWS, 4 * BLK), BF16),
            pltpu.VMEM((2, NY, ROWS, WID), F32),
            pltpu.VMEM((NY,) + square, F32),
            pltpu.VMEM((STEPS, NY, 2) + square, BF16),
            pltpu.VMEM((STEPS, 2) + square, BF16),
            pltpu.VMEM((ROWS, 2 * FEAT), F32),
            pltpu.VMEM((6, ROWS, WID), BF16),
            pltpu.VMEM((6, ROWS, WID), BF16),
            pltpu.VMEM((NY, 8, ROWS), F32),
            pltpu.VMEM((NY - 1, 8, ROWS), F32),
            pltpu.VMEM((2 * DROWS, WID), BF16),
            pltpu.VMEM((DROWS, WID), BF16),
            pltpu.VMEM((DROWS, WID), BF16),
            dma((15,)),
            dma((6,)), dma((6,)),
            dma((HOPS,)), dma((HOPS,)),
            dma((HOPS,)), dma((HOPS,)),
            dma((HOPS,)), dma((HOPS,)),
            dma((HOPS,)), dma((HOPS,)),
            dma, dma,
            dma, dma,
            dma((STEPS,)), dma((STEPS, NY - 1)),
            dma((STEPS, NY - 1)), dma((STEPS,)),
            dma((6,)), dma((6,)),
            dma((STEPS + 2, 2)), dma((STEPS + 2, 2)),
            dma((STEPS + 2, 2)), dma((STEPS + 2, 2)),
            dma((6,)), dma((6,)),
            dma((NY - 1,)), dma((NY - 1,)),
        ],
        compiler_params=pltpu.CompilerParams(
            collective_id=0, has_side_effects=True, vmem_limit_bytes=VMEM_LIMIT
        ),
        name="encoder_to_cross",
    )(
        hidden_in, enc_query, enc_key, enc_value, dec_query, out_proj.T, key_proj, value_proj,
        gain, enc_len.reshape(1, 256), dec_len.reshape(1, 256),
        example_order.reshape(1, 256), enc_bounds, dec_bounds,
    )


def solution(mesh):
    return jax.shard_map(
        body,
        mesh=mesh,
        in_specs=(
            P("wide", "head"), P("wide", "head"), P("wide", "head"), P("wide", "head"),
            P("wide", "head"), P("head", "wide"), P("wide", "head"), P("wide", "head"),
            P(), P(), P(), P(), P(), P(),
        ),
        out_specs=(P("wide", "head"), P("wide", "head")),
        check_vma=False,
    )
```

```python
import jax
import jax.numpy as jnp
from jax import lax
from jax.experimental import pallas as pl
from jax.experimental.pallas import tpu as pltpu
from jax.sharding import PartitionSpec as P

MESH = pl.DeviceIdType.MESH
F32 = jnp.float32
BF16 = jnp.bfloat16

HEAD_DIM = 256
NZ = 16
NY = 4
NX = 4
NW = NY * NZ * 2
ROWS = 128
DROWS = 64
WID = 512
PIECE = 32
BLK = 2 * PIECE
FEAT = NZ * BLK
LANES = FEAT // 128
HOPS = NZ // 2
STEPS = NZ // 4
UNITS = STEPS * NY
GROUP = NY * ROWS
EPSILON = 1e-06
SCALE = 1.0 / 16.0
VMEM_LIMIT = 60 * 1024 * 1024


def nt(a, b):
    return lax.dot_general(a, b, (((1,), (1,)), ((), ())), preferred_element_type=F32)


def nn(a, b):
    return lax.dot_general(a, b, (((1,), (0,)), ((), ())), preferred_element_type=F32)


def iota(shape, dim):
    return lax.broadcasted_iota(jnp.int32, shape, dim)


def attend(q, k, v, allowed):
    scores = jnp.where(allowed, nt(q, k) * SCALE, -1e30)
    weights = jnp.where(allowed, jnp.exp(scores - jnp.max(scores, axis=1, keepdims=True)), 0.0)
    total = jnp.maximum(jnp.sum(weights, axis=1, keepdims=True), 1.0)
    return nn((weights / total).astype(BF16), v).astype(BF16)


def kernel(
    hidden, q_hbm, k_hbm, v_hbm, dq_hbm, wo_hbm, wk_hbm, wv_hbm, gain_hbm,
    elen_hbm, dlen_hbm, order_hbm, ebound_hbm, dbound_hbm,
    enc_out, cross_out,
    q_ref, k_ref, v_ref, gain_ref, gain_c, lens_ref, ebound, dbound,
    wo, kvw, ctx, hid, hid_c, hid_in, part, x1s, x1r, x2s, x2r, res, acc, sums, out_c, out_in, out_w,
    ys, yr, st, str_, dq2, dres, drecv,
    in_sem, first_s, first_r, wo_s, wo_r, wof_s, wof_r, kv_s, kv_r, kvf_s, kvf_r,
    dq_s, dq_r, up_s, up_r, hid_s, hid_r, out_s, out_r, ctx_s, ctx_r, xs1, xr1, xs2, xr2,
    y_s, y_r, st_s, st_r,
):
    w = lax.axis_index("wide")
    x = lax.axis_index("head")
    c = w % 2
    z = (w // 2) % NZ
    y = w // (2 * NZ)
    step_dir = 1 - 2 * c

    def wide(yy, zz, cc):
        return (yy * NZ + zz) * 2 + cc

    sib = (w + step_dir, x)
    z_next = (wide(y, (z + step_dir + NZ) % NZ, c), x)
    z_prev = (wide(y, (z - step_dir + NZ) % NZ, c), x)
    ya, yb, y2 = y + 1 - 2 * (y % 2), NY - 1 - y, (y + 2) % NY
    y_a, y_b, y_2 = (wide(ya, z, c), x), (wide(yb, z, c), x), (wide(y2, z, c), x)
    x_a, x_b = (w, x + 1 - 2 * (x % 2)), (w, NX - 1 - x)
    upper, lower = ((w + 1) % NW, x), ((w + NW - 1) % NW, x)
    adder = (wide(x, z, c), x)
    off_diagonal = x != y
    near = (y_2, y_a, y_b)
    relation = jnp.where(ya == x, 1, jnp.where(yb == x, 2, 0))
    own = NY - 1
    cross = (wide(y, (z - step_dir + NZ) % NZ, 1 - c), x)
    greet = (sib, z_next, z_prev, cross, y_a, y_b, y_2, x_a, x_b, upper, lower)

    def remote(src, dst, ss, rs, dev):
        return pltpu.make_async_remote_copy(
            src_ref=src, dst_ref=dst, send_sem=ss, recv_sem=rs, device_id=dev, device_id_type=MESH
        )

    def cols_of(i, width):
        return pl.ds(pl.multiple_of(i * width, width), width)

    barrier = pltpu.get_barrier_semaphore()
    for dev in greet:
        pl.semaphore_signal(barrier, inc=1, device_id=dev, device_id_type=MESH)

    piece = cols_of(c, PIECE)
    mine = pl.ds(pl.multiple_of(z * BLK + c * PIECE, PIECE), PIECE)
    pairs = (
        (wk_hbm, kvw.at[z, 0, piece]), (wv_hbm, kvw.at[z, 1, piece]),
        (hidden, hid.at[:, pl.ds(0, FEAT)]), (hidden, hid.at[:, pl.ds(FEAT, FEAT)]), (wo_hbm, wo.at[mine]),
        (elen_hbm, lens_ref.at[0]), (dlen_hbm, lens_ref.at[1]), (order_hbm, lens_ref.at[2]),
        (ebound_hbm, ebound), (dbound_hbm, dbound),
        (q_hbm, q_ref), (k_hbm, k_ref), (v_hbm, v_ref),
        (gain_hbm, gain_ref), (dq_hbm, dq2.at[pl.ds(0, DROWS)]),
    )
    loads = [pltpu.make_async_copy(a, b, in_sem.at[i]) for i, (a, b) in enumerate(pairs)]
    for load in loads:
        load.start()

    pl.semaphore_wait(barrier, len(greet))

    around = (z_next, cross, sib)
    wo_first = [
        remote(wo_hbm, wo.at[mine], first_s.at[i], first_r.at[i], dev) for i, dev in enumerate(around)
    ]
    kv_first = [
        remote(kvw.at[z, :, piece], kvw.at[z, :, piece], first_s.at[3 + i], first_r.at[3 + i], dev)
        for i, dev in enumerate(around)
    ]
    for copy in wo_first:
        copy.start()
    for load in loads[:2]:
        load.wait()
    for copy in kv_first:
        copy.start()
    dq_copy = remote(dq_hbm, dq2.at[pl.ds(DROWS, DROWS)], dq_s, dq_r, lower)
    dq_copy.start()

    def turned(ref, by):
        wider = ref[:, pl.ds(pl.multiple_of((by // 2) * 128, 128), FEAT + 128)].astype(F32)
        return jnp.where(by % 2 == 1, wider[:, BLK : BLK + FEAT], wider[:, 0:FEAT])

    def sides(s):
        return slice(s * 128, (s + 1) * 128), slice((LANES - 1 - s) * 128, (LANES - s) * 128)

    def hid_copy(s):
        return remote(hid_c.at[s], hid_in.at[s, relation], hid_s.at[s], hid_r.at[s, relation], adder)

    def hid_got(s, r):
        return remote(hid_in.at[s, r], hid_in.at[s, r], hid_s.at[s], hid_r.at[s, r], adder)

    def out_copy(s, r):
        return remote(out_c.at[s, r], out_in.at[s], out_s.at[s, r], out_r.at[s], near[r])

    for load in loads[2:4]:
        load.wait()
    hid_turned = turned(hid, z)
    for s in range(STEPS):
        for half, cols in enumerate(sides(s)):
            hid_c[s, half] = hid_turned[:, cols].astype(BF16)

    @pl.when(off_diagonal)
    def _():
        hid_copy(0).start()
        hid_in[:, own] = jnp.zeros_like(hid_c)

    @pl.when(jnp.logical_not(off_diagonal))
    def _():
        hid_in[:, own] = hid_c[...]

    for load in loads[4:10]:
        load.wait()

    n = 256
    onehot = jnp.where(lens_ref[2] == iota((n, n), 0), 1.0, 0.0).astype(BF16)
    lens = jnp.concatenate([lens_ref[0], lens_ref[1], jnp.zeros((6, n), jnp.int32)], axis=0)
    ordered = nn(lens.astype(F32).astype(BF16), onehot)
    upto = jnp.where(iota((n, n), 0) <= iota((n, n), 1), 1.0, 0.0).astype(BF16)
    ends = nn(ordered.astype(BF16), upto)
    place = iota((1, n), 1)

    def start(row, first):
        return jnp.sum(jnp.where(place < first, row, 0.0), axis=1, keepdims=True)

    def tags(ends_row, offsets, last):
        pos = jnp.sum(jnp.where(ends_row <= offsets, 1.0, 0.0), axis=1, keepdims=True)
        return jnp.where(pos < last, pos, -1.0)

    rows_i = iota((ROWS, 1), 0)
    enc_base = start(ordered[0:1], ebound[w])
    enc_col = tags(ends[0:1], enc_base + rows_i.astype(F32), ebound[w + 1].astype(F32))
    diag = iota((ROWS, ROWS), 0) == iota((ROWS, ROWS), 1)
    enc_row = jnp.sum(jnp.where(diag, enc_col, 0.0), axis=0, keepdims=True)
    enc_allowed = (enc_col == enc_row) & (enc_row >= 0.0)

    def number(i):
        return (i + 2 * NZ) % NZ

    def wo_block(i):
        return wo.at[cols_of(number(i), BLK)]

    def kv_block(i):
        return kvw.at[number(i)]

    def hop(i, buffer, ss, rs):
        at = buffer(z - step_dir * (i - 1))
        return remote(at, at, ss.at[i - 1], rs.at[i - 1], z_next)

    def got(i, buffer, ss, rs):
        at = buffer(z - step_dir * i)
        return remote(at, at, ss.at[i - 1], rs.at[i - 1], z_next)

    def fan(i, buffer, ss, rs):
        at = buffer(z - step_dir * i)
        return remote(at, at, ss.at[i - 1], rs.at[i - 1], sib)

    def fan_got(i, buffer, ss, rs):
        at = buffer(z + step_dir * i)
        return remote(at, at, ss.at[i - 1], rs.at[i - 1], sib)

    ring_wo, fan_wo = (wo_block, wo_s, wo_r), (wo_block, wof_s, wof_r)
    ring_kv, fan_kv = (kv_block, kv_s, kv_r), (kv_block, kvf_s, kvf_r)

    def forward(i, ring, side):
        hop(i + 1, *ring).start()
        fan(i, *side).start()

    def pass_on(i, ring, side):
        got(i, *ring).wait_recv()

        @pl.when(i < HOPS)
        def _():
            forward(i, ring, side)

    def quad(s):
        return z + 2 * s, z + 2 * s + 1, z - 2 * s - 2, z - 2 * s - 1

    def round_one(s, first, count, index):
        return [
            remote(
                x1s.at[s, i, pl.ds(first, count)], x1r.at[s, i, pl.ds(first, count)],
                xs1.at[index, i], xr1.at[index, i], (x_a, x_b)[i],
            )
            for i in range(2)
        ]

    def round_two(s, first, count, index):
        return [
            remote(
                x2s.at[s, i, pl.ds(first, count)], x2r.at[s, i, pl.ds(first, count)],
                xs2.at[index, i], xr2.at[index, i], (x_b, x_a)[i],
            )
            for i in range(2)
        ]

    x_sent = []

    def project(s, first, count, index):
        @pl.when(jnp.logical_not(off_diagonal))
        def _():
            for r in range(first, min(first + count, own)):
                hid_got(s, r).wait_recv()

        groups = slice(first, first + count)
        weights = jnp.concatenate([wo_block(i)[...] for i in quad(s)], axis=0)
        rows = [ctx[head, groups].reshape(count * ROWS, HEAD_DIM) for head in range(2)]
        term = nt(rows[0], weights[:, 0:HEAD_DIM]) + nt(rows[1], weights[:, HEAD_DIM:WID])
        for half in range(2):
            value = term[:, half * 128 : (half + 1) * 128].reshape(count, ROWS, 128)
            value = value + hid_in[s, groups, half].astype(F32)
            part[s, half, groups] = value
            x1s[s, half, groups] = value.astype(BF16)
        for copy in round_one(s, first, count, index):
            copy.start()
            x_sent.append(copy)

    def fans(s, side):
        for i in (2 * s + 1, 2 * s + 2):
            if i < HOPS:
                fan_got(i, *side).wait_recv()

    def ctx_copy(head, src, dst, index, dev):
        return remote(ctx.at[head, src], ctx.at[head, dst], ctx_s.at[index], ctx_r.at[index], dev)

    for copy in wo_first[:2]:
        copy.wait_recv()
    forward(1, ring_wo, fan_wo)
    for load in loads[10:]:
        load.wait()
    for head in range(2):
        cols = slice(head * HEAD_DIM, (head + 1) * HEAD_DIM)
        ctx[head, own] = attend(q_ref[:, cols], k_ref[:, cols], v_ref[:, cols], enc_allowed)
    ctx_sent = [
        ctx_copy(0, own, 1, 0, y_a), ctx_copy(1, own, 2, 3, y_b),
        ctx_copy(1, own, 1, 2, y_a), ctx_copy(0, own, 2, 1, y_b),
    ]
    for copy in ctx_sent:
        copy.start()
    for copy in kv_first[:2]:
        copy.wait_recv()
    forward(1, ring_kv, fan_kv)
    pass_on(2, ring_wo, fan_wo)

    for copy in wo_first[2:]:
        copy.wait_recv()
    fans(0, fan_wo)
    project(0, 3, 1, 0)

    ctx_copy(0, 1, 1, 0, y_a).wait_recv()
    ctx_sent.append(ctx_copy(0, 1, 0, 4, y_b))
    ctx_sent[-1].start()
    ctx_copy(1, 2, 2, 3, y_b).wait_recv()
    ctx_sent.append(ctx_copy(1, 2, 0, 5, y_a))
    ctx_sent[-1].start()

    @pl.when(off_diagonal)
    def _():
        hid_copy(1).start()
        hid_in[:, 0:own] = jnp.zeros((STEPS, own, 2, ROWS, 128), BF16)

    for i in range(2 * LANES):
        row = gain_ref[pl.ds(y * LANES + i % LANES, 1), :]
        out_w[0:8, i * 128 : (i + 1) * 128] = jnp.broadcast_to(row, (8, 128))
    gain_turned = turned(out_w.at[pl.ds(0, 8)], z)
    for s in range(STEPS):
        for half, cols in enumerate(sides(s)):
            gain_c[s, half] = gain_turned[:, cols]
    sums[...] = jnp.zeros_like(sums)

    def exchange(s, first, count, index):
        groups = slice(first, first + count)
        for half, copy in enumerate(round_one(s, first, count, index)):
            copy.wait_recv()
            total = part[s, half, groups] + x1r[s, half, groups].astype(F32)
            part[s, half, groups] = total
            x2s[s, half, groups] = total.astype(BF16)
            copy = round_two(s, first, count, index)[half]
            copy.start()
            x_sent.append(copy)

    def finish(s, first, count, index):
        groups = slice(first, first + count)
        for half, copy in enumerate(round_two(s, first, count, index)):
            copy.wait_recv()
            total = part[s, half, groups] + x2r[s, half, groups].astype(F32)
            sums[groups] += total * total
            res[s, groups, :, half * 128 : (half + 1) * 128] = (total * gain_c[s, half, 0:1, :]).astype(BF16)
            out_c[s, groups, half] = total.astype(BF16)

        @pl.when(jnp.logical_not(off_diagonal))
        def _():
            for r in range(first, min(first + count, own)):
                out_copy(s, r).start()
            if first + count > own:
                out_in[s] = out_c[s, own]

    def kv_weights(s, kind):
        return jnp.concatenate([kvw[number(i), kind] for i in quad(s)], axis=0)

    def accumulate(s, first, count):
        groups = slice(first, first + count)
        rows = res[s, groups].reshape(count * ROWS, 4 * BLK)
        for kind in range(2):
            term = nn(rows, kv_weights(s, kind)).reshape(count, ROWS, WID)
            acc[kind, groups] = term if s == 0 else acc[kind, groups] + term

    def send_hidden(s):
        @pl.when(off_diagonal)
        def _():
            hid_copy(s).start()

    all_rows, early, late, end = (0, NY), (0, 2), (2, 2), STEPS - 1
    pass_on(3, ring_wo, fan_wo)
    pass_on(2, ring_kv, fan_kv)
    ctx_copy(1, 1, 1, 2, y_a).wait_recv()
    project(0, 1, 1, 7)
    ctx_copy(0, 2, 2, 1, y_b).wait_recv()
    project(0, 2, 1, 1)
    pass_on(4, ring_wo, fan_wo)
    ctx_copy(0, 0, 0, 4, y_b).wait_recv()
    ctx_copy(1, 0, 0, 5, y_a).wait_recv()
    project(0, 0, 1, 6)
    send_hidden(2)
    fans(1, fan_wo)
    project(1, *all_rows, 2)
    pass_on(5, ring_wo, fan_wo)
    pass_on(3, ring_kv, fan_kv)
    for first, index in ((3, 0), (1, 7), (2, 1), (0, 6)):
        exchange(0, first, 1, index)
    send_hidden(3)
    pass_on(6, ring_wo, fan_wo)
    pass_on(4, ring_kv, fan_kv)
    fans(2, fan_wo)
    project(2, *all_rows, 3)
    pass_on(7, ring_wo, fan_wo)
    exchange(1, *all_rows, 2)
    pass_on(5, ring_kv, fan_kv)
    for first, index in ((3, 0), (1, 7), (2, 1), (0, 6)):
        finish(0, first, 1, index)
    pass_on(8, ring_wo, fan_wo)
    fans(3, fan_wo)
    project(3, *early, 4)
    project(3, *late, 5)
    pass_on(6, ring_kv, fan_kv)
    for copy in kv_first[2:]:
        copy.wait_recv()
    fans(0, fan_kv)
    accumulate(0, *all_rows)
    exchange(2, *all_rows, 3)
    pass_on(7, ring_kv, fan_kv)
    finish(1, *all_rows, 2)
    fans(1, fan_kv)
    accumulate(1, *all_rows)
    exchange(3, *early, 4)
    exchange(3, *late, 5)
    pass_on(8, ring_kv, fan_kv)
    finish(2, *all_rows, 3)
    fans(2, fan_kv)
    accumulate(2, *all_rows)
    fans(3, fan_kv)

    y_copies = [remote(ys.at[i], yr.at[i], y_s.at[i], y_r.at[i], (y_a, y_b)[i % 2]) for i in range(6)]

    def y_send(i, value):
        ys[i] = value.astype(BF16)
        y_copies[i].start()

    def y_read(i):
        return yr[i].astype(F32)

    finish(end, *early, 4)
    accumulate(end, *early)
    y_send(0, acc[0, 0])
    y_send(1, acc[1, 0])
    y_send(2, acc[0, 1])
    finish(end, *late, 5)
    accumulate(end, *late)
    y_send(3, acc[1, 2])
    y_copies[1].wait_recv()
    y_send(4, acc[1, 1] + y_read(1))
    y_copies[0].wait_recv()
    y_send(5, acc[0, 2] + y_read(0))

    columns = jnp.sum(sums[...], axis=2, keepdims=True)
    squares = jnp.sum(jnp.where(diag[None], columns, 0.0), axis=1, keepdims=True)
    st[...] = jnp.broadcast_to(squares, (NY, 8, ROWS))
    stat_copies = [remote(st.at[r], str_.at[r], st_s.at[r], st_r.at[r], near[r]) for r in range(own)]
    for copy in stat_copies:
        copy.start()

    @pl.when(off_diagonal)
    def _():
        for s in range(STEPS):
            out_copy(s, 0).wait_recv()

    for s in range(STEPS):
        for half, cols in enumerate(sides(s)):
            for copy in range(2):
                at = slice(cols.start + copy * FEAT, cols.stop + copy * FEAT)
                out_w[:, at] = out_in[s, half].astype(F32)
    enc_out[...] = turned(out_w, (NZ - z) % NZ).astype(BF16)

    lower_half = rows_i < DROWS
    above_end = jnp.minimum(w + 2, NW)
    base = jnp.where(lower_half, start(ordered[1:2], dbound[w]), start(ordered[1:2], dbound[w + 1]))
    last = jnp.where(lower_half, dbound[w + 1].astype(F32), dbound[above_end].astype(F32))
    offset = (rows_i % DROWS).astype(F32)
    dec_col = tags(ends[1:2], base + offset, last)
    dec_allowed = (dec_col == enc_row) & (enc_row >= 0.0)

    for copy in wo_first + kv_first + [dq_copy] + ctx_sent + x_sent:
        copy.wait_send()

    @pl.loop(1, HOPS)
    def _(i):
        hop(i + 1, *ring_wo).wait_send()
        hop(i + 1, *ring_kv).wait_send()
        fan(i, *fan_wo).wait_send()
        fan(i, *fan_kv).wait_send()

    @pl.when(off_diagonal)
    def _():
        for s in range(STEPS):
            hid_copy(s).wait_send()

    @pl.when(jnp.logical_not(off_diagonal))
    def _():
        for s in range(STEPS):
            for r in range(own):
                out_copy(s, r).wait_send()

    for copy in stat_copies:
        copy.wait_recv()
    square = st[own] + str_[0] + str_[1] + str_[2]
    square_col = jnp.sum(jnp.where(diag, square[0:1], 0.0), axis=1, keepdims=True)
    norm = lax.rsqrt(square_col * (1.0 / (NY * FEAT)) + EPSILON)
    dq_copy.wait_recv()

    for i in (2, 3, 4, 5):
        y_copies[i].wait_recv()
    near_keys = ((acc[0, own] + y_read(2) + y_read(5)) * norm).astype(BF16)
    near_values = ((acc[1, own] + y_read(3) + y_read(4)) * norm).astype(BF16)

    def cross(rows, head):
        cols = slice(head * HEAD_DIM, (head + 1) * HEAD_DIM)
        return attend(dq2[rows, cols], near_keys[:, cols], near_values[:, cols], dec_allowed[rows])

    dres[...] = jnp.concatenate([cross(slice(DROWS, ROWS), head) for head in range(2)], axis=1)
    up = remote(dres, drecv, up_s, up_r, upper)
    up.start()
    cross_out[...] = jnp.concatenate([cross(slice(0, DROWS), head) for head in range(2)], axis=1)

    for copy in y_copies + stat_copies:
        copy.wait_send()
    up.wait()
    cross_out[...] = cross_out[...] + drecv[...]


def body(
    hidden_in, enc_query, enc_key, enc_value, dec_query, out_proj, key_proj, value_proj,
    norm_gain, enc_len, dec_len, example_order, enc_bounds, dec_bounds,
):
    vmem = pl.BlockSpec(memory_space=pltpu.VMEM)
    anywhere = pl.BlockSpec(memory_space=pl.ANY)
    dma = pltpu.SemaphoreType.DMA
    gain = norm_gain.reshape(32, 128)
    square = (ROWS, 128)
    return pl.pallas_call(
        kernel,
        out_shape=(
            jax.ShapeDtypeStruct((ROWS, FEAT), BF16),
            jax.ShapeDtypeStruct((DROWS, WID), BF16),
        ),
        in_specs=[anywhere] * 14,
        out_specs=(vmem, vmem),
        scratch_shapes=[
            pltpu.VMEM((ROWS, WID), BF16),
            pltpu.VMEM((ROWS, WID), BF16),
            pltpu.VMEM((ROWS, WID), BF16),
            pltpu.VMEM(gain.shape, F32),
            pltpu.VMEM((STEPS, 2, 8, 128), F32),
            pltpu.VMEM((3, 1, 256), jnp.int32),
            pltpu.SMEM(enc_bounds.shape, jnp.int32),
            pltpu.SMEM(dec_bounds.shape, jnp.int32),
            pltpu.VMEM((FEAT, WID), BF16),
            pltpu.VMEM((NZ, 2, BLK, WID), BF16),
            pltpu.VMEM((2, NY, ROWS, HEAD_DIM), BF16),
            pltpu.VMEM((ROWS, 2 * FEAT), BF16),
            pltpu.VMEM((STEPS, 2) + square, BF16),
            pltpu.VMEM((STEPS, NY, 2) + square, BF16),
            pltpu.VMEM((STEPS, 2, NY) + square, F32),
            pltpu.VMEM((STEPS, 2, NY) + square, BF16),
            pltpu.VMEM((STEPS, 2, NY) + square, BF16),
            pltpu.VMEM((STEPS, 2, NY) + square, BF16),
            pltpu.VMEM((STEPS, 2, NY) + square, BF16),
            pltpu.VMEM((STEPS, NY, ROWS, 4 * BLK), BF16),
            pltpu.VMEM((2, NY, ROWS, WID), F32),
            pltpu.VMEM((NY,) + square, F32),
            pltpu.VMEM((STEPS, NY, 2) + square, BF16),
            pltpu.VMEM((STEPS, 2) + square, BF16),
            pltpu.VMEM((ROWS, 2 * FEAT), F32),
            pltpu.VMEM((6, ROWS, WID), BF16),
            pltpu.VMEM((6, ROWS, WID), BF16),
            pltpu.VMEM((NY, 8, ROWS), F32),
            pltpu.VMEM((NY - 1, 8, ROWS), F32),
            pltpu.VMEM((2 * DROWS, WID), BF16),
            pltpu.VMEM((DROWS, WID), BF16),
            pltpu.VMEM((DROWS, WID), BF16),
            dma((15,)),
            dma((6,)), dma((6,)),
            dma((HOPS,)), dma((HOPS,)),
            dma((HOPS,)), dma((HOPS,)),
            dma((HOPS,)), dma((HOPS,)),
            dma((HOPS,)), dma((HOPS,)),
            dma, dma,
            dma, dma,
            dma((STEPS,)), dma((STEPS, NY - 1)),
            dma((STEPS, NY - 1)), dma((STEPS,)),
            dma((6,)), dma((6,)),
            dma((STEPS + 4, 2)), dma((STEPS + 4, 2)),
            dma((STEPS + 4, 2)), dma((STEPS + 4, 2)),
            dma((6,)), dma((6,)),
            dma((NY - 1,)), dma((NY - 1,)),
        ],
        compiler_params=pltpu.CompilerParams(
            collective_id=0, has_side_effects=True, vmem_limit_bytes=VMEM_LIMIT
        ),
        name="encoder_to_cross",
    )(
        hidden_in, enc_query, enc_key, enc_value, dec_query, out_proj.T, key_proj, value_proj,
        gain, enc_len.reshape(1, 256), dec_len.reshape(1, 256),
        example_order.reshape(1, 256), enc_bounds, dec_bounds,
    )


def solution(mesh):
    return jax.shard_map(
        body,
        mesh=mesh,
        in_specs=(
            P("wide", "head"), P("wide", "head"), P("wide", "head"), P("wide", "head"),
            P("wide", "head"), P("head", "wide"), P("wide", "head"), P("wide", "head"),
            P(), P(), P(), P(), P(), P(),
        ),
        out_specs=(P("wide", "head"), P("wide", "head")),
        check_vma=False,
    )
```

```python
import jax
import jax.numpy as jnp
from jax import lax
from jax.experimental import pallas as pl
from jax.experimental.pallas import tpu as pltpu
from jax.sharding import PartitionSpec as P

MESH = pl.DeviceIdType.MESH
F32 = jnp.float32
BF16 = jnp.bfloat16

HEAD_DIM = 256
NZ = 16
NY = 4
NX = 4
NW = NY * NZ * 2
ROWS = 128
DROWS = 64
WID = 512
PIECE = 32
BLK = 2 * PIECE
FEAT = NZ * BLK
LANES = FEAT // 128
HOPS = NZ // 2
STEPS = NZ // 4
UNITS = STEPS * NY
GROUP = NY * ROWS
EPSILON = 1e-06
SCALE = 1.0 / 16.0
VMEM_LIMIT = 60 * 1024 * 1024


def nt(a, b):
    return lax.dot_general(a, b, (((1,), (1,)), ((), ())), preferred_element_type=F32)


def nn(a, b):
    return lax.dot_general(a, b, (((1,), (0,)), ((), ())), preferred_element_type=F32)


def iota(shape, dim):
    return lax.broadcasted_iota(jnp.int32, shape, dim)


def attend(q, k, v, allowed):
    scores = jnp.where(allowed, nt(q, k) * SCALE, -1e30)
    weights = jnp.where(allowed, jnp.exp(scores - jnp.max(scores, axis=1, keepdims=True)), 0.0)
    total = jnp.maximum(jnp.sum(weights, axis=1, keepdims=True), 1.0)
    return nn((weights / total).astype(BF16), v).astype(BF16)


def kernel(
    hidden, q_hbm, k_hbm, v_hbm, dq_hbm, wo_hbm, wk_hbm, wv_hbm, gain_hbm,
    elen_hbm, dlen_hbm, order_hbm, ebound_hbm, dbound_hbm,
    enc_out, cross_out,
    q_ref, k_ref, v_ref, gain_ref, gain_c, back_c, lens_ref, ebound, dbound,
    wo, kvw, ctx, hid, hid_c, hid_in, part, x1s, x1r, x2s, x2r, res, acc, sums, out_c, out_in, out_w,
    ys, yr, st, str_, dq2, dres, drecv,
    in_sem, first_s, first_r, wo_s, wo_r, wof_s, wof_r, kv_s, kv_r, kvf_s, kvf_r,
    dq_s, dq_r, up_s, up_r, hid_s, hid_r, out_s, out_r, ctx_s, ctx_r, xs1, xr1, xs2, xr2, sum_s, sum_r,
    y_s, y_r, st_s, st_r,
):
    w = lax.axis_index("wide")
    x = lax.axis_index("head")
    c = w % 2
    z = (w // 2) % NZ
    y = w // (2 * NZ)
    step_dir = 1 - 2 * c

    def wide(yy, zz, cc):
        return (yy * NZ + zz) * 2 + cc

    sib = (w + step_dir, x)
    z_next = (wide(y, (z + step_dir + NZ) % NZ, c), x)
    z_prev = (wide(y, (z - step_dir + NZ) % NZ, c), x)
    ya, yb, y2 = y + 1 - 2 * (y % 2), NY - 1 - y, (y + 2) % NY
    y_a, y_b, y_2 = (wide(ya, z, c), x), (wide(yb, z, c), x), (wide(y2, z, c), x)
    xa, xb, x2 = x + 1 - 2 * (x % 2), NX - 1 - x, (x + 2) % NX
    x_a, x_b = (w, xa), (w, xb)
    upper, lower = ((w + 1) % NW, x), ((w + NW - 1) % NW, x)
    adder = (wide(x, z, c), x)
    off_diagonal = x != y
    near = (y_2, y_a, y_b)
    relation = jnp.where(ya == x, 1, jnp.where(yb == x, 2, 0))
    own = NY - 1
    cross = (wide(y, (z - step_dir + NZ) % NZ, 1 - c), x)
    greet = (sib, z_next, z_prev, cross, y_a, y_b, y_2, x_a, x_b, upper, lower)

    def remote(src, dst, ss, rs, dev):
        return pltpu.make_async_remote_copy(
            src_ref=src, dst_ref=dst, send_sem=ss, recv_sem=rs, device_id=dev, device_id_type=MESH
        )

    def cols_of(i, width):
        return pl.ds(pl.multiple_of(i * width, width), width)

    barrier = pltpu.get_barrier_semaphore()
    for dev in greet:
        pl.semaphore_signal(barrier, inc=1, device_id=dev, device_id_type=MESH)

    piece = cols_of(c, PIECE)
    mine = pl.ds(pl.multiple_of(z * BLK + c * PIECE, PIECE), PIECE)
    pairs = (
        (wk_hbm, kvw.at[z, 0, piece]), (wv_hbm, kvw.at[z, 1, piece]),
        (hidden, hid.at[:, pl.ds(0, FEAT)]), (hidden, hid.at[:, pl.ds(FEAT, FEAT)]), (wo_hbm, wo.at[mine]),
        (elen_hbm, lens_ref.at[0]), (dlen_hbm, lens_ref.at[1]), (order_hbm, lens_ref.at[2]),
        (ebound_hbm, ebound), (dbound_hbm, dbound),
        (q_hbm, q_ref), (k_hbm, k_ref), (v_hbm, v_ref),
        (gain_hbm, gain_ref), (dq_hbm, dq2.at[pl.ds(0, DROWS)]),
    )
    loads = [pltpu.make_async_copy(a, b, in_sem.at[i]) for i, (a, b) in enumerate(pairs)]
    for load in loads:
        load.start()

    pl.semaphore_wait(barrier, len(greet))

    around = (z_next, cross, sib)
    wo_first = [
        remote(wo_hbm, wo.at[mine], first_s.at[i], first_r.at[i], dev) for i, dev in enumerate(around)
    ]
    kv_first = [
        remote(kvw.at[z, :, piece], kvw.at[z, :, piece], first_s.at[3 + i], first_r.at[3 + i], dev)
        for i, dev in enumerate(around)
    ]
    for copy in wo_first:
        copy.start()
    for load in loads[:2]:
        load.wait()
    for copy in kv_first:
        copy.start()
    dq_copy = remote(dq_hbm, dq2.at[pl.ds(DROWS, DROWS)], dq_s, dq_r, lower)
    dq_copy.start()

    def turned(ref, by):
        wider = ref[:, pl.ds(pl.multiple_of((by // 2) * 128, 128), FEAT + 128)].astype(F32)
        return jnp.where(by % 2 == 1, wider[:, BLK : BLK + FEAT], wider[:, 0:FEAT])

    def sides(s):
        return slice(s * 128, (s + 1) * 128), slice((LANES - 1 - s) * 128, (LANES - s) * 128)

    def hid_copy(s):
        return remote(hid_c.at[s], hid_in.at[s, relation], hid_s.at[s], hid_r.at[s, relation], adder)

    def hid_got(s, r):
        return remote(hid_in.at[s, r], hid_in.at[s, r], hid_s.at[s], hid_r.at[s, r], adder)

    def out_copy(s, r):
        return remote(out_c.at[s, r], out_in.at[s], out_s.at[s, r], out_r.at[s], near[r])

    for load in loads[2:4]:
        load.wait()
    hid_turned = turned(hid, z)
    for s in range(STEPS):
        for half, cols in enumerate(sides(s)):
            hid_c[s, half] = hid_turned[:, cols].astype(BF16)

    @pl.when(off_diagonal)
    def _():
        hid_copy(0).start()
        hid_in[:, own] = jnp.zeros_like(hid_c)

    @pl.when(jnp.logical_not(off_diagonal))
    def _():
        hid_in[:, own] = hid_c[...]

    for load in loads[4:10]:
        load.wait()

    n = 256
    onehot = jnp.where(lens_ref[2] == iota((n, n), 0), 1.0, 0.0).astype(BF16)
    lens = jnp.concatenate([lens_ref[0], lens_ref[1], jnp.zeros((6, n), jnp.int32)], axis=0)
    ordered = nn(lens.astype(F32).astype(BF16), onehot)
    upto = jnp.where(iota((n, n), 0) <= iota((n, n), 1), 1.0, 0.0).astype(BF16)
    ends = nn(ordered.astype(BF16), upto)
    place = iota((1, n), 1)

    def start(row, first):
        return jnp.sum(jnp.where(place < first, row, 0.0), axis=1, keepdims=True)

    def tags(ends_row, offsets, last):
        pos = jnp.sum(jnp.where(ends_row <= offsets, 1.0, 0.0), axis=1, keepdims=True)
        return jnp.where(pos < last, pos, -1.0)

    rows_i = iota((ROWS, 1), 0)
    enc_base = start(ordered[0:1], ebound[w])
    enc_col = tags(ends[0:1], enc_base + rows_i.astype(F32), ebound[w + 1].astype(F32))
    diag = iota((ROWS, ROWS), 0) == iota((ROWS, ROWS), 1)
    enc_row = jnp.sum(jnp.where(diag, enc_col, 0.0), axis=0, keepdims=True)
    enc_allowed = (enc_col == enc_row) & (enc_row >= 0.0)

    def number(i):
        return (i + 2 * NZ) % NZ

    def wo_block(i):
        return wo.at[cols_of(number(i), BLK)]

    def kv_block(i):
        return kvw.at[number(i)]

    def hop(i, buffer, ss, rs):
        at = buffer(z - step_dir * (i - 1))
        return remote(at, at, ss.at[i - 1], rs.at[i - 1], z_next)

    def got(i, buffer, ss, rs):
        at = buffer(z - step_dir * i)
        return remote(at, at, ss.at[i - 1], rs.at[i - 1], z_next)

    def fan(i, buffer, ss, rs):
        at = buffer(z - step_dir * i)
        return remote(at, at, ss.at[i - 1], rs.at[i - 1], sib)

    def fan_got(i, buffer, ss, rs):
        at = buffer(z + step_dir * i)
        return remote(at, at, ss.at[i - 1], rs.at[i - 1], sib)

    ring_wo, fan_wo = (wo_block, wo_s, wo_r), (wo_block, wof_s, wof_r)
    ring_kv, fan_kv = (kv_block, kv_s, kv_r), (kv_block, kvf_s, kvf_r)

    def forward(i, ring, side):
        hop(i + 1, *ring).start()
        fan(i, *side).start()

    def pass_on(i, ring, side):
        got(i, *ring).wait_recv()

        @pl.when(i < HOPS)
        def _():
            forward(i, ring, side)

    def quad(s):
        return z + 2 * s, z + 2 * s + 1, z - 2 * s - 2, z - 2 * s - 1

    def ctx_copy(head, src, dst, index, dev):
        return remote(ctx.at[head, src], ctx.at[head, dst], ctx_s.at[index], ctx_r.at[index], dev)

    for copy in wo_first[:2]:
        copy.wait_recv()
    forward(1, ring_wo, fan_wo)
    for load in loads[10:]:
        load.wait()
    for head in range(2):
        cols = slice(head * HEAD_DIM, (head + 1) * HEAD_DIM)
        ctx[head, own] = attend(q_ref[:, cols], k_ref[:, cols], v_ref[:, cols], enc_allowed)
    ctx_sent = [
        ctx_copy(0, own, 1, 0, y_a), ctx_copy(1, own, 2, 3, y_b),
        ctx_copy(1, own, 1, 2, y_a), ctx_copy(0, own, 2, 1, y_b),
    ]
    for copy in ctx_sent:
        copy.start()
    for copy in kv_first[:2]:
        copy.wait_recv()
    forward(1, ring_kv, fan_kv)
    pass_on(2, ring_wo, fan_wo)

    ctx_copy(0, 1, 1, 0, y_a).wait_recv()
    ctx_sent.append(ctx_copy(0, 1, 0, 4, y_b))
    ctx_sent[-1].start()
    ctx_copy(1, 2, 2, 3, y_b).wait_recv()
    ctx_sent.append(ctx_copy(1, 2, 0, 5, y_a))
    ctx_sent[-1].start()

    @pl.when(off_diagonal)
    def _():
        hid_copy(1).start()
        hid_in[:, 0:own] = jnp.zeros((STEPS, own, 2, ROWS, 128), BF16)

    for i in range(2 * LANES):
        row = gain_ref[pl.ds(y * LANES + i % LANES, 1), :]
        out_w[0:8, i * 128 : (i + 1) * 128] = jnp.broadcast_to(row, (8, 128))
    gain_turned = turned(out_w.at[pl.ds(0, 8)], z)
    for s in range(STEPS):
        for half, cols in enumerate(sides(s)):
            gain_c[s, half] = gain_turned[:, cols]
            back_c[s, half] = 1.0 / gain_turned[:, cols]
    sums[...] = jnp.zeros_like(sums)

    def round_one(s, first, count, index):
        return [
            remote(
                x1s.at[s, i, pl.ds(first, count)], x1r.at[s, i, pl.ds(first, count)],
                xs1.at[index, i], xr1.at[index, i], (x_a, x_b)[i],
            )
            for i in range(2)
        ]

    def round_two(s, first, count, index):
        return [
            remote(
                x2s.at[s, i, pl.ds(first, count)], x2r.at[s, i, pl.ds(first, count)],
                xs2.at[index, i], xr2.at[index, i], (x_b, x_a)[i],
            )
            for i in range(2)
        ]

    x_sent = []

    def project(s, first, count, index=None):
        @pl.when(jnp.logical_not(off_diagonal))
        def _():
            for r in range(first, min(first + count, own)):
                hid_got(s, r).wait_recv()

        groups = slice(first, first + count)
        weights = jnp.concatenate([wo_block(i)[...] for i in quad(s)], axis=0)
        rows = [ctx[head, groups].reshape(count * ROWS, HEAD_DIM) for head in range(2)]
        term = nt(rows[0], weights[:, 0:HEAD_DIM]) + nt(rows[1], weights[:, HEAD_DIM:WID])
        for half in range(2):
            value = term[:, half * 128 : (half + 1) * 128].reshape(count, ROWS, 128)
            value = value + hid_in[s, groups, half].astype(F32)
            part[s, half, groups] = value
            x1s[s, half, groups] = value.astype(BF16)
        for copy in sum_one(s) if index is None else round_one(s, first, count, index):
            copy.start()
            x_sent.append(copy)

    def sum_one(s):
        return [
            remote(
                x1s.at[s, half, q], x1r.at[s, half, q], sum_s.at[s, k], sum_r.at[s, k], (x_a, x_b)[half]
            )
            for k, (half, q) in enumerate(((0, x2), (1, x2), (0, xa), (1, xb)))
        ]

    def sum_two(s):
        return [
            remote(
                x2s.at[s, half, q], x2r.at[s, half, q], sum_s.at[s, 4 + half], sum_r.at[s, 4 + half],
                (x_b, x_a)[half],
            )
            for half, q in enumerate((xb, xa))
        ]

    def spread_one(s):
        return [
            remote(
                res.at[s, :, x], res.at[s, :, x], sum_s.at[s, 6 + side], sum_r.at[s, 6 + side], dev
            )
            for side, dev in enumerate((x_a, x_b))
        ]

    def spread_two(s):
        return [
            remote(
                res.at[s, half, q], res.at[s, half, q], sum_s.at[s, 8 + half], sum_r.at[s, 8 + half],
                (x_b, x_a)[half],
            )
            for half, q in enumerate((xa, xb))
        ]

    def send(copy):
        copy.start()
        x_sent.append(copy)

    def relay_sum(s):
        for half, q in enumerate((xb, xa)):
            sum_one(s)[half].wait_recv()
            total = part[s, half, q] + x1r[s, half, q].astype(F32)
            x2s[s, half, q] = total.astype(BF16)
            send(sum_two(s)[half])

    def own_sum(s):
        for half in range(2):
            sum_one(s)[2 + half].wait_recv()
            sum_two(s)[half].wait_recv()
            total = part[s, half, x] + x1r[s, half, x].astype(F32) + x2r[s, half, x].astype(F32)
            res[s, half, x] = (total * gain_c[s, half, 0:1, :]).astype(BF16)
        for copy in spread_one(s):
            send(copy)

    def relay_spread(s):
        for side in range(2):
            spread_one(s)[side].wait_recv()
            send(spread_two(s)[side])

    def gathered(s):
        for copy in spread_two(s):
            copy.wait_recv()
        for half in range(2):
            total = res[s, half].astype(F32) * back_c[s, half, 0:1, :]
            sums[...] += total * total
            out_c[s, :, half] = total.astype(BF16)
        go_home(s, 0, NY)

    def go_home(s, first, count):
        @pl.when(jnp.logical_not(off_diagonal))
        def _():
            for r in range(first, min(first + count, own)):
                out_copy(s, r).start()
            if first + count > own:
                out_in[s] = out_c[s, own]

    def exchange(s, first, count, index):
        groups = slice(first, first + count)
        for half, copy in enumerate(round_one(s, first, count, index)):
            copy.wait_recv()
            total = part[s, half, groups] + x1r[s, half, groups].astype(F32)
            part[s, half, groups] = total
            x2s[s, half, groups] = total.astype(BF16)
            copy = round_two(s, first, count, index)[half]
            copy.start()
            x_sent.append(copy)

    def finish(s, first, count, index):
        groups = slice(first, first + count)
        for half, copy in enumerate(round_two(s, first, count, index)):
            copy.wait_recv()
            total = part[s, half, groups] + x2r[s, half, groups].astype(F32)
            sums[groups] += total * total
            res[s, half, groups] = (total * gain_c[s, half, 0:1, :]).astype(BF16)
            out_c[s, groups, half] = total.astype(BF16)
        go_home(s, first, count)

    def kv_weights(s, kind):
        return jnp.concatenate([kvw[number(i), kind] for i in quad(s)], axis=0)

    def accumulate(s, first, count):
        groups = slice(first, first + count)
        rows = [res[s, half, groups].reshape(count * ROWS, 2 * BLK) for half in range(2)]
        rows = jnp.concatenate(rows, axis=1)
        for kind in range(2):
            term = nn(rows, kv_weights(s, kind)).reshape(count, ROWS, WID)
            acc[kind, groups] = term if s == 0 else acc[kind, groups] + term

    def fans(s, side):
        for i in (2 * s + 1, 2 * s + 2):
            if i < HOPS:
                fan_got(i, *side).wait_recv()

    def send_hidden(s):
        @pl.when(off_diagonal)
        def _():
            hid_copy(s).start()

    all_rows, early, late, end = (0, NY), (0, 2), (2, 2), STEPS - 1
    for copy in wo_first[2:]:
        copy.wait_recv()
    pass_on(3, ring_wo, fan_wo)
    fans(0, fan_wo)
    ctx_copy(0, 2, 2, 1, y_b).wait_recv()
    ctx_copy(1, 1, 1, 2, y_a).wait_recv()
    pass_on(2, ring_kv, fan_kv)
    ctx_copy(0, 0, 0, 4, y_b).wait_recv()
    ctx_copy(1, 0, 0, 5, y_a).wait_recv()
    project(0, *all_rows)
    send_hidden(2)
    pass_on(4, ring_wo, fan_wo)
    fans(1, fan_wo)
    project(1, *all_rows)
    pass_on(5, ring_wo, fan_wo)
    pass_on(3, ring_kv, fan_kv)
    relay_sum(0)
    send_hidden(3)
    pass_on(6, ring_wo, fan_wo)
    own_sum(0)
    pass_on(4, ring_kv, fan_kv)
    relay_sum(1)
    fans(2, fan_wo)
    project(2, *all_rows)
    pass_on(7, ring_wo, fan_wo)
    relay_spread(0)
    own_sum(1)
    pass_on(5, ring_kv, fan_kv)
    relay_sum(2)
    pass_on(8, ring_wo, fan_wo)
    gathered(0)
    fans(3, fan_wo)
    project(3, *early, 0)
    project(3, *late, 1)
    pass_on(6, ring_kv, fan_kv)
    relay_spread(1)
    own_sum(2)
    for copy in kv_first[2:]:
        copy.wait_recv()
    fans(0, fan_kv)
    accumulate(0, *all_rows)
    pass_on(7, ring_kv, fan_kv)
    gathered(1)
    exchange(3, *early, 0)
    exchange(3, *late, 1)
    relay_spread(2)
    fans(1, fan_kv)
    accumulate(1, *all_rows)
    pass_on(8, ring_kv, fan_kv)
    gathered(2)
    fans(2, fan_kv)
    accumulate(2, *all_rows)
    fans(3, fan_kv)

    y_copies = [remote(ys.at[i], yr.at[i], y_s.at[i], y_r.at[i], (y_a, y_b)[i % 2]) for i in range(6)]

    def y_send(i, value):
        ys[i] = value.astype(BF16)
        y_copies[i].start()

    def y_read(i):
        return yr[i].astype(F32)

    finish(end, *early, 0)
    accumulate(end, *early)
    y_send(0, acc[0, 0])
    y_send(1, acc[1, 0])
    y_send(2, acc[0, 1])
    finish(end, *late, 1)
    accumulate(end, *late)
    y_send(3, acc[1, 2])
    y_copies[1].wait_recv()
    y_send(4, acc[1, 1] + y_read(1))
    y_copies[0].wait_recv()
    y_send(5, acc[0, 2] + y_read(0))

    columns = jnp.sum(sums[...], axis=2, keepdims=True)
    squares = jnp.sum(jnp.where(diag[None], columns, 0.0), axis=1, keepdims=True)
    st[...] = jnp.broadcast_to(squares, (NY, 8, ROWS))
    stat_copies = [remote(st.at[r], str_.at[r], st_s.at[r], st_r.at[r], near[r]) for r in range(own)]
    for copy in stat_copies:
        copy.start()

    @pl.when(off_diagonal)
    def _():
        for s in range(STEPS):
            out_copy(s, 0).wait_recv()

    for s in range(STEPS):
        for half, cols in enumerate(sides(s)):
            for copy in range(2):
                at = slice(cols.start + copy * FEAT, cols.stop + copy * FEAT)
                out_w[:, at] = out_in[s, half].astype(F32)
    enc_out[...] = turned(out_w, (NZ - z) % NZ).astype(BF16)

    lower_half = rows_i < DROWS
    above_end = jnp.minimum(w + 2, NW)
    base = jnp.where(lower_half, start(ordered[1:2], dbound[w]), start(ordered[1:2], dbound[w + 1]))
    last = jnp.where(lower_half, dbound[w + 1].astype(F32), dbound[above_end].astype(F32))
    offset = (rows_i % DROWS).astype(F32)
    dec_col = tags(ends[1:2], base + offset, last)
    dec_allowed = (dec_col == enc_row) & (enc_row >= 0.0)

    for copy in stat_copies:
        copy.wait_recv()
    square = st[own] + str_[0] + str_[1] + str_[2]
    square_col = jnp.sum(jnp.where(diag, square[0:1], 0.0), axis=1, keepdims=True)
    norm = lax.rsqrt(square_col * (1.0 / (NY * FEAT)) + EPSILON)
    dq_copy.wait_recv()

    for i in (2, 3, 4, 5):
        y_copies[i].wait_recv()
    near_keys = ((acc[0, own] + y_read(2) + y_read(5)) * norm).astype(BF16)
    near_values = ((acc[1, own] + y_read(3) + y_read(4)) * norm).astype(BF16)

    def cross(rows, head):
        cols = slice(head * HEAD_DIM, (head + 1) * HEAD_DIM)
        return attend(dq2[rows, cols], near_keys[:, cols], near_values[:, cols], dec_allowed[rows])

    dres[...] = jnp.concatenate([cross(slice(DROWS, ROWS), head) for head in range(2)], axis=1)
    up = remote(dres, drecv, up_s, up_r, upper)
    up.start()
    cross_out[...] = jnp.concatenate([cross(slice(0, DROWS), head) for head in range(2)], axis=1)

    for copy in wo_first + kv_first + [dq_copy] + ctx_sent + x_sent + y_copies + stat_copies:
        copy.wait_send()

    @pl.loop(1, HOPS)
    def _(i):
        hop(i + 1, *ring_wo).wait_send()
        hop(i + 1, *ring_kv).wait_send()
        fan(i, *fan_wo).wait_send()
        fan(i, *fan_kv).wait_send()

    @pl.when(off_diagonal)
    def _():
        for s in range(STEPS):
            hid_copy(s).wait_send()

    @pl.when(jnp.logical_not(off_diagonal))
    def _():
        for s in range(STEPS):
            for r in range(own):
                out_copy(s, r).wait_send()

    up.wait()
    cross_out[...] = cross_out[...] + drecv[...]


def body(
    hidden_in, enc_query, enc_key, enc_value, dec_query, out_proj, key_proj, value_proj,
    norm_gain, enc_len, dec_len, example_order, enc_bounds, dec_bounds,
):
    vmem = pl.BlockSpec(memory_space=pltpu.VMEM)
    anywhere = pl.BlockSpec(memory_space=pl.ANY)
    dma = pltpu.SemaphoreType.DMA
    gain = norm_gain.reshape(32, 128)
    square = (ROWS, 128)
    return pl.pallas_call(
        kernel,
        out_shape=(
            jax.ShapeDtypeStruct((ROWS, FEAT), BF16),
            jax.ShapeDtypeStruct((DROWS, WID), BF16),
        ),
        in_specs=[anywhere] * 14,
        out_specs=(vmem, vmem),
        scratch_shapes=[
            pltpu.VMEM((ROWS, WID), BF16),
            pltpu.VMEM((ROWS, WID), BF16),
            pltpu.VMEM((ROWS, WID), BF16),
            pltpu.VMEM(gain.shape, F32),
            pltpu.VMEM((STEPS, 2, 8, 128), F32),
            pltpu.VMEM((STEPS, 2, 8, 128), F32),
            pltpu.VMEM((3, 1, 256), jnp.int32),
            pltpu.SMEM(enc_bounds.shape, jnp.int32),
            pltpu.SMEM(dec_bounds.shape, jnp.int32),
            pltpu.VMEM((FEAT, WID), BF16),
            pltpu.VMEM((NZ, 2, BLK, WID), BF16),
            pltpu.VMEM((2, NY, ROWS, HEAD_DIM), BF16),
            pltpu.VMEM((ROWS, 2 * FEAT), BF16),
            pltpu.VMEM((STEPS, 2) + square, BF16),
            pltpu.VMEM((STEPS, NY, 2) + square, BF16),
            pltpu.VMEM((STEPS, 2, NY) + square, F32),
            pltpu.VMEM((STEPS, 2, NY) + square, BF16),
            pltpu.VMEM((STEPS, 2, NY) + square, BF16),
            pltpu.VMEM((STEPS, 2, NY) + square, BF16),
            pltpu.VMEM((STEPS, 2, NY) + square, BF16),
            pltpu.VMEM((STEPS, 2, NY) + square, BF16),
            pltpu.VMEM((2, NY, ROWS, WID), F32),
            pltpu.VMEM((NY,) + square, F32),
            pltpu.VMEM((STEPS, NY, 2) + square, BF16),
            pltpu.VMEM((STEPS, 2) + square, BF16),
            pltpu.VMEM((ROWS, 2 * FEAT), F32),
            pltpu.VMEM((6, ROWS, WID), BF16),
            pltpu.VMEM((6, ROWS, WID), BF16),
            pltpu.VMEM((NY, 8, ROWS), F32),
            pltpu.VMEM((NY - 1, 8, ROWS), F32),
            pltpu.VMEM((2 * DROWS, WID), BF16),
            pltpu.VMEM((DROWS, WID), BF16),
            pltpu.VMEM((DROWS, WID), BF16),
            dma((15,)),
            dma((6,)), dma((6,)),
            dma((HOPS,)), dma((HOPS,)),
            dma((HOPS,)), dma((HOPS,)),
            dma((HOPS,)), dma((HOPS,)),
            dma((HOPS,)), dma((HOPS,)),
            dma, dma,
            dma, dma,
            dma((STEPS,)), dma((STEPS, NY - 1)),
            dma((STEPS, NY - 1)), dma((STEPS,)),
            dma((6,)), dma((6,)),
            dma((2, 2)), dma((2, 2)),
            dma((2, 2)), dma((2, 2)),
            dma((STEPS - 1, 10)), dma((STEPS - 1, 10)),
            dma((6,)), dma((6,)),
            dma((NY - 1,)), dma((NY - 1,)),
        ],
        compiler_params=pltpu.CompilerParams(
            collective_id=0, has_side_effects=True, vmem_limit_bytes=VMEM_LIMIT
        ),
        name="encoder_to_cross",
    )(
        hidden_in, enc_query, enc_key, enc_value, dec_query, out_proj.T, key_proj, value_proj,
        gain, enc_len.reshape(1, 256), dec_len.reshape(1, 256),
        example_order.reshape(1, 256), enc_bounds, dec_bounds,
    )


def solution(mesh):
    return jax.shard_map(
        body,
        mesh=mesh,
        in_specs=(
            P("wide", "head"), P("wide", "head"), P("wide", "head"), P("wide", "head"),
            P("wide", "head"), P("head", "wide"), P("wide", "head"), P("wide", "head"),
            P(), P(), P(), P(), P(), P(),
        ),
        out_specs=(P("wide", "head"), P("wide", "head")),
        check_vma=False,
    )
```

```python
import jax
import jax.numpy as jnp
from jax import lax
from jax.experimental import pallas as pl
from jax.experimental.pallas import tpu as pltpu
from jax.sharding import PartitionSpec as P

MESH = pl.DeviceIdType.MESH
F32 = jnp.float32
BF16 = jnp.bfloat16

HEAD_DIM = 256
NZ = 16
NY = 4
NX = 4
NW = NY * NZ * 2
ROWS = 128
DROWS = 64
WID = 512
PIECE = 32
BLK = 2 * PIECE
FEAT = NZ * BLK
LANES = FEAT // 128
HOPS = NZ // 2
STEPS = NZ // 4
UNITS = STEPS * NY
GROUP = NY * ROWS
EPSILON = 1e-06
SCALE = 1.0 / 16.0
VMEM_LIMIT = 60 * 1024 * 1024


def nt(a, b):
    return lax.dot_general(a, b, (((1,), (1,)), ((), ())), preferred_element_type=F32)


def nn(a, b):
    return lax.dot_general(a, b, (((1,), (0,)), ((), ())), preferred_element_type=F32)


def iota(shape, dim):
    return lax.broadcasted_iota(jnp.int32, shape, dim)


def attend(q, k, v, allowed):
    scores = jnp.where(allowed, nt(q, k) * SCALE, -1e30)
    weights = jnp.where(allowed, jnp.exp(scores - jnp.max(scores, axis=1, keepdims=True)), 0.0)
    total = jnp.maximum(jnp.sum(weights, axis=1, keepdims=True), 1.0)
    return nn((weights / total).astype(BF16), v).astype(BF16)


def kernel(
    hidden, q_hbm, k_hbm, v_hbm, dq_hbm, wo_hbm, wk_hbm, wv_hbm, gain_hbm,
    elen_hbm, dlen_hbm, order_hbm, ebound_hbm, dbound_hbm,
    enc_out, cross_out,
    q_ref, k_ref, v_ref, gain_ref, gain_c, lens_ref, ebound, dbound,
    wo, kvw, ctx, hid, hid_c, hid_in, part, x1s, x1r, x2s, x2r, res, acc, sums, out_c, out_in, out_w,
    ys, yr, st, str_, dq2, dres, drecv,
    in_sem, first_s, first_r, wo_s, wo_r, wof_r, kv_s, kv_r, kvf_r,
    dq_s, dq_r, up_s, up_r, hid_s, hid_r, out_s, out_r, ctx_s, ctx_r, xs1, xr1, xs2, xr2,
    y_s, y_r, st_s, st_r,
):
    w = lax.axis_index("wide")
    x = lax.axis_index("head")
    c = w % 2
    z = (w // 2) % NZ
    y = w // (2 * NZ)
    step_dir = 1 - 2 * c

    def wide(yy, zz, cc):
        return (yy * NZ + zz) * 2 + cc

    sib = (w + step_dir, x)
    z_next = (wide(y, (z + step_dir + NZ) % NZ, c), x)
    z_prev = (wide(y, (z - step_dir + NZ) % NZ, c), x)
    ya, yb, y2 = y + 1 - 2 * (y % 2), NY - 1 - y, (y + 2) % NY
    y_a, y_b, y_2 = (wide(ya, z, c), x), (wide(yb, z, c), x), (wide(y2, z, c), x)
    x_a, x_b = (w, x + 1 - 2 * (x % 2)), (w, NX - 1 - x)
    upper, lower = ((w + 1) % NW, x), ((w + NW - 1) % NW, x)
    adder = (wide(x, z, c), x)
    off_diagonal = x != y
    near = (y_2, y_a, y_b)
    relation = jnp.where(ya == x, 1, jnp.where(yb == x, 2, 0))
    own = NY - 1
    cross = (wide(y, (z - step_dir + NZ) % NZ, 1 - c), x)
    greet = (sib, z_next, z_prev, cross, y_a, y_b, y_2, x_a, x_b, upper, lower)

    def remote(src, dst, ss, rs, dev):
        return pltpu.make_async_remote_copy(
            src_ref=src, dst_ref=dst, send_sem=ss, recv_sem=rs, device_id=dev, device_id_type=MESH
        )

    def cols_of(i, width):
        return pl.ds(pl.multiple_of(i * width, width), width)

    barrier = pltpu.get_barrier_semaphore()
    for dev in greet:
        pl.semaphore_signal(barrier, inc=1, device_id=dev, device_id_type=MESH)

    piece = cols_of(c, PIECE)
    mine = piece
    pairs = (
        (wk_hbm, kvw.at[0, 0, piece]), (wv_hbm, kvw.at[0, 1, piece]),
        (hidden, hid.at[:, pl.ds(0, FEAT)]), (hidden, hid.at[:, pl.ds(FEAT, FEAT)]), (wo_hbm, wo.at[mine]),
        (elen_hbm, lens_ref.at[0]), (dlen_hbm, lens_ref.at[1]), (order_hbm, lens_ref.at[2]),
        (ebound_hbm, ebound), (dbound_hbm, dbound),
        (q_hbm, q_ref), (k_hbm, k_ref), (v_hbm, v_ref),
        (gain_hbm, gain_ref), (dq_hbm, dq2.at[pl.ds(0, DROWS)]),
    )
    loads = [pltpu.make_async_copy(a, b, in_sem.at[i]) for i, (a, b) in enumerate(pairs)]
    for load in loads:
        load.start()

    pl.semaphore_wait(barrier, len(greet))

    def out_at(i):
        return jnp.where(c == 0, NZ - i, i)

    def in_at(i):
        return jnp.where(c == 0, i, NZ - i)

    def rows_at(i, offset, count):
        return pl.ds(pl.multiple_of(i * BLK + offset, PIECE), count)

    around = ((z_next, out_at(1)), (cross, in_at(1)), (sib, 0))
    wo_first = [
        remote(wo_hbm, wo.at[rows_at(to, c * PIECE, PIECE)], wo_s, first_r.at[i], dev)
        for i, (dev, to) in enumerate(around)
    ]
    kv_first = [
        remote(kvw.at[0, :, piece], kvw.at[to, :, piece], first_s, first_r.at[3 + i], dev)
        for i, (dev, to) in enumerate(around)
    ]
    for copy in wo_first:
        copy.start()
    for load in loads[:2]:
        load.wait()
    for copy in kv_first:
        copy.start()
    dq_copy = remote(dq_hbm, dq2.at[pl.ds(DROWS, DROWS)], dq_s, dq_r, lower)
    dq_copy.start()

    def turned(ref, by):
        wider = ref[:, pl.ds(pl.multiple_of((by // 2) * 128, 128), FEAT + 128)].astype(F32)
        return jnp.where(by % 2 == 1, wider[:, BLK : BLK + FEAT], wider[:, 0:FEAT])

    def sides(s):
        return slice(s * 128, (s + 1) * 128), slice((LANES - 1 - s) * 128, (LANES - s) * 128)

    def hid_copy(s):
        return remote(hid_c.at[s], hid_in.at[s, relation], hid_s, hid_r.at[s, relation], adder)

    def hid_got(s, r):
        return remote(hid_in.at[s, r], hid_in.at[s, r], hid_s, hid_r.at[s, r], adder)

    def out_copy(s, r):
        return remote(out_c.at[s, r], out_in.at[s], out_s, out_r.at[s], near[r])

    for load in loads[2:4]:
        load.wait()
    hid_turned = turned(hid, z)
    for s in range(STEPS):
        for half, cols in enumerate(sides(s)):
            hid_c[s, half] = hid_turned[:, cols].astype(BF16)

    @pl.when(off_diagonal)
    def _():
        hid_copy(0).start()
        hid_in[:, own] = jnp.zeros_like(hid_c)

    @pl.when(jnp.logical_not(off_diagonal))
    def _():
        hid_in[:, own] = hid_c[...]

    for load in loads[4:10]:
        load.wait()

    n = 256
    onehot = jnp.where(lens_ref[2] == iota((n, n), 0), 1.0, 0.0).astype(BF16)
    lens = jnp.concatenate([lens_ref[0], lens_ref[1], jnp.zeros((6, n), jnp.int32)], axis=0)
    ordered = nn(lens.astype(F32).astype(BF16), onehot)
    upto = jnp.where(iota((n, n), 0) <= iota((n, n), 1), 1.0, 0.0).astype(BF16)
    ends = nn(ordered.astype(BF16), upto)
    place = iota((1, n), 1)

    def start(row, first):
        return jnp.sum(jnp.where(place < first, row, 0.0), axis=1, keepdims=True)

    def tags(ends_row, offsets, last):
        pos = jnp.sum(jnp.where(ends_row <= offsets, 1.0, 0.0), axis=1, keepdims=True)
        return jnp.where(pos < last, pos, -1.0)

    rows_i = iota((ROWS, 1), 0)
    enc_base = start(ordered[0:1], ebound[w])
    enc_col = tags(ends[0:1], enc_base + rows_i.astype(F32), ebound[w + 1].astype(F32))
    diag = iota((ROWS, ROWS), 0) == iota((ROWS, ROWS), 1)
    enc_row = jnp.sum(jnp.where(diag, enc_col, 0.0), axis=0, keepdims=True)
    enc_allowed = (enc_col == enc_row) & (enc_row >= 0.0)

    def wo_blocks(i, count):
        return wo.at[rows_at(i, 0, count * BLK)]

    def kv_blocks(i, count):
        return kvw.at[pl.ds(i, count)]

    def hop(i, blocks, ss, rs, _):
        return remote(blocks(out_at(i - 1), 1), blocks(out_at(i), 1), ss, rs.at[i - 1], z_next)

    def fan(k, blocks, ss, _, rs, arrives=False):
        count = min(2, HOPS - 1 - 2 * k)
        low = NZ - 2 * k - count if count == 2 else NZ - 2 * k - 1
        start = jnp.where(c == (1 if arrives else 0), low, 2 * k + 1)
        at = blocks(start, count)
        return remote(at, at, ss, rs.at[k], sib)

    ring_wo = (wo_blocks, wo_s, wo_r, wof_r)
    ring_kv = (kv_blocks, kv_s, kv_r, kvf_r)

    def forward(i, ring):
        hop(i + 1, *ring).start()
        if i % 2 == 0 or i == HOPS - 1:
            fan((i - 1) // 2, *ring).start()

    def pass_on(i, ring):
        hop(i, *ring).wait_recv()
        if i < HOPS:
            forward(i, ring)

    def ctx_copy(head, src, dst, index, dev):
        return remote(ctx.at[head, src], ctx.at[head, dst], ctx_s, ctx_r.at[index], dev)

    for copy in wo_first[:2]:
        copy.wait_recv()
    forward(1, ring_wo)
    for load in loads[10:]:
        load.wait()
    for head in range(2):
        cols = slice(head * HEAD_DIM, (head + 1) * HEAD_DIM)
        ctx[head, own] = attend(q_ref[:, cols], k_ref[:, cols], v_ref[:, cols], enc_allowed)
    ctx_first = [
        ctx_copy(0, own, 1, 0, y_a), ctx_copy(1, own, 2, 3, y_b),
        ctx_copy(1, own, 1, 2, y_a), ctx_copy(0, own, 2, 1, y_b),
    ]
    for copy in ctx_first:
        copy.start()
    for copy in kv_first[:2]:
        copy.wait_recv()
    forward(1, ring_kv)
    pass_on(2, ring_wo)

    ctx_copy(0, 1, 1, 0, y_a).wait_recv()
    ctx_copy(0, 1, 0, 4, y_b).start()
    ctx_copy(1, 2, 2, 3, y_b).wait_recv()
    ctx_copy(1, 2, 0, 5, y_a).start()

    @pl.when(off_diagonal)
    def _():
        hid_copy(1).start()
        hid_in[:, 0:own] = jnp.zeros((STEPS, own, 2, ROWS, 128), BF16)

    for i in range(2 * LANES):
        row = gain_ref[pl.ds(y * LANES + i % LANES, 1), :]
        out_w[0:8, i * 128 : (i + 1) * 128] = jnp.broadcast_to(row, (8, 128))
    gain_turned = turned(out_w.at[pl.ds(0, 8)], z)
    for s in range(STEPS):
        for half, cols in enumerate(sides(s)):
            gain_c[s, half] = gain_turned[:, cols]
    sums[...] = jnp.zeros_like(sums)

    def round_one(s, first, count, index):
        return [
            remote(
                x1s.at[s, i, pl.ds(first, count)], x1r.at[s, i, pl.ds(first, count)],
                xs1, xr1.at[index, i], (x_a, x_b)[i],
            )
            for i in range(2)
        ]

    def round_two(s, first, count, index):
        return [
            remote(
                x2s.at[s, i, pl.ds(first, count)], x2r.at[s, i, pl.ds(first, count)],
                xs2, xr2.at[index, i], (x_b, x_a)[i],
            )
            for i in range(2)
        ]

    def project(s, first, count, index):
        @pl.when(jnp.logical_not(off_diagonal))
        def _():
            for r in range(first, min(first + count, own)):
                hid_got(s, r).wait_recv()

        groups = slice(first, first + count)
        weights = jnp.concatenate([wo[cols, :] for cols in sides(s)], axis=0)
        rows = [ctx[head, groups].reshape(count * ROWS, HEAD_DIM) for head in range(2)]
        term = nt(rows[0], weights[:, 0:HEAD_DIM]) + nt(rows[1], weights[:, HEAD_DIM:WID])
        for half in range(2):
            value = term[:, half * 128 : (half + 1) * 128].reshape(count, ROWS, 128)
            value = value + hid_in[s, groups, half].astype(F32)
            part[s, half, groups] = value
            x1s[s, half, groups] = value.astype(BF16)
        for copy in round_one(s, first, count, index):
            copy.start()

    def exchange(s, first, count, index):
        groups = slice(first, first + count)
        for half, copy in enumerate(round_one(s, first, count, index)):
            copy.wait_recv()
            total = part[s, half, groups] + x1r[s, half, groups].astype(F32)
            part[s, half, groups] = total
            x2s[s, half, groups] = total.astype(BF16)
            copy = round_two(s, first, count, index)[half]
            copy.start()

    def finish(s, first, count, index):
        groups = slice(first, first + count)
        for half, copy in enumerate(round_two(s, first, count, index)):
            copy.wait_recv()
            total = part[s, half, groups] + x2r[s, half, groups].astype(F32)
            sums[groups] += total * total
            res[s, groups, :, half * 128 : (half + 1) * 128] = (total * gain_c[s, half, 0:1, :]).astype(BF16)
            out_c[s, groups, half] = total.astype(BF16)

        @pl.when(jnp.logical_not(off_diagonal))
        def _():
            for r in range(first, min(first + count, own)):
                out_copy(s, r).start()
            if first + count > own:
                out_in[s] = out_c[s, own]

    def kv_weights(s, kind):
        quad = (2 * s, 2 * s + 1, NZ - 2 - 2 * s, NZ - 1 - 2 * s)
        return jnp.concatenate([kvw[i, kind] for i in quad], axis=0)

    def accumulate(s, first, count):
        groups = slice(first, first + count)
        rows = res[s, groups].reshape(count * ROWS, 4 * BLK)
        for kind in range(2):
            term = nn(rows, kv_weights(s, kind)).reshape(count, ROWS, WID)
            acc[kind, groups] = term if s == 0 else acc[kind, groups] + term

    def fans(s, ring):
        fan(s, *ring, arrives=True).wait_recv()

    def send_hidden(s):
        @pl.when(off_diagonal)
        def _():
            hid_copy(s).start()

    all_rows, early, late, end = (0, NY), (0, 2), (2, 2), STEPS - 1
    for copy in wo_first[2:]:
        copy.wait_recv()
    pass_on(3, ring_wo)
    fans(0, ring_wo)
    ctx_copy(0, 2, 2, 1, y_b).wait_recv()
    project(0, *late, 0)
    pass_on(2, ring_kv)
    pass_on(4, ring_wo)
    ctx_copy(1, 1, 1, 2, y_a).wait_recv()
    ctx_copy(0, 0, 0, 4, y_b).wait_recv()
    ctx_copy(1, 0, 0, 5, y_a).wait_recv()
    project(0, *early, 1)
    send_hidden(2)
    fans(1, ring_wo)
    project(1, *all_rows, 2)
    pass_on(5, ring_wo)
    pass_on(3, ring_kv)
    exchange(0, *late, 0)
    exchange(0, *early, 1)
    send_hidden(3)
    pass_on(6, ring_wo)
    pass_on(4, ring_kv)
    fans(2, ring_wo)
    project(2, *all_rows, 3)
    pass_on(7, ring_wo)
    exchange(1, *all_rows, 2)
    pass_on(5, ring_kv)
    finish(0, *late, 0)
    finish(0, *early, 1)
    pass_on(8, ring_wo)
    fans(3, ring_wo)
    project(3, *early, 4)
    project(3, *late, 5)
    pass_on(6, ring_kv)
    for copy in kv_first[2:]:
        copy.wait_recv()
    fans(0, ring_kv)
    accumulate(0, *all_rows)
    exchange(2, *all_rows, 3)
    pass_on(7, ring_kv)
    finish(1, *all_rows, 2)
    fans(1, ring_kv)
    accumulate(1, *all_rows)
    exchange(3, *early, 4)
    exchange(3, *late, 5)
    pass_on(8, ring_kv)
    finish(2, *all_rows, 3)
    fans(2, ring_kv)
    accumulate(2, *all_rows)
    fans(3, ring_kv)

    y_copies = [remote(ys.at[i], yr.at[i], y_s, y_r.at[i], (y_a, y_b)[i % 2]) for i in range(6)]

    def y_send(i, value):
        ys[i] = value.astype(BF16)
        y_copies[i].start()

    def y_read(i):
        return yr[i].astype(F32)

    finish(end, *early, 4)
    accumulate(end, *early)
    y_send(0, acc[0, 0])
    y_send(1, acc[1, 0])
    y_send(2, acc[0, 1])
    finish(end, *late, 5)
    accumulate(end, *late)
    y_send(3, acc[1, 2])
    y_copies[1].wait_recv()
    y_send(4, acc[1, 1] + y_read(1))
    y_copies[0].wait_recv()
    y_send(5, acc[0, 2] + y_read(0))

    columns = jnp.sum(sums[...], axis=2, keepdims=True)
    squares = jnp.sum(jnp.where(diag[None], columns, 0.0), axis=1, keepdims=True)
    st[...] = jnp.broadcast_to(squares, (NY, 8, ROWS))
    stat_copies = [remote(st.at[r], str_.at[r], st_s, st_r.at[r], near[r]) for r in range(own)]
    for copy in stat_copies:
        copy.start()

    @pl.when(off_diagonal)
    def _():
        for s in range(STEPS):
            out_copy(s, 0).wait_recv()

    for s in range(STEPS):
        for half, cols in enumerate(sides(s)):
            for copy in range(2):
                at = slice(cols.start + copy * FEAT, cols.stop + copy * FEAT)
                out_w[:, at] = out_in[s, half].astype(F32)
    enc_out[...] = turned(out_w, (NZ - z) % NZ).astype(BF16)

    lower_half = rows_i < DROWS
    above_end = jnp.minimum(w + 2, NW)
    base = jnp.where(lower_half, start(ordered[1:2], dbound[w]), start(ordered[1:2], dbound[w + 1]))
    last = jnp.where(lower_half, dbound[w + 1].astype(F32), dbound[above_end].astype(F32))
    offset = (rows_i % DROWS).astype(F32)
    dec_col = tags(ends[1:2], base + offset, last)
    dec_allowed = (dec_col == enc_row) & (enc_row >= 0.0)

    for copy in stat_copies:
        copy.wait_recv()
    square = st[own] + str_[0] + str_[1] + str_[2]
    square_col = jnp.sum(jnp.where(diag, square[0:1], 0.0), axis=1, keepdims=True)
    norm = lax.rsqrt(square_col * (1.0 / (NY * FEAT)) + EPSILON)
    dq_copy.wait_recv()

    for i in (2, 3, 4, 5):
        y_copies[i].wait_recv()
    near_keys = ((acc[0, own] + y_read(2) + y_read(5)) * norm).astype(BF16)
    near_values = ((acc[1, own] + y_read(3) + y_read(4)) * norm).astype(BF16)

    def cross(rows, head):
        cols = slice(head * HEAD_DIM, (head + 1) * HEAD_DIM)
        return attend(dq2[rows, cols], near_keys[:, cols], near_values[:, cols], dec_allowed[rows])

    dres[...] = jnp.concatenate([cross(slice(DROWS, ROWS), head) for head in range(2)], axis=1)
    up = remote(dres, drecv, up_s, up_r, upper)
    up.start()
    cross_out[...] = jnp.concatenate([cross(slice(0, DROWS), head) for head in range(2)], axis=1)

    def left(sent, sem):
        remote(sent, sent, sem, up_r, sib).wait_send()

    left(wo.at[pl.ds(0, 14 * BLK + 3 * PIECE)], wo_s)
    left(kvw.at[pl.ds(0, 14)], kv_s)
    left(kvw.at[pl.ds(0, 3), 0], first_s)
    left(ctx.at[:, pl.ds(0, 3)], ctx_s)
    left(x1s, xs1)
    left(x2s, xs2)
    left(ys, y_s)
    left(st.at[pl.ds(0, 3)], st_s)
    dq_copy.wait_send()

    @pl.when(off_diagonal)
    def _():
        left(hid_c, hid_s)

    @pl.when(jnp.logical_not(off_diagonal))
    def _():
        left(out_c.at[pl.ds(0, 3)], out_s)

    up.wait()
    cross_out[...] = cross_out[...] + drecv[...]


def body(
    hidden_in, enc_query, enc_key, enc_value, dec_query, out_proj, key_proj, value_proj,
    norm_gain, enc_len, dec_len, example_order, enc_bounds, dec_bounds,
):
    vmem = pl.BlockSpec(memory_space=pltpu.VMEM)
    anywhere = pl.BlockSpec(memory_space=pl.ANY)
    dma = pltpu.SemaphoreType.DMA
    gain = norm_gain.reshape(32, 128)
    square = (ROWS, 128)
    return pl.pallas_call(
        kernel,
        out_shape=(
            jax.ShapeDtypeStruct((ROWS, FEAT), BF16),
            jax.ShapeDtypeStruct((DROWS, WID), BF16),
        ),
        in_specs=[anywhere] * 14,
        out_specs=(vmem, vmem),
        scratch_shapes=[
            pltpu.VMEM((ROWS, WID), BF16),
            pltpu.VMEM((ROWS, WID), BF16),
            pltpu.VMEM((ROWS, WID), BF16),
            pltpu.VMEM(gain.shape, F32),
            pltpu.VMEM((STEPS, 2, 8, 128), F32),
            pltpu.VMEM((3, 1, 256), jnp.int32),
            pltpu.SMEM(enc_bounds.shape, jnp.int32),
            pltpu.SMEM(dec_bounds.shape, jnp.int32),
            pltpu.VMEM((FEAT, WID), BF16),
            pltpu.VMEM((NZ, 2, BLK, WID), BF16),
            pltpu.VMEM((2, NY, ROWS, HEAD_DIM), BF16),
            pltpu.VMEM((ROWS, 2 * FEAT), BF16),
            pltpu.VMEM((STEPS, 2) + square, BF16),
            pltpu.VMEM((STEPS, NY, 2) + square, BF16),
            pltpu.VMEM((STEPS, 2, NY) + square, F32),
            pltpu.VMEM((STEPS, 2, NY) + square, BF16),
            pltpu.VMEM((STEPS, 2, NY) + square, BF16),
            pltpu.VMEM((STEPS, 2, NY) + square, BF16),
            pltpu.VMEM((STEPS, 2, NY) + square, BF16),
            pltpu.VMEM((STEPS, NY, ROWS, 4 * BLK), BF16),
            pltpu.VMEM((2, NY, ROWS, WID), F32),
            pltpu.VMEM((NY,) + square, F32),
            pltpu.VMEM((STEPS, NY, 2) + square, BF16),
            pltpu.VMEM((STEPS, 2) + square, BF16),
            pltpu.VMEM((ROWS, 2 * FEAT), F32),
            pltpu.VMEM((6, ROWS, WID), BF16),
            pltpu.VMEM((6, ROWS, WID), BF16),
            pltpu.VMEM((NY, 8, ROWS), F32),
            pltpu.VMEM((NY - 1, 8, ROWS), F32),
            pltpu.VMEM((2 * DROWS, WID), BF16),
            pltpu.VMEM((DROWS, WID), BF16),
            pltpu.VMEM((DROWS, WID), BF16),
            dma((15,)),
            dma, dma((6,)),
            dma, dma((HOPS,)), dma((STEPS,)),
            dma, dma((HOPS,)), dma((STEPS,)),
            dma, dma,
            dma, dma,
            dma, dma((STEPS, NY - 1)),
            dma, dma((STEPS,)),
            dma, dma((6,)),
            dma, dma((STEPS + 2, 2)),
            dma, dma((STEPS + 2, 2)),
            dma, dma((6,)),
            dma, dma((NY - 1,)),
        ],
        compiler_params=pltpu.CompilerParams(
            collective_id=0, has_side_effects=True, vmem_limit_bytes=VMEM_LIMIT
        ),
        name="encoder_to_cross",
    )(
        hidden_in, enc_query, enc_key, enc_value, dec_query, out_proj.T, key_proj, value_proj,
        gain, enc_len.reshape(1, 256), dec_len.reshape(1, 256),
        example_order.reshape(1, 256), enc_bounds, dec_bounds,
    )


def solution(mesh):
    return jax.shard_map(
        body,
        mesh=mesh,
        in_specs=(
            P("wide", "head"), P("wide", "head"), P("wide", "head"), P("wide", "head"),
            P("wide", "head"), P("head", "wide"), P("wide", "head"), P("wide", "head"),
            P(), P(), P(), P(), P(), P(),
        ),
        out_specs=(P("wide", "head"), P("wide", "head")),
        check_vma=False,
    )
```

```python
import jax
import jax.numpy as jnp
from jax import lax
from jax.experimental import pallas as pl
from jax.experimental.pallas import tpu as pltpu
from jax.sharding import PartitionSpec as P

MESH = pl.DeviceIdType.MESH
F32 = jnp.float32
BF16 = jnp.bfloat16

HEAD_DIM = 256
NZ = 16
NY = 4
NX = 4
NW = NY * NZ * 2
ROWS = 128
DROWS = 64
WID = 512
PIECE = 32
BLK = 2 * PIECE
FEAT = NZ * BLK
LANES = FEAT // 128
HOPS = NZ // 2
STEPS = NZ // 4
UNITS = STEPS * NY
GROUP = NY * ROWS
EPSILON = 1e-06
SCALE = 1.0 / 16.0
VMEM_LIMIT = 60 * 1024 * 1024


def nt(a, b):
    return lax.dot_general(a, b, (((1,), (1,)), ((), ())), preferred_element_type=F32)


def nn(a, b):
    return lax.dot_general(a, b, (((1,), (0,)), ((), ())), preferred_element_type=F32)


def iota(shape, dim):
    return lax.broadcasted_iota(jnp.int32, shape, dim)


def attend(q, k, v, allowed):
    scores = jnp.where(allowed, nt(q, k) * SCALE, -1e30)
    weights = jnp.where(allowed, jnp.exp(scores - jnp.max(scores, axis=1, keepdims=True)), 0.0)
    total = jnp.maximum(jnp.sum(weights, axis=1, keepdims=True), 1.0)
    return nn((weights / total).astype(BF16), v).astype(BF16)


def kernel(
    hidden, q_hbm, k_hbm, v_hbm, dq_hbm, wo_hbm, wk_hbm, wv_hbm, gain_hbm,
    elen_hbm, dlen_hbm, order_hbm, ebound_hbm, dbound_hbm,
    enc_out, cross_out,
    q_ref, k_ref, v_ref, gain_ref, gain_c, lens_ref, ebound, dbound,
    wo, kvw, ctx, hid, hid_c, hid_in, part, x1s, x1r, x2s, x2r, res, acc, sums, out_c, out_in, out_w,
    ys, yr, st, str_, dq2, dres, drecv,
    in_sem, first_s, first_r, wo_s, wo_r, wof_r, kv_s, kv_r, kvf_r,
    dq_s, dq_r, up_s, up_r, hid_s, hid_r, out_s, out_r, ctx_s, ctx_r, xs1, xr1, xs2, xr2,
    y_s, y_r, st_s, st_r,
):
    w = lax.axis_index("wide")
    x = lax.axis_index("head")
    c = w % 2
    z = (w // 2) % NZ
    y = w // (2 * NZ)
    step_dir = 1 - 2 * c

    def wide(yy, zz, cc):
        return (yy * NZ + zz) * 2 + cc

    sib = (w + step_dir, x)
    z_next = (wide(y, (z + step_dir + NZ) % NZ, c), x)
    z_prev = (wide(y, (z - step_dir + NZ) % NZ, c), x)
    ya, yb, y2 = y + 1 - 2 * (y % 2), NY - 1 - y, (y + 2) % NY
    y_a, y_b, y_2 = (wide(ya, z, c), x), (wide(yb, z, c), x), (wide(y2, z, c), x)
    x_a, x_b = (w, x + 1 - 2 * (x % 2)), (w, NX - 1 - x)
    upper, lower = ((w + 1) % NW, x), ((w + NW - 1) % NW, x)
    adder = (wide(x, z, c), x)
    off_diagonal = x != y
    near = (y_2, y_a, y_b)
    relation = jnp.where(ya == x, 1, jnp.where(yb == x, 2, 0))
    own = NY - 1
    cross = (wide(y, (z - step_dir + NZ) % NZ, 1 - c), x)
    greet = (sib, z_next, z_prev, cross, y_a, y_b, y_2, x_a, x_b, upper, lower)

    def remote(src, dst, ss, rs, dev):
        return pltpu.make_async_remote_copy(
            src_ref=src, dst_ref=dst, send_sem=ss, recv_sem=rs, device_id=dev, device_id_type=MESH
        )

    def cols_of(i, width):
        return pl.ds(pl.multiple_of(i * width, width), width)

    barrier = pltpu.get_barrier_semaphore()
    for dev in greet:
        pl.semaphore_signal(barrier, inc=1, device_id=dev, device_id_type=MESH)

    piece = cols_of(c, PIECE)
    mine = piece
    pairs = (
        (wk_hbm, kvw.at[0, 0, piece]), (wv_hbm, kvw.at[0, 1, piece]),
        (hidden, hid.at[:, pl.ds(0, FEAT)]), (hidden, hid.at[:, pl.ds(FEAT, FEAT)]), (wo_hbm, wo.at[mine]),
        (elen_hbm, lens_ref.at[0]), (dlen_hbm, lens_ref.at[1]), (order_hbm, lens_ref.at[2]),
        (ebound_hbm, ebound), (dbound_hbm, dbound),
        (q_hbm, q_ref), (k_hbm, k_ref), (v_hbm, v_ref),
        (gain_hbm, gain_ref), (dq_hbm, dq2.at[pl.ds(0, DROWS)]),
    )
    loads = [pltpu.make_async_copy(a, b, in_sem.at[i]) for i, (a, b) in enumerate(pairs)]
    for load in loads:
        load.start()

    pl.semaphore_wait(barrier, len(greet))

    def out_at(i):
        return jnp.where(c == 0, NZ - i, i)

    def in_at(i):
        return jnp.where(c == 0, i, NZ - i)

    def rows_at(i, offset, count):
        return pl.ds(pl.multiple_of(i * BLK + offset, PIECE), count)

    around = ((z_next, out_at(1)), (cross, in_at(1)), (sib, 0))
    wo_first = [
        remote(wo_hbm, wo.at[rows_at(to, c * PIECE, PIECE)], wo_s, first_r.at[i], dev)
        for i, (dev, to) in enumerate(around)
    ]
    kv_first = [
        remote(kvw.at[0, :, piece], kvw.at[to, :, piece], first_s, first_r.at[3 + i], dev)
        for i, (dev, to) in enumerate(around)
    ]
    for copy in wo_first:
        copy.start()
    for load in loads[:2]:
        load.wait()
    for copy in kv_first:
        copy.start()
    dq_copy = remote(dq_hbm, dq2.at[pl.ds(DROWS, DROWS)], dq_s, dq_r, lower)
    dq_copy.start()

    def turned(ref, by):
        wider = ref[:, pl.ds(pl.multiple_of((by // 2) * 128, 128), FEAT + 128)].astype(F32)
        return jnp.where(by % 2 == 1, wider[:, BLK : BLK + FEAT], wider[:, 0:FEAT])

    def sides(s):
        return slice(s * 128, (s + 1) * 128), slice((LANES - 1 - s) * 128, (LANES - s) * 128)

    def hid_copy(s):
        return remote(hid_c.at[s], hid_in.at[s, relation], hid_s, hid_r.at[s, relation], adder)

    def hid_got(s, r):
        return remote(hid_in.at[s, r], hid_in.at[s, r], hid_s, hid_r.at[s, r], adder)

    def out_copy(s, r):
        return remote(out_c.at[s, r], out_in.at[s], out_s, out_r.at[s], near[r])

    for load in loads[2:4]:
        load.wait()
    hid_turned = turned(hid, z)
    for s in range(STEPS):
        for half, cols in enumerate(sides(s)):
            hid_c[s, half] = hid_turned[:, cols].astype(BF16)

    @pl.when(off_diagonal)
    def _():
        hid_copy(0).start()
        hid_in[:, own] = jnp.zeros_like(hid_c)

    @pl.when(jnp.logical_not(off_diagonal))
    def _():
        hid_in[:, own] = hid_c[...]

    for load in loads[4:10]:
        load.wait()

    n = 256
    onehot = jnp.where(lens_ref[2] == iota((n, n), 0), 1.0, 0.0).astype(BF16)
    lens = jnp.concatenate([lens_ref[0], lens_ref[1], jnp.zeros((6, n), jnp.int32)], axis=0)
    ordered = nn(lens.astype(F32).astype(BF16), onehot)
    upto = jnp.where(iota((n, n), 0) <= iota((n, n), 1), 1.0, 0.0).astype(BF16)
    ends = nn(ordered.astype(BF16), upto)
    place = iota((1, n), 1)

    def start(row, first):
        return jnp.sum(jnp.where(place < first, row, 0.0), axis=1, keepdims=True)

    def tags(ends_row, offsets, last):
        pos = jnp.sum(jnp.where(ends_row <= offsets, 1.0, 0.0), axis=1, keepdims=True)
        return jnp.where(pos < last, pos, -1.0)

    rows_i = iota((ROWS, 1), 0)
    enc_base = start(ordered[0:1], ebound[w])
    enc_col = tags(ends[0:1], enc_base + rows_i.astype(F32), ebound[w + 1].astype(F32))
    diag = iota((ROWS, ROWS), 0) == iota((ROWS, ROWS), 1)
    enc_row = jnp.sum(jnp.where(diag, enc_col, 0.0), axis=0, keepdims=True)
    enc_allowed = (enc_col == enc_row) & (enc_row >= 0.0)

    def wo_blocks(i, count):
        return wo.at[rows_at(i, 0, count * BLK)]

    def kv_blocks(i, count):
        return kvw.at[pl.ds(i, count)]

    def hop(i, blocks, ss, rs, _):
        return remote(blocks(out_at(i - 1), 1), blocks(out_at(i), 1), ss, rs.at[i - 1], z_next)

    def fan(k, blocks, ss, _, rs, arrives=False):
        count = min(2, HOPS - 1 - 2 * k)
        low = NZ - 2 * k - count if count == 2 else NZ - 2 * k - 1
        start = jnp.where(c == (1 if arrives else 0), low, 2 * k + 1)
        at = blocks(start, count)
        return remote(at, at, ss, rs.at[k], sib)

    ring_wo = (wo_blocks, wo_s, wo_r, wof_r)
    ring_kv = (kv_blocks, kv_s, kv_r, kvf_r)

    def forward(i, ring):
        hop(i + 1, *ring).start()
        if i % 2 == 0 or i == HOPS - 1:
            fan((i - 1) // 2, *ring).start()

    def pass_on(i, ring):
        hop(i, *ring).wait_recv()
        if i < HOPS:
            forward(i, ring)

    def ctx_copy(head, src, dst, index, dev):
        return remote(ctx.at[head, src], ctx.at[head, dst], ctx_s, ctx_r.at[index], dev)

    for copy in wo_first[:2]:
        copy.wait_recv()
    forward(1, ring_wo)
    for copy in kv_first[:2]:
        copy.wait_recv()
    forward(1, ring_kv)
    for load in loads[10:]:
        load.wait()
    for head in range(2):
        cols = slice(head * HEAD_DIM, (head + 1) * HEAD_DIM)
        ctx[head, own] = attend(q_ref[:, cols], k_ref[:, cols], v_ref[:, cols], enc_allowed)
    ctx_first = [
        ctx_copy(0, own, 1, 0, y_a), ctx_copy(1, own, 2, 3, y_b),
        ctx_copy(1, own, 1, 2, y_a), ctx_copy(0, own, 2, 1, y_b),
    ]
    for copy in ctx_first:
        copy.start()
    pass_on(2, ring_wo)

    ctx_copy(0, 1, 1, 0, y_a).wait_recv()
    ctx_copy(0, 1, 0, 4, y_b).start()
    ctx_copy(1, 2, 2, 3, y_b).wait_recv()
    ctx_copy(1, 2, 0, 5, y_a).start()

    @pl.when(off_diagonal)
    def _():
        hid_copy(1).start()
        hid_in[:, 0:own] = jnp.zeros((STEPS, own, 2, ROWS, 128), BF16)

    for i in range(2 * LANES):
        row = gain_ref[pl.ds(y * LANES + i % LANES, 1), :]
        out_w[0:8, i * 128 : (i + 1) * 128] = jnp.broadcast_to(row, (8, 128))
    gain_turned = turned(out_w.at[pl.ds(0, 8)], z)
    for s in range(STEPS):
        for half, cols in enumerate(sides(s)):
            gain_c[s, half] = gain_turned[:, cols]
    sums[...] = jnp.zeros_like(sums)

    def round_one(s, first, count, index):
        return [
            remote(
                x1s.at[s, i, pl.ds(first, count)], x1r.at[s, i, pl.ds(first, count)],
                xs1, xr1.at[index, i], (x_a, x_b)[i],
            )
            for i in range(2)
        ]

    def round_two(s, first, count, index):
        return [
            remote(
                x2s.at[s, i, pl.ds(first, count)], x2r.at[s, i, pl.ds(first, count)],
                xs2, xr2.at[index, i], (x_b, x_a)[i],
            )
            for i in range(2)
        ]

    def project(s, first, count, index):
        @pl.when(jnp.logical_not(off_diagonal))
        def _():
            for r in range(first, min(first + count, own)):
                hid_got(s, r).wait_recv()

        groups = slice(first, first + count)
        weights = jnp.concatenate([wo[cols, :] for cols in sides(s)], axis=0)
        rows = [ctx[head, groups].reshape(count * ROWS, HEAD_DIM) for head in range(2)]
        term = nt(rows[0], weights[:, 0:HEAD_DIM]) + nt(rows[1], weights[:, HEAD_DIM:WID])
        for half in range(2):
            value = term[:, half * 128 : (half + 1) * 128].reshape(count, ROWS, 128)
            value = value + hid_in[s, groups, half].astype(F32)
            part[s, half, groups] = value
            x1s[s, half, groups] = value.astype(BF16)
        for copy in round_one(s, first, count, index):
            copy.start()

    def exchange(s, first, count, index):
        groups = slice(first, first + count)
        for half, copy in enumerate(round_one(s, first, count, index)):
            copy.wait_recv()
            total = part[s, half, groups] + x1r[s, half, groups].astype(F32)
            part[s, half, groups] = total
            x2s[s, half, groups] = total.astype(BF16)
            copy = round_two(s, first, count, index)[half]
            copy.start()

    def finish(s, first, count, index):
        groups = slice(first, first + count)
        for half, copy in enumerate(round_two(s, first, count, index)):
            copy.wait_recv()
            total = part[s, half, groups] + x2r[s, half, groups].astype(F32)
            sums[groups] += total * total
            res[s, groups, :, half * 128 : (half + 1) * 128] = (total * gain_c[s, half, 0:1, :]).astype(BF16)
            out_c[s, groups, half] = total.astype(BF16)

        @pl.when(jnp.logical_not(off_diagonal))
        def _():
            for r in range(first, min(first + count, own)):
                out_copy(s, r).start()
            if first + count > own:
                out_in[s] = out_c[s, own]

    def kv_weights(s, kind):
        quad = (2 * s, 2 * s + 1, NZ - 2 - 2 * s, NZ - 1 - 2 * s)
        return jnp.concatenate([kvw[i, kind] for i in quad], axis=0)

    def accumulate(s, first, count):
        groups = slice(first, first + count)
        rows = res[s, groups].reshape(count * ROWS, 4 * BLK)
        for kind in range(2):
            term = nn(rows, kv_weights(s, kind)).reshape(count, ROWS, WID)
            acc[kind, groups] = term if s == 0 else acc[kind, groups] + term

    def fans(s, ring):
        fan(s, *ring, arrives=True).wait_recv()

    def send_hidden(s):
        @pl.when(off_diagonal)
        def _():
            hid_copy(s).start()

    all_rows, early, late, end = (0, NY), (0, 2), (2, 2), STEPS - 1
    for copy in wo_first[2:] + kv_first[2:]:
        copy.wait_recv()
    pass_on(2, ring_kv)
    pass_on(3, ring_wo)
    fans(0, ring_wo)
    ctx_copy(0, 2, 2, 1, y_b).wait_recv()
    project(0, *late, 0)
    ctx_copy(1, 1, 1, 2, y_a).wait_recv()
    ctx_copy(0, 0, 0, 4, y_b).wait_recv()
    ctx_copy(1, 0, 0, 5, y_a).wait_recv()
    project(0, *early, 1)
    send_hidden(2)
    pass_on(3, ring_kv)
    pass_on(4, ring_wo)
    fans(1, ring_wo)
    project(1, *all_rows, 2)
    pass_on(5, ring_wo)
    pass_on(4, ring_kv)
    exchange(0, *late, 0)
    exchange(0, *early, 1)
    send_hidden(3)
    pass_on(6, ring_wo)
    fans(2, ring_wo)
    project(2, *all_rows, 3)
    pass_on(5, ring_kv)
    pass_on(7, ring_wo)
    exchange(1, *all_rows, 2)
    finish(0, *late, 0)
    finish(0, *early, 1)
    pass_on(8, ring_wo)
    pass_on(6, ring_kv)
    fans(3, ring_wo)
    project(3, *early, 4)
    project(3, *late, 5)
    exchange(2, *all_rows, 3)
    pass_on(7, ring_kv)
    finish(1, *all_rows, 2)
    fans(0, ring_kv)
    accumulate(0, *all_rows)
    exchange(3, *early, 4)
    exchange(3, *late, 5)
    pass_on(8, ring_kv)
    fans(1, ring_kv)
    accumulate(1, *all_rows)
    finish(2, *all_rows, 3)
    fans(2, ring_kv)
    accumulate(2, *all_rows)
    fans(3, ring_kv)

    y_copies = [remote(ys.at[i], yr.at[i], y_s, y_r.at[i], (y_a, y_b)[i % 2]) for i in range(6)]

    def y_send(i, value):
        ys[i] = value.astype(BF16)
        y_copies[i].start()

    def y_read(i):
        return yr[i].astype(F32)

    finish(end, *early, 4)
    accumulate(end, *early)
    y_send(0, acc[0, 0])
    y_send(1, acc[1, 0])
    y_send(2, acc[0, 1])
    finish(end, *late, 5)
    accumulate(end, *late)
    y_send(3, acc[1, 2])
    y_copies[1].wait_recv()
    y_send(4, acc[1, 1] + y_read(1))
    y_copies[0].wait_recv()
    y_send(5, acc[0, 2] + y_read(0))

    columns = jnp.sum(sums[...], axis=2, keepdims=True)
    squares = jnp.sum(jnp.where(diag[None], columns, 0.0), axis=1, keepdims=True)
    st[...] = jnp.broadcast_to(squares, (NY, 8, ROWS))
    stat_copies = [remote(st.at[r], str_.at[r], st_s, st_r.at[r], near[r]) for r in range(own)]
    for copy in stat_copies:
        copy.start()

    @pl.when(off_diagonal)
    def _():
        for s in range(STEPS):
            out_copy(s, 0).wait_recv()

    for s in range(STEPS):
        for half, cols in enumerate(sides(s)):
            for copy in range(2):
                at = slice(cols.start + copy * FEAT, cols.stop + copy * FEAT)
                out_w[:, at] = out_in[s, half].astype(F32)
    enc_out[...] = turned(out_w, (NZ - z) % NZ).astype(BF16)

    lower_half = rows_i < DROWS
    above_end = jnp.minimum(w + 2, NW)
    base = jnp.where(lower_half, start(ordered[1:2], dbound[w]), start(ordered[1:2], dbound[w + 1]))
    last = jnp.where(lower_half, dbound[w + 1].astype(F32), dbound[above_end].astype(F32))
    offset = (rows_i % DROWS).astype(F32)
    dec_col = tags(ends[1:2], base + offset, last)
    dec_allowed = (dec_col == enc_row) & (enc_row >= 0.0)

    for copy in stat_copies:
        copy.wait_recv()
    square = st[own] + str_[0] + str_[1] + str_[2]
    square_col = jnp.sum(jnp.where(diag, square[0:1], 0.0), axis=1, keepdims=True)
    norm = lax.rsqrt(square_col * (1.0 / (NY * FEAT)) + EPSILON)
    dq_copy.wait_recv()

    for i in (2, 3, 4, 5):
        y_copies[i].wait_recv()
    near_keys = ((acc[0, own] + y_read(2) + y_read(5)) * norm).astype(BF16)
    near_values = ((acc[1, own] + y_read(3) + y_read(4)) * norm).astype(BF16)

    def cross(rows, head):
        cols = slice(head * HEAD_DIM, (head + 1) * HEAD_DIM)
        return attend(dq2[rows, cols], near_keys[:, cols], near_values[:, cols], dec_allowed[rows])

    dres[...] = jnp.concatenate([cross(slice(DROWS, ROWS), head) for head in range(2)], axis=1)
    up = remote(dres, drecv, up_s, up_r, upper)
    up.start()
    cross_out[...] = jnp.concatenate([cross(slice(0, DROWS), head) for head in range(2)], axis=1)

    def left(sent, sem):
        remote(sent, sent, sem, up_r, sib).wait_send()

    left(wo.at[pl.ds(0, 14 * BLK + 3 * PIECE)], wo_s)
    left(kvw.at[pl.ds(0, 14)], kv_s)
    left(kvw.at[pl.ds(0, 3), 0], first_s)
    left(ctx.at[:, pl.ds(0, 3)], ctx_s)
    left(x1s, xs1)
    left(x2s, xs2)
    left(ys, y_s)
    left(st.at[pl.ds(0, 3)], st_s)
    dq_copy.wait_send()

    @pl.when(off_diagonal)
    def _():
        left(hid_c, hid_s)

    @pl.when(jnp.logical_not(off_diagonal))
    def _():
        left(out_c.at[pl.ds(0, 3)], out_s)

    up.wait()
    cross_out[...] = cross_out[...] + drecv[...]


def body(
    hidden_in, enc_query, enc_key, enc_value, dec_query, out_proj, key_proj, value_proj,
    norm_gain, enc_len, dec_len, example_order, enc_bounds, dec_bounds,
):
    vmem = pl.BlockSpec(memory_space=pltpu.VMEM)
    anywhere = pl.BlockSpec(memory_space=pl.ANY)
    dma = pltpu.SemaphoreType.DMA
    gain = norm_gain.reshape(32, 128)
    square = (ROWS, 128)
    return pl.pallas_call(
        kernel,
        out_shape=(
            jax.ShapeDtypeStruct((ROWS, FEAT), BF16),
            jax.ShapeDtypeStruct((DROWS, WID), BF16),
        ),
        in_specs=[anywhere] * 14,
        out_specs=(vmem, vmem),
        scratch_shapes=[
            pltpu.VMEM((ROWS, WID), BF16),
            pltpu.VMEM((ROWS, WID), BF16),
            pltpu.VMEM((ROWS, WID), BF16),
            pltpu.VMEM(gain.shape, F32),
            pltpu.VMEM((STEPS, 2, 8, 128), F32),
            pltpu.VMEM((3, 1, 256), jnp.int32),
            pltpu.SMEM(enc_bounds.shape, jnp.int32),
            pltpu.SMEM(dec_bounds.shape, jnp.int32),
            pltpu.VMEM((FEAT, WID), BF16),
            pltpu.VMEM((NZ, 2, BLK, WID), BF16),
            pltpu.VMEM((2, NY, ROWS, HEAD_DIM), BF16),
            pltpu.VMEM((ROWS, 2 * FEAT), BF16),
            pltpu.VMEM((STEPS, 2) + square, BF16),
            pltpu.VMEM((STEPS, NY, 2) + square, BF16),
            pltpu.VMEM((STEPS, 2, NY) + square, F32),
            pltpu.VMEM((STEPS, 2, NY) + square, BF16),
            pltpu.VMEM((STEPS, 2, NY) + square, BF16),
            pltpu.VMEM((STEPS, 2, NY) + square, BF16),
            pltpu.VMEM((STEPS, 2, NY) + square, BF16),
            pltpu.VMEM((STEPS, NY, ROWS, 4 * BLK), BF16),
            pltpu.VMEM((2, NY, ROWS, WID), F32),
            pltpu.VMEM((NY,) + square, F32),
            pltpu.VMEM((STEPS, NY, 2) + square, BF16),
            pltpu.VMEM((STEPS, 2) + square, BF16),
            pltpu.VMEM((ROWS, 2 * FEAT), F32),
            pltpu.VMEM((6, ROWS, WID), BF16),
            pltpu.VMEM((6, ROWS, WID), BF16),
            pltpu.VMEM((NY, 8, ROWS), F32),
            pltpu.VMEM((NY - 1, 8, ROWS), F32),
            pltpu.VMEM((2 * DROWS, WID), BF16),
            pltpu.VMEM((DROWS, WID), BF16),
            pltpu.VMEM((DROWS, WID), BF16),
            dma((15,)),
            dma, dma((6,)),
            dma, dma((HOPS,)), dma((STEPS,)),
            dma, dma((HOPS,)), dma((STEPS,)),
            dma, dma,
            dma, dma,
            dma, dma((STEPS, NY - 1)),
            dma, dma((STEPS,)),
            dma, dma((6,)),
            dma, dma((STEPS + 2, 2)),
            dma, dma((STEPS + 2, 2)),
            dma, dma((6,)),
            dma, dma((NY - 1,)),
        ],
        compiler_params=pltpu.CompilerParams(
            collective_id=0, has_side_effects=True, vmem_limit_bytes=VMEM_LIMIT
        ),
        name="encoder_to_cross",
    )(
        hidden_in, enc_query, enc_key, enc_value, dec_query, out_proj.T, key_proj, value_proj,
        gain, enc_len.reshape(1, 256), dec_len.reshape(1, 256),
        example_order.reshape(1, 256), enc_bounds, dec_bounds,
    )


def solution(mesh):
    return jax.shard_map(
        body,
        mesh=mesh,
        in_specs=(
            P("wide", "head"), P("wide", "head"), P("wide", "head"), P("wide", "head"),
            P("wide", "head"), P("head", "wide"), P("wide", "head"), P("wide", "head"),
            P(), P(), P(), P(), P(), P(),
        ),
        out_specs=(P("wide", "head"), P("wide", "head")),
        check_vma=False,
    )
```

```python
import jax
import jax.numpy as jnp
from jax import lax
from jax.experimental import pallas as pl
from jax.experimental.pallas import tpu as pltpu
from jax.sharding import PartitionSpec as P

MESH = pl.DeviceIdType.MESH
F32 = jnp.float32
BF16 = jnp.bfloat16

HEAD_DIM = 256
NZ = 16
NY = 4
NX = 4
NW = NY * NZ * 2
ROWS = 128
DROWS = 64
WID = 512
PIECE = 32
BLK = 2 * PIECE
FEAT = NZ * BLK
LANES = FEAT // 128
HOPS = NZ // 2
STEPS = NZ // 4
UNITS = STEPS * NY
GROUP = NY * ROWS
EPSILON = 1e-06
SCALE = 1.0 / 16.0
VMEM_LIMIT = 60 * 1024 * 1024


def nt(a, b):
    return lax.dot_general(a, b, (((1,), (1,)), ((), ())), preferred_element_type=F32)


def nn(a, b):
    return lax.dot_general(a, b, (((1,), (0,)), ((), ())), preferred_element_type=F32)


def iota(shape, dim):
    return lax.broadcasted_iota(jnp.int32, shape, dim)


def attend(q, k, v, allowed):
    scores = jnp.where(allowed, nt(q, k) * SCALE, -1e30)
    weights = jnp.where(allowed, jnp.exp(scores - jnp.max(scores, axis=1, keepdims=True)), 0.0)
    total = jnp.maximum(jnp.sum(weights, axis=1, keepdims=True), 1.0)
    return nn((weights / total).astype(BF16), v).astype(BF16)


def kernel(
    hidden, q_hbm, k_hbm, v_hbm, dq_hbm, wo_hbm, wk_hbm, wv_hbm, gain_hbm,
    elen_hbm, dlen_hbm, order_hbm, ebound_hbm, dbound_hbm,
    enc_out, cross_out,
    q_ref, k_ref, v_ref, gain_ref, gain_c, lens_ref, ebound, dbound,
    wo, kvw, ctx, hid, hid_c, hid_in, part, x1s, x1r, x2s, x2r, res, acc, sums, out_c, out_in, out_w, enc_c,
    ys, yr, st, str_, dq2, dres, drecv,
    in_sem, first_s, first_r, wo_s, wo_r, wof_r, kv_s, kv_r, kvf_r,
    dq_s, dq_r, up_s, up_r, hid_s, hid_r, out_s, out_r, ctx_s, ctx_r, xs1, xr1, xs2, xr2,
    y_s, y_r, st_s, st_r,
):
    w = lax.axis_index("wide")
    x = lax.axis_index("head")
    c = w % 2
    z = (w // 2) % NZ
    y = w // (2 * NZ)
    step_dir = 1 - 2 * c

    def wide(yy, zz, cc):
        return (yy * NZ + zz) * 2 + cc

    sib = (w + step_dir, x)
    z_next = (wide(y, (z + step_dir + NZ) % NZ, c), x)
    z_prev = (wide(y, (z - step_dir + NZ) % NZ, c), x)
    ya, yb, y2 = y + 1 - 2 * (y % 2), NY - 1 - y, (y + 2) % NY
    y_a, y_b, y_2 = (wide(ya, z, c), x), (wide(yb, z, c), x), (wide(y2, z, c), x)
    x_a, x_b = (w, x + 1 - 2 * (x % 2)), (w, NX - 1 - x)
    upper, lower = ((w + 1) % NW, x), ((w + NW - 1) % NW, x)
    adder = (wide(x, z, c), x)
    off_diagonal = x != y
    near = (y_2, y_a, y_b)
    relation = jnp.where(ya == x, 1, jnp.where(yb == x, 2, 0))
    own = NY - 1
    cross = (wide(y, (z - step_dir + NZ) % NZ, 1 - c), x)
    greet = (sib, z_next, z_prev, cross, y_a, y_b, y_2, x_a, x_b, upper, lower)

    def remote(src, dst, ss, rs, dev):
        return pltpu.make_async_remote_copy(
            src_ref=src, dst_ref=dst, send_sem=ss, recv_sem=rs, device_id=dev, device_id_type=MESH
        )

    def cols_of(i, width):
        return pl.ds(pl.multiple_of(i * width, width), width)

    barrier = pltpu.get_barrier_semaphore()
    for dev in greet:
        pl.semaphore_signal(barrier, inc=1, device_id=dev, device_id_type=MESH)

    piece = cols_of(c, PIECE)
    mine = piece
    pairs = (
        (wo_hbm, wo.at[mine]), (wk_hbm, kvw.at[0, 0, piece]), (wv_hbm, kvw.at[0, 1, piece]),
        (hidden, hid.at[:, pl.ds(0, FEAT)]), (hidden, hid.at[:, pl.ds(FEAT, FEAT)]),
        (elen_hbm, lens_ref.at[0]), (dlen_hbm, lens_ref.at[1]), (order_hbm, lens_ref.at[2]),
        (ebound_hbm, ebound), (dbound_hbm, dbound),
        (q_hbm, q_ref), (k_hbm, k_ref), (v_hbm, v_ref),
        (gain_hbm, gain_ref), (dq_hbm, dq2.at[pl.ds(0, DROWS)]),
    )
    loads = [pltpu.make_async_copy(a, b, in_sem.at[i]) for i, (a, b) in enumerate(pairs)]
    for load in loads:
        load.start()

    pl.semaphore_wait(barrier, len(greet))

    def out_at(i):
        return jnp.where(c == 0, NZ - i, i)

    def in_at(i):
        return jnp.where(c == 0, i, NZ - i)

    def rows_at(i, offset, count):
        return pl.ds(pl.multiple_of(i * BLK + offset, PIECE), count)

    around = ((z_next, out_at(1)), (cross, in_at(1)), (sib, 0))
    wo_first = [
        remote(wo.at[mine], wo.at[rows_at(to, c * PIECE, PIECE)], wo_s, first_r.at[i], dev)
        for i, (dev, to) in enumerate(around)
    ]
    kv_first = [
        remote(kvw.at[0, :, piece], kvw.at[to, :, piece], first_s, first_r.at[3 + i], dev)
        for i, (dev, to) in enumerate(around)
    ]
    loads[0].wait()
    for copy in wo_first:
        copy.start()
    for load in loads[1:3]:
        load.wait()
    for copy in kv_first:
        copy.start()
    dq_copy = remote(dq2.at[pl.ds(0, DROWS)], dq2.at[pl.ds(DROWS, DROWS)], dq_s, dq_r, lower)

    def turned(ref, by):
        wider = ref[:, pl.ds(pl.multiple_of((by // 2) * 128, 128), FEAT + 128)].astype(F32)
        return jnp.where(by % 2 == 1, wider[:, BLK : BLK + FEAT], wider[:, 0:FEAT])

    def sides(s):
        return slice(s * 128, (s + 1) * 128), slice((LANES - 1 - s) * 128, (LANES - s) * 128)

    def hid_copy(s):
        return remote(hid_c.at[s], hid_in.at[s, relation], hid_s, hid_r.at[s, relation], adder)

    def hid_got(s, r):
        return remote(hid_in.at[s, r], hid_in.at[s, r], hid_s, hid_r.at[s, r], adder)

    def out_copy(s, r):
        return remote(out_c.at[s, r], out_in.at[s], out_s, out_r.at[s], near[r])

    for load in loads[3:5]:
        load.wait()
    hid_turned = turned(hid, z)
    for s in range(STEPS):
        for half, cols in enumerate(sides(s)):
            hid_c[s, half] = hid_turned[:, cols].astype(BF16)

    @pl.when(off_diagonal)
    def _():
        hid_copy(0).start()
        hid_in[:, own] = jnp.zeros_like(hid_c)

    @pl.when(jnp.logical_not(off_diagonal))
    def _():
        hid_in[:, own] = hid_c[...]

    for load in loads[5:10]:
        load.wait()

    n = 256
    onehot = jnp.where(lens_ref[2] == iota((n, n), 0), 1.0, 0.0).astype(BF16)
    lens = jnp.concatenate([lens_ref[0], lens_ref[1], jnp.zeros((6, n), jnp.int32)], axis=0)
    ordered = nn(lens.astype(F32).astype(BF16), onehot)
    upto = jnp.where(iota((n, n), 0) <= iota((n, n), 1), 1.0, 0.0).astype(BF16)
    ends = nn(ordered.astype(BF16), upto)
    place = iota((1, n), 1)

    def start(row, first):
        return jnp.sum(jnp.where(place < first, row, 0.0), axis=1, keepdims=True)

    def tags(ends_row, offsets, last):
        pos = jnp.sum(jnp.where(ends_row <= offsets, 1.0, 0.0), axis=1, keepdims=True)
        return jnp.where(pos < last, pos, -1.0)

    rows_i = iota((ROWS, 1), 0)
    enc_base = start(ordered[0:1], ebound[w])
    enc_col = tags(ends[0:1], enc_base + rows_i.astype(F32), ebound[w + 1].astype(F32))
    diag = iota((ROWS, ROWS), 0) == iota((ROWS, ROWS), 1)
    enc_row = jnp.sum(jnp.where(diag, enc_col, 0.0), axis=0, keepdims=True)
    enc_allowed = (enc_col == enc_row) & (enc_row >= 0.0)

    def wo_blocks(i, count):
        return wo.at[rows_at(i, 0, count * BLK)]

    def kv_blocks(i, count):
        return kvw.at[pl.ds(i, count)]

    def hop(i, blocks, ss, rs, _):
        return remote(blocks(out_at(i - 1), 1), blocks(out_at(i), 1), ss, rs.at[i - 1], z_next)

    def fan(k, blocks, ss, _, rs, arrives=False):
        count = min(2, HOPS - 1 - 2 * k)
        low = NZ - 2 * k - count if count == 2 else NZ - 2 * k - 1
        start = jnp.where(c == (1 if arrives else 0), low, 2 * k + 1)
        at = blocks(start, count)
        return remote(at, at, ss, rs.at[k], sib)

    ring_wo = (wo_blocks, wo_s, wo_r, wof_r)
    ring_kv = (kv_blocks, kv_s, kv_r, kvf_r)

    def forward(i, ring):
        hop(i + 1, *ring).start()
        if i % 2 == 0 or i == HOPS - 1:
            fan((i - 1) // 2, *ring).start()

    def pass_on(i, ring):
        hop(i, *ring).wait_recv()
        if i < HOPS:
            forward(i, ring)

    def ctx_copy(head, src, dst, index, dev):
        return remote(ctx.at[head, src], ctx.at[head, dst], ctx_s, ctx_r.at[index], dev)

    for copy in wo_first[:2]:
        copy.wait_recv()
    forward(1, ring_wo)
    for copy in kv_first[:2]:
        copy.wait_recv()
    forward(1, ring_kv)
    for load in loads[10:]:
        load.wait()
    dq_copy.start()
    for head in range(2):
        cols = slice(head * HEAD_DIM, (head + 1) * HEAD_DIM)
        ctx[head, own] = attend(q_ref[:, cols], k_ref[:, cols], v_ref[:, cols], enc_allowed)
    ctx_first = [
        ctx_copy(0, own, 1, 0, y_a), ctx_copy(1, own, 2, 3, y_b),
        ctx_copy(1, own, 1, 2, y_a), ctx_copy(0, own, 2, 1, y_b),
    ]
    for copy in ctx_first:
        copy.start()
    pass_on(2, ring_wo)

    ctx_copy(0, 1, 1, 0, y_a).wait_recv()
    ctx_copy(0, 1, 0, 4, y_b).start()
    ctx_copy(1, 2, 2, 3, y_b).wait_recv()
    ctx_copy(1, 2, 0, 5, y_a).start()

    @pl.when(off_diagonal)
    def _():
        hid_copy(1).start()
        hid_in[:, 0:own] = jnp.zeros((STEPS, own, 2, ROWS, 128), BF16)

    for i in range(2 * LANES):
        row = gain_ref[pl.ds(y * LANES + i % LANES, 1), :]
        out_w[0:8, i * 128 : (i + 1) * 128] = jnp.broadcast_to(row, (8, 128))
    gain_turned = turned(out_w.at[pl.ds(0, 8)], z)
    for s in range(STEPS):
        for half, cols in enumerate(sides(s)):
            gain_c[s, half] = gain_turned[:, cols]
    sums[...] = jnp.zeros_like(sums)

    def round_one(s, first, count, index):
        return [
            remote(
                x1s.at[s, i, pl.ds(first, count)], x1r.at[s, i, pl.ds(first, count)],
                xs1, xr1.at[index, i], (x_a, x_b)[i],
            )
            for i in range(2)
        ]

    def round_two(s, first, count, index):
        return [
            remote(
                x2s.at[s, i, pl.ds(first, count)], x2r.at[s, i, pl.ds(first, count)],
                xs2, xr2.at[index, i], (x_b, x_a)[i],
            )
            for i in range(2)
        ]

    def project(s, first, count, index):
        @pl.when(jnp.logical_not(off_diagonal))
        def _():
            for r in range(first, min(first + count, own)):
                hid_got(s, r).wait_recv()

        groups = slice(first, first + count)
        weights = jnp.concatenate([wo[cols, :] for cols in sides(s)], axis=0)
        rows = [ctx[head, groups].reshape(count * ROWS, HEAD_DIM) for head in range(2)]
        term = nt(rows[0], weights[:, 0:HEAD_DIM]) + nt(rows[1], weights[:, HEAD_DIM:WID])
        for half in range(2):
            value = term[:, half * 128 : (half + 1) * 128].reshape(count, ROWS, 128)
            value = value + hid_in[s, groups, half].astype(F32)
            part[s, half, groups] = value
            x1s[s, half, groups] = value.astype(BF16)
        for copy in round_one(s, first, count, index):
            copy.start()

    def exchange(s, first, count, index):
        groups = slice(first, first + count)
        for half, copy in enumerate(round_one(s, first, count, index)):
            copy.wait_recv()
            total = part[s, half, groups] + x1r[s, half, groups].astype(F32)
            part[s, half, groups] = total
            x2s[s, half, groups] = total.astype(BF16)
            copy = round_two(s, first, count, index)[half]
            copy.start()

    def finish(s, first, count, index):
        groups = slice(first, first + count)
        for half, copy in enumerate(round_two(s, first, count, index)):
            copy.wait_recv()
            total = part[s, half, groups] + x2r[s, half, groups].astype(F32)
            sums[groups] += total * total
            res[s, groups, :, half * 128 : (half + 1) * 128] = (total * gain_c[s, half, 0:1, :]).astype(BF16)
            out_c[s, groups, half] = total.astype(BF16)

        @pl.when(jnp.logical_not(off_diagonal))
        def _():
            for r in range(first, min(first + count, own)):
                out_copy(s, r).start()
            if first + count > own:
                out_in[s] = out_c[s, own]

    def kv_weights(s, kind):
        quad = (2 * s, 2 * s + 1, NZ - 2 - 2 * s, NZ - 1 - 2 * s)
        return jnp.concatenate([kvw[i, kind] for i in quad], axis=0)

    def accumulate(s, first, count):
        groups = slice(first, first + count)
        rows = res[s, groups].reshape(count * ROWS, 4 * BLK)
        for kind in range(2):
            term = nn(rows, kv_weights(s, kind)).reshape(count, ROWS, WID)
            acc[kind, groups] = term if s == 0 else acc[kind, groups] + term

    def fans(s, ring):
        fan(s, *ring, arrives=True).wait_recv()

    def send_hidden(s):
        @pl.when(off_diagonal)
        def _():
            hid_copy(s).start()

    all_rows, early, late, end = (0, NY), (0, 2), (2, 2), STEPS - 1
    for copy in wo_first[2:] + kv_first[2:]:
        copy.wait_recv()
    pass_on(2, ring_kv)
    pass_on(3, ring_wo)
    fans(0, ring_wo)
    ctx_copy(0, 2, 2, 1, y_b).wait_recv()
    project(0, *late, 0)
    ctx_copy(1, 1, 1, 2, y_a).wait_recv()
    ctx_copy(0, 0, 0, 4, y_b).wait_recv()
    ctx_copy(1, 0, 0, 5, y_a).wait_recv()
    project(0, *early, 1)
    send_hidden(2)
    pass_on(3, ring_kv)
    pass_on(4, ring_wo)
    fans(1, ring_wo)
    project(1, *all_rows, 2)
    pass_on(5, ring_wo)
    pass_on(4, ring_kv)
    exchange(0, *late, 0)
    exchange(0, *early, 1)
    send_hidden(3)
    pass_on(6, ring_wo)
    fans(2, ring_wo)
    project(2, *all_rows, 3)
    pass_on(5, ring_kv)
    pass_on(7, ring_wo)
    exchange(1, *all_rows, 2)
    finish(0, *late, 0)
    finish(0, *early, 1)
    pass_on(8, ring_wo)
    pass_on(6, ring_kv)
    fans(3, ring_wo)
    project(3, *early, 4)
    project(3, *late, 5)
    exchange(2, *all_rows, 3)
    pass_on(7, ring_kv)
    finish(1, *all_rows, 2)
    fans(0, ring_kv)
    accumulate(0, *all_rows)
    exchange(3, *early, 4)
    exchange(3, *late, 5)
    pass_on(8, ring_kv)
    fans(1, ring_kv)
    accumulate(1, *early)
    finish(2, *all_rows, 3)
    fans(2, ring_kv)
    accumulate(2, *early)
    fans(3, ring_kv)

    y_copies = [remote(ys.at[i], yr.at[i], y_s, y_r.at[i], (y_a, y_b)[i % 2]) for i in range(6)]

    def y_send(i, value):
        ys[i] = value.astype(BF16)
        y_copies[i].start()

    def y_read(i):
        return yr[i].astype(F32)

    finish(end, *early, 4)
    accumulate(end, *early)
    y_send(0, acc[0, 0])
    y_send(1, acc[1, 0])
    y_send(2, acc[0, 1])
    accumulate(1, *late)
    accumulate(2, *late)
    finish(end, *late, 5)
    accumulate(end, *late)
    y_send(3, acc[1, 2])
    y_copies[1].wait_recv()
    y_send(4, acc[1, 1] + y_read(1))
    y_copies[0].wait_recv()
    y_send(5, acc[0, 2] + y_read(0))

    columns = jnp.sum(sums[...], axis=2, keepdims=True)
    squares = jnp.sum(jnp.where(diag[None], columns, 0.0), axis=1, keepdims=True)
    st[...] = jnp.broadcast_to(squares, (NY, 8, ROWS))
    stat_copies = [remote(st.at[r], str_.at[r], st_s, st_r.at[r], near[r]) for r in range(own)]
    for copy in stat_copies:
        copy.start()

    @pl.when(off_diagonal)
    def _():
        for s in range(STEPS):
            out_copy(s, 0).wait_recv()

    for s in range(STEPS):
        for half, cols in enumerate(sides(s)):
            for copy in range(2):
                at = slice(cols.start + copy * FEAT, cols.stop + copy * FEAT)
                out_w[:, at] = out_in[s, half].astype(F32)
    enc_c[...] = turned(out_w, (NZ - z) % NZ).astype(BF16)
    enc_copy = pltpu.make_async_copy(enc_c, enc_out, in_sem.at[0])
    enc_copy.start()

    lower_half = rows_i < DROWS
    above_end = jnp.minimum(w + 2, NW)
    base = jnp.where(lower_half, start(ordered[1:2], dbound[w]), start(ordered[1:2], dbound[w + 1]))
    last = jnp.where(lower_half, dbound[w + 1].astype(F32), dbound[above_end].astype(F32))
    offset = (rows_i % DROWS).astype(F32)
    dec_col = tags(ends[1:2], base + offset, last)
    dec_allowed = (dec_col == enc_row) & (enc_row >= 0.0)

    for copy in stat_copies:
        copy.wait_recv()
    square = st[own] + str_[0] + str_[1] + str_[2]
    square_col = jnp.sum(jnp.where(diag, square[0:1], 0.0), axis=1, keepdims=True)
    norm = lax.rsqrt(square_col * (1.0 / (NY * FEAT)) + EPSILON)
    dq_copy.wait_recv()

    for i in (2, 3, 4, 5):
        y_copies[i].wait_recv()
    near_keys = ((acc[0, own] + y_read(2) + y_read(5)) * norm).astype(BF16)
    near_values = ((acc[1, own] + y_read(3) + y_read(4)) * norm).astype(BF16)

    def cross(rows, head):
        cols = slice(head * HEAD_DIM, (head + 1) * HEAD_DIM)
        return attend(dq2[rows, cols], near_keys[:, cols], near_values[:, cols], dec_allowed[rows])

    dres[...] = jnp.concatenate([cross(slice(DROWS, ROWS), head) for head in range(2)], axis=1)
    up = remote(dres, drecv, up_s, up_r, upper)
    up.start()
    cross_out[...] = jnp.concatenate([cross(slice(0, DROWS), head) for head in range(2)], axis=1)

    def left(sent, sem):
        remote(sent, sent, sem, up_r, sib).wait_send()

    left(wo.at[pl.ds(0, 14 * BLK + 3 * PIECE)], wo_s)
    left(kvw.at[pl.ds(0, 14)], kv_s)
    left(kvw.at[pl.ds(0, 3), 0], first_s)
    left(ctx.at[:, pl.ds(0, 3)], ctx_s)
    left(x1s, xs1)
    left(x2s, xs2)
    left(ys, y_s)
    left(st.at[pl.ds(0, 3)], st_s)
    dq_copy.wait_send()

    @pl.when(off_diagonal)
    def _():
        left(hid_c, hid_s)

    @pl.when(jnp.logical_not(off_diagonal))
    def _():
        left(out_c.at[pl.ds(0, 3)], out_s)

    enc_copy.wait()
    up.wait()
    cross_out[...] = cross_out[...] + drecv[...]


def body(
    hidden_in, enc_query, enc_key, enc_value, dec_query, out_proj, key_proj, value_proj,
    norm_gain, enc_len, dec_len, example_order, enc_bounds, dec_bounds,
):
    vmem = pl.BlockSpec(memory_space=pltpu.VMEM)
    anywhere = pl.BlockSpec(memory_space=pl.ANY)
    dma = pltpu.SemaphoreType.DMA
    gain = norm_gain.reshape(32, 128)
    square = (ROWS, 128)
    return pl.pallas_call(
        kernel,
        out_shape=(
            jax.ShapeDtypeStruct((ROWS, FEAT), BF16),
            jax.ShapeDtypeStruct((DROWS, WID), BF16),
        ),
        in_specs=[anywhere] * 14,
        out_specs=(anywhere, vmem),
        scratch_shapes=[
            pltpu.VMEM((ROWS, WID), BF16),
            pltpu.VMEM((ROWS, WID), BF16),
            pltpu.VMEM((ROWS, WID), BF16),
            pltpu.VMEM(gain.shape, F32),
            pltpu.VMEM((STEPS, 2, 8, 128), F32),
            pltpu.VMEM((3, 1, 256), jnp.int32),
            pltpu.SMEM(enc_bounds.shape, jnp.int32),
            pltpu.SMEM(dec_bounds.shape, jnp.int32),
            pltpu.VMEM((FEAT, WID), BF16),
            pltpu.VMEM((NZ, 2, BLK, WID), BF16),
            pltpu.VMEM((2, NY, ROWS, HEAD_DIM), BF16),
            pltpu.VMEM((ROWS, 2 * FEAT), BF16),
            pltpu.VMEM((STEPS, 2) + square, BF16),
            pltpu.VMEM((STEPS, NY, 2) + square, BF16),
            pltpu.VMEM((STEPS, 2, NY) + square, F32),
            pltpu.VMEM((STEPS, 2, NY) + square, BF16),
            pltpu.VMEM((STEPS, 2, NY) + square, BF16),
            pltpu.VMEM((STEPS, 2, NY) + square, BF16),
            pltpu.VMEM((STEPS, 2, NY) + square, BF16),
            pltpu.VMEM((STEPS, NY, ROWS, 4 * BLK), BF16),
            pltpu.VMEM((2, NY, ROWS, WID), F32),
            pltpu.VMEM((NY,) + square, F32),
            pltpu.VMEM((STEPS, NY, 2) + square, BF16),
            pltpu.VMEM((STEPS, 2) + square, BF16),
            pltpu.VMEM((ROWS, 2 * FEAT), F32),
            pltpu.VMEM((ROWS, FEAT), BF16),
            pltpu.VMEM((6, ROWS, WID), BF16),
            pltpu.VMEM((6, ROWS, WID), BF16),
            pltpu.VMEM((NY, 8, ROWS), F32),
            pltpu.VMEM((NY - 1, 8, ROWS), F32),
            pltpu.VMEM((2 * DROWS, WID), BF16),
            pltpu.VMEM((DROWS, WID), BF16),
            pltpu.VMEM((DROWS, WID), BF16),
            dma((15,)),
            dma, dma((6,)),
            dma, dma((HOPS,)), dma((STEPS,)),
            dma, dma((HOPS,)), dma((STEPS,)),
            dma, dma,
            dma, dma,
            dma, dma((STEPS, NY - 1)),
            dma, dma((STEPS,)),
            dma, dma((6,)),
            dma, dma((STEPS + 2, 2)),
            dma, dma((STEPS + 2, 2)),
            dma, dma((6,)),
            dma, dma((NY - 1,)),
        ],
        compiler_params=pltpu.CompilerParams(
            collective_id=0, has_side_effects=True, vmem_limit_bytes=VMEM_LIMIT
        ),
        name="encoder_to_cross",
    )(
        hidden_in, enc_query, enc_key, enc_value, dec_query, out_proj.T, key_proj, value_proj,
        gain, enc_len.reshape(1, 256), dec_len.reshape(1, 256),
        example_order.reshape(1, 256), enc_bounds, dec_bounds,
    )


def solution(mesh):
    return jax.shard_map(
        body,
        mesh=mesh,
        in_specs=(
            P("wide", "head"), P("wide", "head"), P("wide", "head"), P("wide", "head"),
            P("wide", "head"), P("head", "wide"), P("wide", "head"), P("wide", "head"),
            P(), P(), P(), P(), P(), P(),
        ),
        out_specs=(P("wide", "head"), P("wide", "head")),
        check_vma=False,
    )
```

```python
import jax
import jax.numpy as jnp
from jax import lax
from jax.experimental import pallas as pl
from jax.experimental.pallas import tpu as pltpu
from jax.sharding import PartitionSpec as P

MESH = pl.DeviceIdType.MESH
F32 = jnp.float32
BF16 = jnp.bfloat16

HEAD_DIM = 256
NZ = 16
NY = 4
NX = 4
NW = NY * NZ * 2
ROWS = 128
DROWS = 64
WID = 512
PIECE = 32
BLK = 2 * PIECE
FEAT = NZ * BLK
LANES = FEAT // 128
HOPS = NZ // 2
STEPS = NZ // 4
UNITS = STEPS * NY
GROUP = NY * ROWS
EPSILON = 1e-06
SCALE = 1.0 / 16.0
VMEM_LIMIT = 60 * 1024 * 1024


def nt(a, b):
    return lax.dot_general(a, b, (((1,), (1,)), ((), ())), preferred_element_type=F32)


def nn(a, b):
    return lax.dot_general(a, b, (((1,), (0,)), ((), ())), preferred_element_type=F32)


def iota(shape, dim):
    return lax.broadcasted_iota(jnp.int32, shape, dim)


def attend(q, k, v, allowed):
    scores = jnp.where(allowed, nt(q, k) * SCALE, -1e30)
    weights = jnp.where(allowed, jnp.exp(scores - jnp.max(scores, axis=1, keepdims=True)), 0.0)
    total = jnp.maximum(jnp.sum(weights, axis=1, keepdims=True), 1.0)
    return nn((weights / total).astype(BF16), v).astype(BF16)


def kernel(
    hidden, q_hbm, k_hbm, v_hbm, dq_hbm, wo_hbm, wk_hbm, wv_hbm, gain_hbm,
    elen_hbm, dlen_hbm, order_hbm, ebound_hbm, dbound_hbm,
    enc_out, cross_out,
    q_ref, k_ref, v_ref, gain_ref, gain_c, lens_ref, ebound, dbound,
    wo, kvw, ctx, hid, hid_c, hid_in, part, x1s, x1r, x2s, x2r, res, acc, sums, out_c, out_in, out_w, enc_c,
    ys, yr, st, str_, dq2, dres, drecv,
    in_sem, first_s, first_r, wo_s, wo_r, wof_r, kv_s, kv_r, kvf_r,
    dq_s, dq_r, up_s, up_r, hid_s, hid_r, out_s, out_r, ctx_s, ctx_r, xs1, xr1, xs2, xr2,
    y_s, y_r, st_s, st_r,
):
    w = lax.axis_index("wide")
    x = lax.axis_index("head")
    c = w % 2
    z = (w // 2) % NZ
    y = w // (2 * NZ)
    step_dir = 1 - 2 * c

    def wide(yy, zz, cc):
        return (yy * NZ + zz) * 2 + cc

    sib = (w + step_dir, x)
    z_next = (wide(y, (z + step_dir + NZ) % NZ, c), x)
    z_prev = (wide(y, (z - step_dir + NZ) % NZ, c), x)
    ya, yb, y2 = y + 1 - 2 * (y % 2), NY - 1 - y, (y + 2) % NY
    y_a, y_b, y_2 = (wide(ya, z, c), x), (wide(yb, z, c), x), (wide(y2, z, c), x)
    x_a, x_b = (w, x + 1 - 2 * (x % 2)), (w, NX - 1 - x)
    upper, lower = ((w + 1) % NW, x), ((w + NW - 1) % NW, x)
    adder = (wide(x, z, c), x)
    off_diagonal = x != y
    near = (y_2, y_a, y_b)
    relation = jnp.where(ya == x, 1, jnp.where(yb == x, 2, 0))
    own = NY - 1
    cross = (wide(y, (z - step_dir + NZ) % NZ, 1 - c), x)
    greet = (sib, z_next, z_prev, cross, y_a, y_b, y_2, x_a, x_b, upper, lower)

    def remote(src, dst, ss, rs, dev):
        return pltpu.make_async_remote_copy(
            src_ref=src, dst_ref=dst, send_sem=ss, recv_sem=rs, device_id=dev, device_id_type=MESH
        )

    def cols_of(i, width):
        return pl.ds(pl.multiple_of(i * width, width), width)

    barrier = pltpu.get_barrier_semaphore()
    for dev in greet:
        pl.semaphore_signal(barrier, inc=1, device_id=dev, device_id_type=MESH)

    piece = cols_of(c, PIECE)
    mine = piece
    pairs = (
        (wo_hbm, wo.at[mine]), (wk_hbm, kvw.at[0, 0, piece]), (wv_hbm, kvw.at[0, 1, piece]),
        (hidden, hid.at[:, pl.ds(0, FEAT)]), (hidden, hid.at[:, pl.ds(FEAT, FEAT)]),
        (elen_hbm, lens_ref.at[0]), (dlen_hbm, lens_ref.at[1]), (order_hbm, lens_ref.at[2]),
        (ebound_hbm, ebound), (dbound_hbm, dbound),
        (q_hbm, q_ref), (k_hbm, k_ref), (v_hbm, v_ref),
        (gain_hbm, gain_ref), (dq_hbm, dq2.at[pl.ds(0, DROWS)]),
    )
    loads = [pltpu.make_async_copy(a, b, in_sem.at[i]) for i, (a, b) in enumerate(pairs)]
    for load in loads:
        load.start()

    pl.semaphore_wait(barrier, len(greet))

    def out_at(i):
        return jnp.where(c == 0, NZ - i, i)

    def in_at(i):
        return jnp.where(c == 0, i, NZ - i)

    def rows_at(i, offset, count):
        return pl.ds(pl.multiple_of(i * BLK + offset, PIECE), count)

    around = ((z_next, out_at(1)), (cross, in_at(1)), (sib, 0))
    wo_first = [
        remote(wo.at[mine], wo.at[rows_at(to, c * PIECE, PIECE)], wo_s, first_r.at[i], dev)
        for i, (dev, to) in enumerate(around)
    ]
    kv_first = [
        remote(kvw.at[0, :, piece], kvw.at[to, :, piece], first_s, first_r.at[3 + i], dev)
        for i, (dev, to) in enumerate(around)
    ]
    loads[0].wait()
    for copy in wo_first:
        copy.start()
    for load in loads[1:3]:
        load.wait()
    for copy in kv_first:
        copy.start()
    dq_copy = remote(dq2.at[pl.ds(0, DROWS)], dq2.at[pl.ds(DROWS, DROWS)], dq_s, dq_r, lower)

    def turned(ref, by):
        wider = ref[:, pl.ds(pl.multiple_of((by // 2) * 128, 128), FEAT + 128)].astype(F32)
        return jnp.where(by % 2 == 1, wider[:, BLK : BLK + FEAT], wider[:, 0:FEAT])

    def sides(s):
        return slice(s * 128, (s + 1) * 128), slice((LANES - 1 - s) * 128, (LANES - s) * 128)

    def hid_copy(s):
        return remote(hid_c.at[s], hid_in.at[s, relation], hid_s, hid_r.at[s, relation], adder)

    def hid_got(s, r):
        return remote(hid_in.at[s, r], hid_in.at[s, r], hid_s, hid_r.at[s, r], adder)

    def out_copy(s, r):
        return remote(out_c.at[s, r], out_in.at[s], out_s, out_r.at[s], near[r])

    for load in loads[3:5]:
        load.wait()
    hid_turned = turned(hid, z)
    for s in range(STEPS):
        for half, cols in enumerate(sides(s)):
            hid_c[s, half] = hid_turned[:, cols].astype(BF16)

    @pl.when(off_diagonal)
    def _():
        hid_copy(0).start()
        hid_in[:, own] = jnp.zeros_like(hid_c)

    @pl.when(jnp.logical_not(off_diagonal))
    def _():
        hid_in[:, own] = hid_c[...]

    for load in loads[5:10]:
        load.wait()

    n = 256
    onehot = jnp.where(lens_ref[2] == iota((n, n), 0), 1.0, 0.0).astype(BF16)
    lens = jnp.concatenate([lens_ref[0], lens_ref[1], jnp.zeros((6, n), jnp.int32)], axis=0)
    ordered = nn(lens.astype(F32).astype(BF16), onehot)
    upto = jnp.where(iota((n, n), 0) <= iota((n, n), 1), 1.0, 0.0).astype(BF16)
    ends = nn(ordered.astype(BF16), upto)
    place = iota((1, n), 1)

    def start(row, first):
        return jnp.sum(jnp.where(place < first, row, 0.0), axis=1, keepdims=True)

    def tags(ends_row, offsets, last):
        pos = jnp.sum(jnp.where(ends_row <= offsets, 1.0, 0.0), axis=1, keepdims=True)
        return jnp.where(pos < last, pos, -1.0)

    rows_i = iota((ROWS, 1), 0)
    enc_base = start(ordered[0:1], ebound[w])
    enc_col = tags(ends[0:1], enc_base + rows_i.astype(F32), ebound[w + 1].astype(F32))
    diag = iota((ROWS, ROWS), 0) == iota((ROWS, ROWS), 1)
    enc_row = jnp.sum(jnp.where(diag, enc_col, 0.0), axis=0, keepdims=True)
    enc_allowed = (enc_col == enc_row) & (enc_row >= 0.0)

    def wo_blocks(i, count):
        return wo.at[rows_at(i, 0, count * BLK)]

    def kv_blocks(i, count):
        return kvw.at[pl.ds(i, count)]

    def hop(i, blocks, ss, rs, _):
        return remote(blocks(out_at(i - 1), 1), blocks(out_at(i), 1), ss, rs.at[i - 1], z_next)

    def fan(k, blocks, ss, _, rs, arrives=False):
        count = min(2, HOPS - 1 - 2 * k)
        low = NZ - 2 * k - count if count == 2 else NZ - 2 * k - 1
        start = jnp.where(c == (1 if arrives else 0), low, 2 * k + 1)
        at = blocks(start, count)
        return remote(at, at, ss, rs.at[k], sib)

    ring_wo = (wo_blocks, wo_s, wo_r, wof_r)
    ring_kv = (kv_blocks, kv_s, kv_r, kvf_r)

    def forward(i, ring):
        hop(i + 1, *ring).start()
        if i % 2 == 0 or i == HOPS - 1:
            fan((i - 1) // 2, *ring).start()

    def pass_on(i, ring):
        hop(i, *ring).wait_recv()
        if i < HOPS:
            forward(i, ring)

    def ctx_copy(head, src, dst, index, dev):
        return remote(ctx.at[head, src], ctx.at[head, dst], ctx_s, ctx_r.at[index], dev)

    for copy in wo_first[:2]:
        copy.wait_recv()
    forward(1, ring_wo)
    for copy in kv_first[:2]:
        copy.wait_recv()
    forward(1, ring_kv)
    for load in loads[10:]:
        load.wait()
    dq_copy.start()
    for head in range(2):
        cols = slice(head * HEAD_DIM, (head + 1) * HEAD_DIM)
        ctx[head, own] = attend(q_ref[:, cols], k_ref[:, cols], v_ref[:, cols], enc_allowed)
    ctx_first = [
        ctx_copy(0, own, 1, 0, y_a), ctx_copy(1, own, 2, 3, y_b),
        ctx_copy(1, own, 1, 2, y_a), ctx_copy(0, own, 2, 1, y_b),
    ]
    for copy in ctx_first:
        copy.start()
    pass_on(2, ring_wo)

    ctx_copy(0, 1, 1, 0, y_a).wait_recv()
    ctx_copy(0, 1, 0, 4, y_b).start()
    ctx_copy(1, 2, 2, 3, y_b).wait_recv()
    ctx_copy(1, 2, 0, 5, y_a).start()

    @pl.when(off_diagonal)
    def _():
        hid_copy(1).start()
        hid_in[:, 0:own] = jnp.zeros((STEPS, own, 2, ROWS, 128), BF16)

    for i in range(2 * LANES):
        row = gain_ref[pl.ds(y * LANES + i % LANES, 1), :]
        out_w[0:8, i * 128 : (i + 1) * 128] = jnp.broadcast_to(row, (8, 128))
    gain_turned = turned(out_w.at[pl.ds(0, 8)], z)
    for s in range(STEPS):
        for half, cols in enumerate(sides(s)):
            gain_c[s, half] = gain_turned[:, cols]
    sums[...] = jnp.zeros_like(sums)

    def round_one(s, first, count, index):
        return [
            remote(
                x1s.at[s, i, pl.ds(first, count)], x1r.at[s, i, pl.ds(first, count)],
                xs1, xr1.at[index, i], (x_a, x_b)[i],
            )
            for i in range(2)
        ]

    def round_two(s, first, count, index):
        return [
            remote(
                x2s.at[s, i, pl.ds(first, count)], x2r.at[s, i, pl.ds(first, count)],
                xs2, xr2.at[index, i], (x_b, x_a)[i],
            )
            for i in range(2)
        ]

    def project(s, first, count, index):
        @pl.when(jnp.logical_not(off_diagonal))
        def _():
            for r in range(first, min(first + count, own)):
                hid_got(s, r).wait_recv()

        groups = slice(first, first + count)
        weights = jnp.concatenate([wo[cols, :] for cols in sides(s)], axis=0)
        rows = [ctx[head, groups].reshape(count * ROWS, HEAD_DIM) for head in range(2)]
        term = nt(rows[0], weights[:, 0:HEAD_DIM]) + nt(rows[1], weights[:, HEAD_DIM:WID])
        for half in range(2):
            value = term[:, half * 128 : (half + 1) * 128].reshape(count, ROWS, 128)
            value = value + hid_in[s, groups, half].astype(F32)
            part[s, half, groups] = value
            x1s[s, half, groups] = value.astype(BF16)
        for copy in round_one(s, first, count, index):
            copy.start()

    def exchange(s, first, count, index):
        groups = slice(first, first + count)
        for half, copy in enumerate(round_one(s, first, count, index)):
            copy.wait_recv()
            total = part[s, half, groups] + x1r[s, half, groups].astype(F32)
            part[s, half, groups] = total
            x2s[s, half, groups] = total.astype(BF16)
            copy = round_two(s, first, count, index)[half]
            copy.start()

    def finish(s, first, count, index):
        groups = slice(first, first + count)
        for half, copy in enumerate(round_two(s, first, count, index)):
            copy.wait_recv()
            total = part[s, half, groups] + x2r[s, half, groups].astype(F32)
            sums[groups] += total * total
            res[s, groups, :, half * 128 : (half + 1) * 128] = (total * gain_c[s, half, 0:1, :]).astype(BF16)
            out_c[s, groups, half] = total.astype(BF16)

        @pl.when(jnp.logical_not(off_diagonal))
        def _():
            for r in range(first, min(first + count, own)):
                out_copy(s, r).start()
            if first + count > own:
                out_in[s] = out_c[s, own]

    def kv_weights(s, kind):
        quad = (2 * s, 2 * s + 1, NZ - 2 - 2 * s, NZ - 1 - 2 * s)
        return jnp.concatenate([kvw[i, kind] for i in quad], axis=0)

    def accumulate(s, first, count):
        groups = slice(first, first + count)
        rows = res[s, groups].reshape(count * ROWS, 4 * BLK)
        for kind in range(2):
            term = nn(rows, kv_weights(s, kind)).reshape(count, ROWS, WID)
            acc[kind, groups] = term if s == 0 else acc[kind, groups] + term

    def fans(s, ring):
        fan(s, *ring, arrives=True).wait_recv()

    def send_hidden(s):
        @pl.when(off_diagonal)
        def _():
            hid_copy(s).start()

    all_rows, early, late, end = (0, NY), (0, 2), (2, 2), STEPS - 1
    for copy in wo_first[2:] + kv_first[2:]:
        copy.wait_recv()
    pass_on(2, ring_kv)
    pass_on(3, ring_wo)
    fans(0, ring_wo)
    ctx_copy(0, 2, 2, 1, y_b).wait_recv()
    project(0, *late, 0)
    ctx_copy(1, 1, 1, 2, y_a).wait_recv()
    ctx_copy(0, 0, 0, 4, y_b).wait_recv()
    ctx_copy(1, 0, 0, 5, y_a).wait_recv()
    project(0, *early, 1)
    send_hidden(2)
    pass_on(3, ring_kv)
    pass_on(4, ring_wo)
    fans(1, ring_wo)
    project(1, *all_rows, 2)
    pass_on(5, ring_wo)
    pass_on(4, ring_kv)
    exchange(0, *late, 0)
    exchange(0, *early, 1)
    send_hidden(3)
    pass_on(6, ring_wo)
    fans(2, ring_wo)
    project(2, *all_rows, 3)
    pass_on(5, ring_kv)
    pass_on(7, ring_wo)
    exchange(1, *all_rows, 2)
    finish(0, *late, 0)
    finish(0, *early, 1)
    pass_on(8, ring_wo)
    pass_on(6, ring_kv)
    fans(3, ring_wo)
    project(3, *early, 4)
    project(3, *late, 5)
    exchange(2, *all_rows, 3)
    pass_on(7, ring_kv)
    finish(1, *all_rows, 2)
    fans(0, ring_kv)
    accumulate(0, *all_rows)
    exchange(3, *early, 4)
    exchange(3, *late, 5)
    pass_on(8, ring_kv)
    fans(1, ring_kv)
    accumulate(1, *early)
    finish(2, *all_rows, 3)
    fans(2, ring_kv)
    accumulate(2, *early)
    fans(3, ring_kv)

    y_copies = [remote(ys.at[i], yr.at[i], y_s, y_r.at[i], (y_a, y_b)[i % 2]) for i in range(6)]

    def y_send(i, value):
        ys[i] = value.astype(BF16)
        y_copies[i].start()

    def y_read(i):
        return yr[i].astype(F32)

    finish(end, *early, 4)
    accumulate(end, *early)
    y_send(0, acc[0, 0])
    y_send(1, acc[1, 0])
    y_send(2, acc[0, 1])
    accumulate(1, *late)
    accumulate(2, *late)
    finish(end, *late, 5)
    accumulate(end, *late)
    y_send(3, acc[1, 2])
    y_copies[1].wait_recv()
    y_send(4, acc[1, 1] + y_read(1))
    y_copies[0].wait_recv()
    y_send(5, acc[0, 2] + y_read(0))

    columns = jnp.sum(sums[...], axis=2, keepdims=True)
    squares = jnp.sum(jnp.where(diag[None], columns, 0.0), axis=1, keepdims=True)
    st[...] = jnp.broadcast_to(squares, (NY, 8, ROWS))
    stat_copies = [remote(st.at[r], str_.at[r], st_s, st_r.at[r], near[r]) for r in range(own)]
    for copy in stat_copies:
        copy.start()

    @pl.when(off_diagonal)
    def _():
        for s in range(STEPS):
            out_copy(s, 0).wait_recv()

    for s in range(STEPS):
        for half, cols in enumerate(sides(s)):
            for copy in range(2):
                at = slice(cols.start + copy * FEAT, cols.stop + copy * FEAT)
                out_w[:, at] = out_in[s, half].astype(F32)
    enc_c[...] = turned(out_w, (NZ - z) % NZ)
    enc_copy = pltpu.make_async_copy(enc_c, enc_out, in_sem.at[0])
    enc_copy.start()

    lower_half = rows_i < DROWS
    above_end = jnp.minimum(w + 2, NW)
    base = jnp.where(lower_half, start(ordered[1:2], dbound[w]), start(ordered[1:2], dbound[w + 1]))
    last = jnp.where(lower_half, dbound[w + 1].astype(F32), dbound[above_end].astype(F32))
    offset = (rows_i % DROWS).astype(F32)
    dec_col = tags(ends[1:2], base + offset, last)
    dec_allowed = (dec_col == enc_row) & (enc_row >= 0.0)

    for copy in stat_copies:
        copy.wait_recv()
    square = st[own] + str_[0] + str_[1] + str_[2]
    square_col = jnp.sum(jnp.where(diag, square[0:1], 0.0), axis=1, keepdims=True)
    norm = lax.rsqrt(square_col * (1.0 / (NY * FEAT)) + EPSILON)
    dq_copy.wait_recv()

    for i in (2, 3, 4, 5):
        y_copies[i].wait_recv()
    near_keys = ((acc[0, own] + y_read(2) + y_read(5)) * norm).astype(BF16)
    near_values = ((acc[1, own] + y_read(3) + y_read(4)) * norm).astype(BF16)

    def cross(rows, head):
        cols = slice(head * HEAD_DIM, (head + 1) * HEAD_DIM)
        return attend(dq2[rows, cols], near_keys[:, cols], near_values[:, cols], dec_allowed[rows])

    dres[...] = jnp.concatenate([cross(slice(DROWS, ROWS), head) for head in range(2)], axis=1)
    up = remote(dres, drecv, up_s, up_r, upper)
    up.start()
    cross_out[...] = jnp.concatenate([cross(slice(0, DROWS), head) for head in range(2)], axis=1).astype(F32)

    def left(sent, sem):
        remote(sent, sent, sem, up_r, sib).wait_send()

    left(wo.at[pl.ds(0, 14 * BLK + 3 * PIECE)], wo_s)
    left(kvw.at[pl.ds(0, 14)], kv_s)
    left(kvw.at[pl.ds(0, 3), 0], first_s)
    left(ctx.at[:, pl.ds(0, 3)], ctx_s)
    left(x1s, xs1)
    left(x2s, xs2)
    left(ys, y_s)
    left(st.at[pl.ds(0, 3)], st_s)
    dq_copy.wait_send()

    @pl.when(off_diagonal)
    def _():
        left(hid_c, hid_s)

    @pl.when(jnp.logical_not(off_diagonal))
    def _():
        left(out_c.at[pl.ds(0, 3)], out_s)

    enc_copy.wait()
    up.wait()
    cross_out[...] = cross_out[...] + drecv[...].astype(F32)


def body(
    hidden_in, enc_query, enc_key, enc_value, dec_query, out_proj, key_proj, value_proj,
    norm_gain, enc_len, dec_len, example_order, enc_bounds, dec_bounds,
):
    vmem = pl.BlockSpec(memory_space=pltpu.VMEM)
    anywhere = pl.BlockSpec(memory_space=pl.ANY)
    dma = pltpu.SemaphoreType.DMA
    gain = norm_gain.reshape(32, 128)
    square = (ROWS, 128)
    hidden, context = pl.pallas_call(
        kernel,
        out_shape=(
            jax.ShapeDtypeStruct((ROWS, FEAT), F32),
            jax.ShapeDtypeStruct((DROWS, WID), F32),
        ),
        in_specs=[anywhere] * 14,
        out_specs=(anywhere, vmem),
        scratch_shapes=[
            pltpu.VMEM((ROWS, WID), BF16),
            pltpu.VMEM((ROWS, WID), BF16),
            pltpu.VMEM((ROWS, WID), BF16),
            pltpu.VMEM(gain.shape, F32),
            pltpu.VMEM((STEPS, 2, 8, 128), F32),
            pltpu.VMEM((3, 1, 256), jnp.int32),
            pltpu.SMEM(enc_bounds.shape, jnp.int32),
            pltpu.SMEM(dec_bounds.shape, jnp.int32),
            pltpu.VMEM((FEAT, WID), BF16),
            pltpu.VMEM((NZ, 2, BLK, WID), BF16),
            pltpu.VMEM((2, NY, ROWS, HEAD_DIM), BF16),
            pltpu.VMEM((ROWS, 2 * FEAT), BF16),
            pltpu.VMEM((STEPS, 2) + square, BF16),
            pltpu.VMEM((STEPS, NY, 2) + square, BF16),
            pltpu.VMEM((STEPS, 2, NY) + square, F32),
            pltpu.VMEM((STEPS, 2, NY) + square, BF16),
            pltpu.VMEM((STEPS, 2, NY) + square, BF16),
            pltpu.VMEM((STEPS, 2, NY) + square, BF16),
            pltpu.VMEM((STEPS, 2, NY) + square, BF16),
            pltpu.VMEM((STEPS, NY, ROWS, 4 * BLK), BF16),
            pltpu.VMEM((2, NY, ROWS, WID), F32),
            pltpu.VMEM((NY,) + square, F32),
            pltpu.VMEM((STEPS, NY, 2) + square, BF16),
            pltpu.VMEM((STEPS, 2) + square, BF16),
            pltpu.VMEM((ROWS, 2 * FEAT), F32),
            pltpu.VMEM((ROWS, FEAT), F32),
            pltpu.VMEM((6, ROWS, WID), BF16),
            pltpu.VMEM((6, ROWS, WID), BF16),
            pltpu.VMEM((NY, 8, ROWS), F32),
            pltpu.VMEM((NY - 1, 8, ROWS), F32),
            pltpu.VMEM((2 * DROWS, WID), BF16),
            pltpu.VMEM((DROWS, WID), BF16),
            pltpu.VMEM((DROWS, WID), BF16),
            dma((15,)),
            dma, dma((6,)),
            dma, dma((HOPS,)), dma((STEPS,)),
            dma, dma((HOPS,)), dma((STEPS,)),
            dma, dma,
            dma, dma,
            dma, dma((STEPS, NY - 1)),
            dma, dma((STEPS,)),
            dma, dma((6,)),
            dma, dma((STEPS + 2, 2)),
            dma, dma((STEPS + 2, 2)),
            dma, dma((6,)),
            dma, dma((NY - 1,)),
        ],
        compiler_params=pltpu.CompilerParams(
            collective_id=0, has_side_effects=True, vmem_limit_bytes=VMEM_LIMIT
        ),
        name="encoder_to_cross",
    )(
        hidden_in, enc_query, enc_key, enc_value, dec_query, out_proj.T, key_proj, value_proj,
        gain, enc_len.reshape(1, 256), dec_len.reshape(1, 256),
        example_order.reshape(1, 256), enc_bounds, dec_bounds,
    )
    return hidden.astype(BF16), context.astype(BF16)


def solution(mesh):
    return jax.shard_map(
        body,
        mesh=mesh,
        in_specs=(
            P("wide", "head"), P("wide", "head"), P("wide", "head"), P("wide", "head"),
            P("wide", "head"), P("head", "wide"), P("wide", "head"), P("wide", "head"),
            P(), P(), P(), P(), P(), P(),
        ),
        out_specs=(P("wide", "head"), P("wide", "head")),
        check_vma=False,
    )
```

```python
import jax
import jax.numpy as jnp
from jax import lax
from jax.experimental import pallas as pl
from jax.experimental.pallas import tpu as pltpu
from jax.sharding import PartitionSpec as P

MESH = pl.DeviceIdType.MESH
F32 = jnp.float32
BF16 = jnp.bfloat16

HEAD_DIM = 256
NZ = 16
NY = 4
NX = 4
NW = NY * NZ * 2
ROWS = 128
DROWS = 64
WID = 512
PIECE = 32
BLK = 2 * PIECE
FEAT = NZ * BLK
LANES = FEAT // 128
HOPS = NZ // 2
STEPS = NZ // 4
UNITS = STEPS * NY
GROUP = NY * ROWS
EPSILON = 1e-06
SCALE = 1.0 / 16.0
VMEM_LIMIT = 60 * 1024 * 1024


def nt(a, b):
    return lax.dot_general(a, b, (((1,), (1,)), ((), ())), preferred_element_type=F32)


def nn(a, b):
    return lax.dot_general(a, b, (((1,), (0,)), ((), ())), preferred_element_type=F32)


def iota(shape, dim):
    return lax.broadcasted_iota(jnp.int32, shape, dim)


def attend(q, k, v, allowed):
    scores = jnp.where(allowed, nt(q, k) * SCALE, -1e30)
    weights = jnp.where(allowed, jnp.exp(scores - jnp.max(scores, axis=1, keepdims=True)), 0.0)
    total = jnp.maximum(jnp.sum(weights, axis=1, keepdims=True), 1.0)
    return nn((weights / total).astype(BF16), v).astype(BF16)


def kernel(
    hidden, q_hbm, k_hbm, v_hbm, dq_hbm, wo_hbm, wk_hbm, wv_hbm, gain_hbm,
    elen_hbm, dlen_hbm, order_hbm, ebound_hbm, dbound_hbm,
    enc_out, cross_out,
    q_ref, k_ref, v_ref, gain_ref, gain_c, lens_ref, ebound, dbound,
    wo, kvw, ctx, hid, hid_c, hid_in, part, x1s, x1r, x2s, x2r, res, acc, sums, out_c, out_in, out_w, enc_c,
    ys, yr, st, str_, dq2, dres, drecv,
    in_sem, first_s, first_r, wo_s, wo_r, wof_r, kv_s, kv_r, kvf_r,
    dq_s, dq_r, up_s, up_r, hid_s, hid_r, out_s, out_r, ctx_s, ctx_r, xs1, xr1, xs2, xr2,
    y_s, y_r, st_s, st_r,
):
    w = lax.axis_index("wide")
    x = lax.axis_index("head")
    c = w % 2
    z = (w // 2) % NZ
    y = w // (2 * NZ)
    step_dir = 1 - 2 * c

    def wide(yy, zz, cc):
        return (yy * NZ + zz) * 2 + cc

    sib = (w + step_dir, x)
    z_next = (wide(y, (z + step_dir + NZ) % NZ, c), x)
    z_prev = (wide(y, (z - step_dir + NZ) % NZ, c), x)
    ya, yb, y2 = y + 1 - 2 * (y % 2), NY - 1 - y, (y + 2) % NY
    y_a, y_b, y_2 = (wide(ya, z, c), x), (wide(yb, z, c), x), (wide(y2, z, c), x)
    x_a, x_b = (w, x + 1 - 2 * (x % 2)), (w, NX - 1 - x)
    upper, lower = ((w + 1) % NW, x), ((w + NW - 1) % NW, x)
    adder = (wide(x, z, c), x)
    off_diagonal = x != y
    near = (y_2, y_a, y_b)
    relation = jnp.where(ya == x, 1, jnp.where(yb == x, 2, 0))
    own = NY - 1
    cross = (wide(y, (z - step_dir + NZ) % NZ, 1 - c), x)
    greet = (sib, z_next, z_prev, cross, y_a, y_b, y_2, x_a, x_b, upper, lower)

    def remote(src, dst, ss, rs, dev):
        return pltpu.make_async_remote_copy(
            src_ref=src, dst_ref=dst, send_sem=ss, recv_sem=rs, device_id=dev, device_id_type=MESH
        )

    def cols_of(i, width):
        return pl.ds(pl.multiple_of(i * width, width), width)

    barrier = pltpu.get_barrier_semaphore()
    for dev in greet:
        pl.semaphore_signal(barrier, inc=1, device_id=dev, device_id_type=MESH)

    piece = cols_of(c, PIECE)
    mine = piece
    pairs = (
        (wo_hbm, wo.at[mine]), (wk_hbm, kvw.at[0, 0, piece]), (wv_hbm, kvw.at[0, 1, piece]),
        (hidden, hid.at[:, pl.ds(0, FEAT)]), (hidden, hid.at[:, pl.ds(FEAT, FEAT)]),
        (elen_hbm, lens_ref.at[0]), (dlen_hbm, lens_ref.at[1]), (order_hbm, lens_ref.at[2]),
        (ebound_hbm, ebound), (dbound_hbm, dbound),
        (q_hbm, q_ref), (k_hbm, k_ref), (v_hbm, v_ref),
        (gain_hbm, gain_ref), (dq_hbm, dq2.at[pl.ds(0, DROWS)]),
    )
    loads = [pltpu.make_async_copy(a, b, in_sem.at[i]) for i, (a, b) in enumerate(pairs)]
    for load in loads:
        load.start()

    pl.semaphore_wait(barrier, len(greet))

    def out_at(i):
        return jnp.where(c == 0, NZ - i, i)

    def in_at(i):
        return jnp.where(c == 0, i, NZ - i)

    def rows_at(i, offset, count):
        return pl.ds(pl.multiple_of(i * BLK + offset, PIECE), count)

    around = ((z_next, out_at(1)), (cross, in_at(1)), (sib, 0))
    wo_first = [
        remote(wo.at[mine], wo.at[rows_at(to, c * PIECE, PIECE)], wo_s, first_r.at[i], dev)
        for i, (dev, to) in enumerate(around)
    ]
    kv_first = [
        remote(kvw.at[0, :, piece], kvw.at[to, :, piece], first_s, first_r.at[3 + i], dev)
        for i, (dev, to) in enumerate(around)
    ]
    loads[0].wait()
    for copy in wo_first:
        copy.start()
    for load in loads[1:3]:
        load.wait()
    for copy in kv_first:
        copy.start()
    dq_copy = remote(dq2.at[pl.ds(0, DROWS)], dq2.at[pl.ds(DROWS, DROWS)], dq_s, dq_r, lower)

    def turned(ref, by):
        wider = ref[:, pl.ds(pl.multiple_of((by // 2) * 128, 128), FEAT + 128)].astype(F32)
        return jnp.where(by % 2 == 1, wider[:, BLK : BLK + FEAT], wider[:, 0:FEAT])

    def sides(s):
        return slice(s * 128, (s + 1) * 128), slice((LANES - 1 - s) * 128, (LANES - s) * 128)

    def hid_copy(s):
        return remote(hid_c.at[s], hid_in.at[s, relation], hid_s, hid_r.at[s, relation], adder)

    def hid_got(s, r):
        return remote(hid_in.at[s, r], hid_in.at[s, r], hid_s, hid_r.at[s, r], adder)

    def out_copy(s, r):
        return remote(out_c.at[s, r], out_in.at[s], out_s, out_r.at[s], near[r])

    for load in loads[3:5]:
        load.wait()
    hid_turned = turned(hid, z)
    for s in range(STEPS):
        for half, cols in enumerate(sides(s)):
            hid_c[s, half] = hid_turned[:, cols].astype(BF16)

    @pl.when(off_diagonal)
    def _():
        hid_copy(0).start()
        hid_in[:, own] = jnp.zeros_like(hid_c)

    @pl.when(jnp.logical_not(off_diagonal))
    def _():
        hid_in[:, own] = hid_c[...]

    for load in loads[5:10]:
        load.wait()

    n = 256
    onehot = jnp.where(lens_ref[2] == iota((n, n), 0), 1.0, 0.0).astype(BF16)
    lens = jnp.concatenate([lens_ref[0], lens_ref[1], jnp.zeros((6, n), jnp.int32)], axis=0)
    ordered = nn(lens.astype(F32).astype(BF16), onehot)
    upto = jnp.where(iota((n, n), 0) <= iota((n, n), 1), 1.0, 0.0).astype(BF16)
    ends = nn(ordered.astype(BF16), upto)
    place = iota((1, n), 1)

    def start(row, first):
        return jnp.sum(jnp.where(place < first, row, 0.0), axis=1, keepdims=True)

    def tags(ends_row, offsets, last):
        pos = jnp.sum(jnp.where(ends_row <= offsets, 1.0, 0.0), axis=1, keepdims=True)
        return jnp.where(pos < last, pos, -1.0)

    rows_i = iota((ROWS, 1), 0)
    enc_base = start(ordered[0:1], ebound[w])
    enc_col = tags(ends[0:1], enc_base + rows_i.astype(F32), ebound[w + 1].astype(F32))
    diag = iota((ROWS, ROWS), 0) == iota((ROWS, ROWS), 1)
    enc_row = jnp.sum(jnp.where(diag, enc_col, 0.0), axis=0, keepdims=True)
    enc_allowed = (enc_col == enc_row) & (enc_row >= 0.0)

    def wo_blocks(i, count):
        return wo.at[rows_at(i, 0, count * BLK)]

    def kv_blocks(i, count):
        return kvw.at[pl.ds(i, count)]

    def hop(i, blocks, ss, rs, _):
        return remote(blocks(out_at(i - 1), 1), blocks(out_at(i), 1), ss, rs.at[i - 1], z_next)

    def fan(k, blocks, ss, _, rs, arrives=False):
        count = min(2, HOPS - 1 - 2 * k)
        low = NZ - 2 * k - count if count == 2 else NZ - 2 * k - 1
        start = jnp.where(c == (1 if arrives else 0), low, 2 * k + 1)
        at = blocks(start, count)
        return remote(at, at, ss, rs.at[k], sib)

    ring_wo = (wo_blocks, wo_s, wo_r, wof_r)
    ring_kv = (kv_blocks, kv_s, kv_r, kvf_r)

    def forward(i, ring):
        hop(i + 1, *ring).start()
        if i % 2 == 0 or i == HOPS - 1:
            fan((i - 1) // 2, *ring).start()

    def pass_on(i, ring):
        hop(i, *ring).wait_recv()
        if i < HOPS:
            forward(i, ring)

    def ctx_copy(head, src, dst, index, dev):
        return remote(ctx.at[head, src], ctx.at[head, dst], ctx_s, ctx_r.at[index], dev)

    for copy in wo_first[:2]:
        copy.wait_recv()
    forward(1, ring_wo)
    for copy in kv_first[:2]:
        copy.wait_recv()
    forward(1, ring_kv)
    for load in loads[10:]:
        load.wait()
    dq_copy.start()
    for head in range(2):
        cols = slice(head * HEAD_DIM, (head + 1) * HEAD_DIM)
        ctx[head, own] = attend(q_ref[:, cols], k_ref[:, cols], v_ref[:, cols], enc_allowed)
    ctx_first = [
        ctx_copy(0, own, 1, 0, y_a), ctx_copy(1, own, 2, 3, y_b),
        ctx_copy(1, own, 1, 2, y_a), ctx_copy(0, own, 2, 1, y_b),
    ]
    for copy in ctx_first:
        copy.start()
    pass_on(2, ring_wo)

    ctx_copy(0, 1, 1, 0, y_a).wait_recv()
    ctx_copy(0, 1, 0, 4, y_b).start()
    ctx_copy(1, 2, 2, 3, y_b).wait_recv()
    ctx_copy(1, 2, 0, 5, y_a).start()

    @pl.when(off_diagonal)
    def _():
        hid_copy(1).start()
        hid_in[:, 0:own] = jnp.zeros((STEPS, own, 2, ROWS, 128), BF16)

    for i in range(2 * LANES):
        row = gain_ref[pl.ds(y * LANES + i % LANES, 1), :]
        out_w[0:8, i * 128 : (i + 1) * 128] = jnp.broadcast_to(row, (8, 128))
    gain_turned = turned(out_w.at[pl.ds(0, 8)], z)
    for s in range(STEPS):
        for half, cols in enumerate(sides(s)):
            gain_c[s, half] = gain_turned[:, cols]
    sums[...] = jnp.zeros_like(sums)

    def round_one(s, first, count, index):
        return [
            remote(
                x1s.at[s, i, pl.ds(first, count)], x1r.at[s, i, pl.ds(first, count)],
                xs1, xr1.at[index, i], (x_a, x_b)[i],
            )
            for i in range(2)
        ]

    def round_two(s, first, count, index):
        return [
            remote(
                x2s.at[s, i, pl.ds(first, count)], x2r.at[s, i, pl.ds(first, count)],
                xs2, xr2.at[index, i], (x_b, x_a)[i],
            )
            for i in range(2)
        ]

    def project(s, first, count, index):
        @pl.when(jnp.logical_not(off_diagonal))
        def _():
            for r in range(first, min(first + count, own)):
                hid_got(s, r).wait_recv()

        groups = slice(first, first + count)
        weights = jnp.concatenate([wo[cols, :] for cols in sides(s)], axis=0)
        rows = [ctx[head, groups].reshape(count * ROWS, HEAD_DIM) for head in range(2)]
        term = nt(rows[0], weights[:, 0:HEAD_DIM]) + nt(rows[1], weights[:, HEAD_DIM:WID])
        for half in range(2):
            value = term[:, half * 128 : (half + 1) * 128].reshape(count, ROWS, 128)
            value = value + hid_in[s, groups, half].astype(F32)
            part[s, half, groups] = value
            x1s[s, half, groups] = value.astype(BF16)
        for copy in round_one(s, first, count, index):
            copy.start()

    def exchange(s, first, count, index):
        groups = slice(first, first + count)
        for half, copy in enumerate(round_one(s, first, count, index)):
            copy.wait_recv()
            total = part[s, half, groups] + x1r[s, half, groups].astype(F32)
            part[s, half, groups] = total
            x2s[s, half, groups] = total.astype(BF16)
            copy = round_two(s, first, count, index)[half]
            copy.start()

    def finish(s, first, count, index):
        groups = slice(first, first + count)
        for half, copy in enumerate(round_two(s, first, count, index)):
            copy.wait_recv()
            total = part[s, half, groups] + x2r[s, half, groups].astype(F32)
            sums[groups] += total * total
            res[s, groups, :, half * 128 : (half + 1) * 128] = (total * gain_c[s, half, 0:1, :]).astype(BF16)
            out_c[s, groups, half] = total.astype(BF16)

        @pl.when(jnp.logical_not(off_diagonal))
        def _():
            for r in range(first, min(first + count, own)):
                out_copy(s, r).start()
            if first + count > own:
                out_in[s] = out_c[s, own]

    def kv_weights(s, kind):
        quad = (2 * s, 2 * s + 1, NZ - 2 - 2 * s, NZ - 1 - 2 * s)
        return jnp.concatenate([kvw[i, kind] for i in quad], axis=0)

    def accumulate(s, first, count):
        groups = slice(first, first + count)
        rows = res[s, groups].reshape(count * ROWS, 4 * BLK)
        for kind in range(2):
            term = nn(rows, kv_weights(s, kind)).reshape(count, ROWS, WID)
            acc[kind, groups] = term if s == 0 else acc[kind, groups] + term

    def fans(s, ring):
        fan(s, *ring, arrives=True).wait_recv()

    def send_hidden(s):
        @pl.when(off_diagonal)
        def _():
            hid_copy(s).start()

    all_rows, early, late, end = (0, NY), (0, 2), (2, 2), STEPS - 1
    for copy in wo_first[2:] + kv_first[2:]:
        copy.wait_recv()
    pass_on(2, ring_kv)
    pass_on(3, ring_wo)
    fans(0, ring_wo)
    ctx_copy(0, 2, 2, 1, y_b).wait_recv()
    project(0, *late, 0)
    ctx_copy(1, 1, 1, 2, y_a).wait_recv()
    ctx_copy(0, 0, 0, 4, y_b).wait_recv()
    ctx_copy(1, 0, 0, 5, y_a).wait_recv()
    project(0, *early, 1)
    send_hidden(2)
    pass_on(3, ring_kv)
    pass_on(4, ring_wo)
    fans(1, ring_wo)
    project(1, *all_rows, 2)
    pass_on(5, ring_wo)
    pass_on(4, ring_kv)
    exchange(0, *late, 0)
    exchange(0, *early, 1)
    send_hidden(3)
    pass_on(6, ring_wo)
    fans(2, ring_wo)
    project(2, *all_rows, 3)
    pass_on(5, ring_kv)
    pass_on(7, ring_wo)
    exchange(1, *all_rows, 2)
    finish(0, *late, 0)
    finish(0, *early, 1)
    pass_on(8, ring_wo)
    pass_on(6, ring_kv)
    fans(3, ring_wo)
    project(3, *early, 4)
    project(3, *late, 5)
    exchange(2, *all_rows, 3)
    pass_on(7, ring_kv)
    finish(1, *all_rows, 2)
    fans(0, ring_kv)
    exchange(3, *early, 4)
    exchange(3, *late, 5)
    accumulate(0, *early)
    pass_on(8, ring_kv)
    fans(1, ring_kv)
    accumulate(1, *early)
    finish(2, *all_rows, 3)
    fans(2, ring_kv)
    accumulate(2, *early)
    fans(3, ring_kv)

    y_copies = [remote(ys.at[i], yr.at[i], y_s, y_r.at[i], (y_a, y_b)[i % 2]) for i in range(6)]

    def y_send(i, value):
        ys[i] = value.astype(BF16)
        y_copies[i].start()

    def y_read(i):
        return yr[i].astype(F32)

    finish(end, *early, 4)
    accumulate(end, *early)
    y_send(0, acc[0, 0])
    y_send(1, acc[1, 0])
    y_send(2, acc[0, 1])
    accumulate(0, *late)
    accumulate(1, *late)
    accumulate(2, *late)
    finish(end, *late, 5)
    accumulate(end, *late)
    y_send(3, acc[1, 2])
    y_copies[1].wait_recv()
    y_send(4, acc[1, 1] + y_read(1))
    y_copies[0].wait_recv()
    y_send(5, acc[0, 2] + y_read(0))

    columns = jnp.sum(sums[...], axis=2, keepdims=True)
    squares = jnp.sum(jnp.where(diag[None], columns, 0.0), axis=1, keepdims=True)
    st[...] = jnp.broadcast_to(squares, (NY, 8, ROWS))
    stat_copies = [remote(st.at[r], str_.at[r], st_s, st_r.at[r], near[r]) for r in range(own)]
    for copy in stat_copies:
        copy.start()

    @pl.when(off_diagonal)
    def _():
        for s in range(STEPS):
            out_copy(s, 0).wait_recv()

    for s in range(STEPS):
        for half, cols in enumerate(sides(s)):
            for copy in range(2):
                at = slice(cols.start + copy * FEAT, cols.stop + copy * FEAT)
                out_w[:, at] = out_in[s, half].astype(F32)
    enc_c[...] = turned(out_w, (NZ - z) % NZ).astype(BF16)
    enc_copy = pltpu.make_async_copy(enc_c, enc_out, in_sem.at[0])
    enc_copy.start()

    lower_half = rows_i < DROWS
    above_end = jnp.minimum(w + 2, NW)
    base = jnp.where(lower_half, start(ordered[1:2], dbound[w]), start(ordered[1:2], dbound[w + 1]))
    last = jnp.where(lower_half, dbound[w + 1].astype(F32), dbound[above_end].astype(F32))
    offset = (rows_i % DROWS).astype(F32)
    dec_col = tags(ends[1:2], base + offset, last)
    dec_allowed = (dec_col == enc_row) & (enc_row >= 0.0)

    for copy in stat_copies:
        copy.wait_recv()
    square = st[own] + str_[0] + str_[1] + str_[2]
    square_col = jnp.sum(jnp.where(diag, square[0:1], 0.0), axis=1, keepdims=True)
    norm = lax.rsqrt(square_col * (1.0 / (NY * FEAT)) + EPSILON)
    dq_copy.wait_recv()

    for i in (2, 3, 4, 5):
        y_copies[i].wait_recv()
    near_keys = ((acc[0, own] + y_read(2) + y_read(5)) * norm).astype(BF16)
    near_values = ((acc[1, own] + y_read(3) + y_read(4)) * norm).astype(BF16)

    def cross(rows, head):
        cols = slice(head * HEAD_DIM, (head + 1) * HEAD_DIM)
        return attend(dq2[rows, cols], near_keys[:, cols], near_values[:, cols], dec_allowed[rows])

    dres[...] = jnp.concatenate([cross(slice(DROWS, ROWS), head) for head in range(2)], axis=1)
    up = remote(dres, drecv, up_s, up_r, upper)
    up.start()
    cross_out[...] = jnp.concatenate([cross(slice(0, DROWS), head) for head in range(2)], axis=1)

    def left(sent, sem):
        remote(sent, sent, sem, up_r, sib).wait_send()

    left(wo.at[pl.ds(0, 14 * BLK + 3 * PIECE)], wo_s)
    left(kvw.at[pl.ds(0, 14)], kv_s)
    left(kvw.at[pl.ds(0, 3), 0], first_s)
    left(ctx.at[:, pl.ds(0, 3)], ctx_s)
    left(x1s, xs1)
    left(x2s, xs2)
    left(ys, y_s)
    left(st.at[pl.ds(0, 3)], st_s)
    dq_copy.wait_send()

    @pl.when(off_diagonal)
    def _():
        left(hid_c, hid_s)

    @pl.when(jnp.logical_not(off_diagonal))
    def _():
        left(out_c.at[pl.ds(0, 3)], out_s)

    enc_copy.wait()
    up.wait()
    cross_out[...] = cross_out[...] + drecv[...]


def body(
    hidden_in, enc_query, enc_key, enc_value, dec_query, out_proj, key_proj, value_proj,
    norm_gain, enc_len, dec_len, example_order, enc_bounds, dec_bounds,
):
    vmem = pl.BlockSpec(memory_space=pltpu.VMEM)
    anywhere = pl.BlockSpec(memory_space=pl.ANY)
    dma = pltpu.SemaphoreType.DMA
    gain = norm_gain.reshape(32, 128)
    square = (ROWS, 128)
    return pl.pallas_call(
        kernel,
        out_shape=(
            jax.ShapeDtypeStruct((ROWS, FEAT), BF16),
            jax.ShapeDtypeStruct((DROWS, WID), BF16),
        ),
        in_specs=[anywhere] * 14,
        out_specs=(anywhere, vmem),
        scratch_shapes=[
            pltpu.VMEM((ROWS, WID), BF16),
            pltpu.VMEM((ROWS, WID), BF16),
            pltpu.VMEM((ROWS, WID), BF16),
            pltpu.VMEM(gain.shape, F32),
            pltpu.VMEM((STEPS, 2, 8, 128), F32),
            pltpu.VMEM((3, 1, 256), jnp.int32),
            pltpu.SMEM(enc_bounds.shape, jnp.int32),
            pltpu.SMEM(dec_bounds.shape, jnp.int32),
            pltpu.VMEM((FEAT, WID), BF16),
            pltpu.VMEM((NZ, 2, BLK, WID), BF16),
            pltpu.VMEM((2, NY, ROWS, HEAD_DIM), BF16),
            pltpu.VMEM((ROWS, 2 * FEAT), BF16),
            pltpu.VMEM((STEPS, 2) + square, BF16),
            pltpu.VMEM((STEPS, NY, 2) + square, BF16),
            pltpu.VMEM((STEPS, 2, NY) + square, F32),
            pltpu.VMEM((STEPS, 2, NY) + square, BF16),
            pltpu.VMEM((STEPS, 2, NY) + square, BF16),
            pltpu.VMEM((STEPS, 2, NY) + square, BF16),
            pltpu.VMEM((STEPS, 2, NY) + square, BF16),
            pltpu.VMEM((STEPS, NY, ROWS, 4 * BLK), BF16),
            pltpu.VMEM((2, NY, ROWS, WID), F32),
            pltpu.VMEM((NY,) + square, F32),
            pltpu.VMEM((STEPS, NY, 2) + square, BF16),
            pltpu.VMEM((STEPS, 2) + square, BF16),
            pltpu.VMEM((ROWS, 2 * FEAT), F32),
            pltpu.VMEM((ROWS, FEAT), BF16),
            pltpu.VMEM((6, ROWS, WID), BF16),
            pltpu.VMEM((6, ROWS, WID), BF16),
            pltpu.VMEM((NY, 8, ROWS), F32),
            pltpu.VMEM((NY - 1, 8, ROWS), F32),
            pltpu.VMEM((2 * DROWS, WID), BF16),
            pltpu.VMEM((DROWS, WID), BF16),
            pltpu.VMEM((DROWS, WID), BF16),
            dma((15,)),
            dma, dma((6,)),
            dma, dma((HOPS,)), dma((STEPS,)),
            dma, dma((HOPS,)), dma((STEPS,)),
            dma, dma,
            dma, dma,
            dma, dma((STEPS, NY - 1)),
            dma, dma((STEPS,)),
            dma, dma((6,)),
            dma, dma((STEPS + 2, 2)),
            dma, dma((STEPS + 2, 2)),
            dma, dma((6,)),
            dma, dma((NY - 1,)),
        ],
        compiler_params=pltpu.CompilerParams(
            collective_id=0, has_side_effects=True, vmem_limit_bytes=VMEM_LIMIT
        ),
        name="encoder_to_cross",
    )(
        hidden_in, enc_query, enc_key, enc_value, dec_query, out_proj.T, key_proj, value_proj,
        gain, enc_len.reshape(1, 256), dec_len.reshape(1, 256),
        example_order.reshape(1, 256), enc_bounds, dec_bounds,
    )


def solution(mesh):
    return jax.shard_map(
        body,
        mesh=mesh,
        in_specs=(
            P("wide", "head"), P("wide", "head"), P("wide", "head"), P("wide", "head"),
            P("wide", "head"), P("head", "wide"), P("wide", "head"), P("wide", "head"),
            P(), P(), P(), P(), P(), P(),
        ),
        out_specs=(P("wide", "head"), P("wide", "head")),
        check_vma=False,
    )
```
